128 devices in a mesh: rep: 16 (over y_lo, x, core), fsdp: 8 (over z, y_hi).
Axes of the slice: x: 4, y: 4 (y_hi: 2, y_lo: 2; y = y_hi * 2 + y_lo), z: 4, core: 2. Of those that a mesh axis runs over, the one named last changes fastest.
Arguments:
- inputs: bfloat16 [16, 1024, 1536], P('rep', 'fsdp'), may hold values from -6 to 6
- segments: int32 [16, 1024], P('rep'), may hold values from 0 to 4, as said below
- first_gain: bfloat16 [1536], P('fsdp'), may hold values from 0.25 to 1.75
- query_matrix: bfloat16 [1536, 1536], P('fsdp'), may hold values from -0.15625 to 0.15625
- key_matrix: bfloat16 [1536, 256], P('fsdp'), may hold values from -0.15625 to 0.15625
- value_matrix: bfloat16 [1536, 256], P('fsdp'), may hold values from -0.15625 to 0.15625
- output_matrix: bfloat16 [1536, 1536], P('fsdp'), may hold values from -0.625 to 0.625
- second_gain: bfloat16 [1536], P('fsdp'), may hold values from 0.25 to 1.75
- expert_ids: int32 [16, 1024, 4], P('rep', 'fsdp'), may hold values from 0 to 7, all different within a row
- gate_values: float32 [16, 1024, 4], P('rep', 'fsdp'), may hold values from 0.1 to 0.5
- priority: int32 [16, 8, 512], P('rep', 'fsdp'), may hold values from 0 to 511, each once within a row
- gate_weight: bfloat16 [8, 1536, 768], P('fsdp'), may hold values from -0.15625 to 0.15625
- up_weight: bfloat16 [8, 1536, 768], P('fsdp'), may hold values from -0.15625 to 0.15625
- down_weight: bfloat16 [8, 768, 1536], P('fsdp'), may hold values from -0.4375 to 0.4375
- cotangent: bfloat16 [16, 1024, 1536], P('rep', 'fsdp'), may hold values from -6 to 6
Outputs:
- outputs: bfloat16 [16, 1024, 1536], P('rep', 'fsdp')
- input_grad: bfloat16 [16, 1024, 1536], P('rep', 'fsdp')
- first_gain_grad: float32 [1536], P('fsdp')
- query_grad: float32 [1536, 1536], P('fsdp')
- key_grad: float32 [1536, 256], P('fsdp')
- value_grad: float32 [1536, 256], P('fsdp')
- output_grad: float32 [1536, 1536], P('fsdp')
- second_gain_grad: float32 [1536], P('fsdp')
- gate_grad: float32 [8, 1536, 768], P('fsdp')
- up_grad: float32 [8, 1536, 768], P('fsdp')
- down_grad: float32 [8, 768, 1536], P('fsdp')
The draws below stay inside these ranges and needn't reach their ends.
Inputs may be any that keep to these rules, and one draw needn't show every extreme that they name: `segments`: segment numbers never fall along a sequence. `expert_ids`: each token names 4 different experts. `priority`: each device's row is a permutation.
All inputs are finite; a program needn't handle non-finite values.
Results may differ from the reference program's by a relative error of at most 0.025.
Values may be sent and summed in bfloat16 or wider, within the bound.
No kernel may reach another device: no remote copies, remote signals or barrier semaphores. Data moves between devices by JAX's collectives and lax.ppermute only.
A program may use at most 128 MiB of HBM per device.

```python
import math
from functools import partial
import jax
import jax.numpy as jnp
from jax import lax

D = 1536
HEADS = 12
KV_HEADS = 2
HEAD_DIM = 128
FF = 768
TOP = 4
TOK_DEV = 128
WINDOW = 1024
EXPERTS = 8
SEQS = 16
LEN = 1024
CAP = 80
Q_WIDTH = 1536
KV_WIDTH = 256
N_FSDP = 8


def draw_segments(key, part):
    key = jax.random.fold_in(key, 11)
    early_key, late_key = jax.random.split(key)
    early = jax.random.randint(early_key, (SEQS, 2), 1, max(TOK_DEV // 2, 2), dtype=jnp.int32)
    late = jax.random.randint(late_key, (SEQS, 2), LEN - TOK_DEV // 2, LEN, dtype=jnp.int32)
    cuts = jnp.concatenate([early, late], axis=1)
    places = jnp.arange(LEN, dtype=jnp.int32)
    return jnp.sum((places[None, :, None] >= cuts[:, None, :]).astype(jnp.int32), axis=2)


def level_of(rng, extent, shards, low, top_value):
    factor_of, own = 1.0, jax.random.fold_in(rng, 6)
    for dim, parts in shards:
        heights = jnp.exp(jax.random.uniform(jax.random.fold_in(own, dim), (parts,), jnp.float32, low / len(shards), top_value / len(shards)))
        factor_of = factor_of * jnp.repeat(heights, extent[dim] // parts).reshape([-1 if axis == dim else 1 for axis in range(len(extent))])
    return factor_of


def different_ones(own_key, rows, count, top, lift):
    ranking = jax.random.permutation(jax.random.fold_in(own_key, 1), count)
    boost = ranking
    for power in range(3):
        boost = boost * boost // count
    boost = boost * lift // count
    lots = jax.random.randint(jax.random.fold_in(own_key, 2), (rows, count), 0, 4096) + boost
    sure = jax.random.permutation(jax.random.fold_in(own_key, 3), rows)[jnp.arange(count) % rows]
    lots = jnp.where(jnp.arange(rows)[:, None] == sure[None, :], 1 << 14, lots)
    score = lots * count + jnp.arange(count)
    return lax.top_k(score.astype(jnp.int32), top)[1].astype(jnp.int32)


def bell_draw(key, extent, spread, limit, cuts=(), kind=jnp.bfloat16):
    loudness = level_of(key, extent, cuts, -0.22, 0.18) if cuts else 1.0
    drawn = jax.random.normal(key, extent, jnp.float32) * spread * loudness
    return jnp.minimum(jnp.maximum(drawn, -limit), limit).astype(kind)


def setup_inputs(seed: int = 0) -> dict:
    arg_keys = jax.random.split(jax.random.key(seed), 16)
    return {
        "inputs": bell_draw(arg_keys[0], (SEQS, LEN, D), 1.0, 6.0, ((0, 16), (1, 8))),
        "segments": draw_segments(jax.random.fold_in(arg_keys[15], 71), 0),
        "first_gain": jnp.clip(1.0 + 0.15 * jax.random.normal(arg_keys[2], (D,), jnp.float32), 0.25, 1.75).astype(jnp.bfloat16),
        "query_matrix": bell_draw(arg_keys[3], (D, Q_WIDTH), D ** -0.5, 0.15625, ((0, 8),)),
        "key_matrix": bell_draw(arg_keys[4], (D, KV_WIDTH), D ** -0.5, 0.15625, ((0, 8),)),
        "value_matrix": bell_draw(arg_keys[5], (D, KV_WIDTH), D ** -0.5, 0.15625, ((0, 8),)),
        "output_matrix": bell_draw(arg_keys[6], (Q_WIDTH, D), (Q_WIDTH // 16) ** -0.5, 0.625, ((0, 8),)),
        "second_gain": jnp.clip(1.0 + 0.15 * jax.random.normal(arg_keys[7], (D,), jnp.float32), 0.25, 1.75).astype(jnp.bfloat16),
        "expert_ids": different_ones(arg_keys[8], SEQS * LEN, EXPERTS, TOP, 4096).reshape((SEQS, LEN, TOP)),
        "gate_values": jnp.clip(jnp.exp(math.log(0.5) - 1.609438 * jax.random.uniform(arg_keys[9], (SEQS, LEN, TOP), jnp.float32) ** level_of(arg_keys[9], (SEQS, LEN, TOP), ((0, 16), (1, 8)), -0.2, 0.2)), 0.1, 0.5),
        "priority": jax.vmap(lambda own: jax.random.permutation(own, TOK_DEV * TOP))(jax.random.split(arg_keys[10], SEQS * N_FSDP)).reshape((SEQS, N_FSDP, TOK_DEV * TOP)).astype(jnp.int32),
        "gate_weight": bell_draw(arg_keys[11], (EXPERTS, D, FF), D ** -0.5, 0.15625, ((0, 8),)),
        "up_weight": bell_draw(arg_keys[12], (EXPERTS, D, FF), D ** -0.5, 0.15625, ((0, 8),)),
        "down_weight": bell_draw(arg_keys[13], (EXPERTS, FF, D), (FF // 4) ** -0.5, 0.4375, ((0, 8),)),
        "cotangent": bell_draw(arg_keys[14], (SEQS, LEN, D), 1.0, 6.0, ((0, 16), (1, 8))),
    }


EPSILON = 1e-06
THETA = 10000.0
NEGATIVE = -1e+30
TOP_PRECISION = lax.Precision.HIGHEST

@jax.custom_vjp
def lower_precision(v):
    return lax.optimization_barrier(v.astype(jnp.bfloat16)).astype(jnp.float32)

@jax.custom_vjp
def lower_precision_back(v):
    return v

def low_keep(v):
    return (lower_precision(v), None)

def low_pass(kept, grad):
    return (grad,)

def back_keep(v):
    return (v, None)

def back_low(kept, grad):
    return (lower_precision(grad),)
lower_precision.defvjp(low_keep, low_pass)
lower_precision_back.defvjp(back_keep, back_low)

def angles(positions):
    half_width = HEAD_DIM // 2
    frequency = THETA ** (-(jnp.arange(half_width, dtype=jnp.float32) * 2.0) / HEAD_DIM)
    phase = positions.astype(jnp.float32)[:, None] * frequency[None, :]
    return (jnp.cos(phase), jnp.sin(phase))

def rotate(vectors, cosine_table, sine_table):
    half_width = HEAD_DIM // 2
    first_half = vectors[..., :half_width]
    second_half = vectors[..., half_width:]
    cosine_table = cosine_table[:, None, :]
    sine_table = sine_table[:, None, :]
    return jnp.concatenate([first_half * cosine_table - second_half * sine_table, second_half * cosine_table + first_half * sine_table], axis=-1)

def normalize(vectors, gain):
    scale = lax.rsqrt(lax.optimization_barrier(jnp.mean(vectors * vectors, axis=-1, keepdims=True)) + EPSILON)
    return vectors * scale * gain

def attend_one(pieces):
    queries, keys_rot, value_rows, segment_row = pieces
    grouped = queries.reshape(LEN, KV_HEADS, HEADS // KV_HEADS, HEAD_DIM)
    scores = jnp.einsum('qgjd,kgd->gjqk', grouped, keys_rot, precision=TOP_PRECISION) * HEAD_DIM ** (-0.5)
    scores = lower_precision_back(scores)
    places = jnp.arange(LEN, dtype=jnp.int32)
    allowed = (places[None, :] <= places[:, None]) & (places[:, None] - places[None, :] < WINDOW) & (segment_row[None, :] == segment_row[:, None])
    scores = jnp.where(allowed[None, None], scores, NEGATIVE)
    row_max = lax.optimization_barrier(jnp.max(scores, axis=-1, keepdims=True))
    weights = jnp.exp(scores - row_max)
    probs = lower_precision(weights / lax.optimization_barrier(jnp.sum(weights, axis=-1, keepdims=True)))
    mixed_output = jnp.einsum('gjqk,kgd->qgjd', probs, value_rows, precision=TOP_PRECISION)
    return mixed_output.reshape(LEN, HEADS * HEAD_DIM)

def expert_one(pieces):
    rows, gate_w, up_w, down_w = pieces
    gate_pre = lower_precision_back(jnp.einsum('rd,df->rf', rows, gate_w, precision=TOP_PRECISION))
    up_pre = lower_precision_back(jnp.einsum('rd,df->rf', rows, up_w, precision=TOP_PRECISION))
    hidden = lower_precision(jax.nn.silu(gate_pre) * up_pre)
    return lower_precision(lower_precision_back(jnp.einsum('rf,fd->rd', hidden, down_w, precision=TOP_PRECISION)))

def slot_places(route_row, order_row, expert_count):
    ordered = jnp.zeros_like(route_row).at[order_row].set(route_row)
    onehot_marks = (ordered[:, None] == jnp.arange(expert_count, dtype=jnp.int32)[None, :]).astype(jnp.int32)
    counts = jnp.cumsum(onehot_marks, axis=0)
    rank_list = lax.optimization_barrier(jnp.sum(counts * onehot_marks, axis=1)) - 1
    return rank_list[order_row].astype(jnp.int32)

def forward(segments, places_index, pair_gate, inputs, first_gain, query_matrix, key_matrix, value_matrix, output_matrix, second_gain, gate_weight, up_weight, down_weight):
    block_count = SEQS * N_FSDP
    normalized_input = lower_precision(normalize(inputs, first_gain))
    query_before_rotation = lower_precision_back(jnp.einsum('cjg,gn->cjn', normalized_input, query_matrix, precision=TOP_PRECISION))
    key_before_rotation = lower_precision_back(jnp.einsum('cjg,gn->cjn', normalized_input, key_matrix, precision=TOP_PRECISION))
    value_rows = lower_precision(lower_precision_back(jnp.einsum('cjg,gn->cjn', normalized_input, value_matrix, precision=TOP_PRECISION)))
    cosine_table, sine_table = angles(jnp.arange(LEN, dtype=jnp.int32))
    queries = lower_precision(rotate(query_before_rotation.reshape(SEQS, LEN, HEADS, HEAD_DIM), cosine_table, sine_table))
    keys_rot = lower_precision(rotate(key_before_rotation.reshape(SEQS, LEN, KV_HEADS, HEAD_DIM), cosine_table, sine_table))
    value_rows = value_rows.reshape(SEQS, LEN, KV_HEADS, HEAD_DIM)
    mixed_output = lax.map(jax.checkpoint(attend_one), (queries, keys_rot, value_rows, segments))
    mixed_output = lower_precision(lower_precision_back(mixed_output))
    attention_output = lower_precision_back(jnp.einsum('aeb,by->aey', mixed_output, output_matrix, precision=TOP_PRECISION))
    residual = inputs + attention_output
    second = lower_precision(normalize(residual, second_gain))
    blocks = second.reshape(block_count, TOK_DEV, D)
    pair_rows = lower_precision_back(jnp.repeat(blocks, TOP, axis=1))
    buffer = jnp.zeros((EXPERTS * block_count * CAP + 1, D), jnp.float32)
    buffer = buffer.at[places_index.reshape(-1)].add(pair_rows.reshape(-1, D))
    buffer = buffer[:-1].reshape(EXPERTS, block_count * CAP, D)
    results = lax.map(jax.checkpoint(expert_one), (buffer, gate_weight, up_weight, down_weight))
    flat_results = jnp.concatenate([results.reshape(-1, D), jnp.zeros((1, D), jnp.float32)], axis=0)
    picked = flat_results[places_index]
    weighted = picked * pair_gate[..., None]
    mixture = lax.optimization_barrier(jnp.sum(weighted.reshape(block_count, TOK_DEV, TOP, D), axis=2)).reshape(SEQS, LEN, D)
    return residual + mixture

def reference(inputs, segments, first_gain, query_matrix, key_matrix, value_matrix, output_matrix, second_gain, expert_ids, gate_values, priority, gate_weight, up_weight, down_weight, cotangent):
    block_count = SEQS * N_FSDP
    route_rows = expert_ids.reshape(block_count, TOK_DEV * TOP).astype(jnp.int32)
    order_rows = priority.reshape(block_count, TOK_DEV * TOP).astype(jnp.int32)
    slots = jax.vmap(partial(slot_places, expert_count=EXPERTS))(route_rows, order_rows)
    kept_pair = slots < CAP
    owner_block = jnp.arange(block_count, dtype=jnp.int32)[:, None]
    places_index = jnp.where(kept_pair, route_rows * (block_count * CAP) + owner_block * CAP + slots, EXPERTS * block_count * CAP).astype(jnp.int32)
    pair_gate = gate_values.reshape(block_count, TOK_DEV * TOP).astype(jnp.float32) * kept_pair.astype(jnp.float32)
    floats = tuple((item.astype(jnp.float32) for item in (inputs, first_gain, query_matrix, key_matrix, value_matrix, output_matrix, second_gain, gate_weight, up_weight, down_weight)))
    result, pullback = jax.vjp(partial(forward, segments.astype(jnp.int32), places_index, pair_gate), *floats)
    gradients = pullback(cotangent.astype(jnp.float32))
    return (result.astype(jnp.bfloat16), gradients[0].astype(jnp.bfloat16), gradients[1], gradients[2], gradients[3], gradients[4], gradients[5], gradients[6], gradients[7], gradients[8], gradients[9])
```

```python
import jax
import jax.numpy as jnp
from jax import lax
from jax.sharding import Mesh
from jax.sharding import PartitionSpec as P

HEADS = 12
KV_HEADS = 2
HEAD_DIM = 128
TOP = 4
WINDOW = 1024

EPSILON = 1e-06
THETA = 10000.0
NEGATIVE = -1e30

YLO, XS, CORES = 2, 4, 2
REP = ("ylo", "x", "core")
BF = jnp.bfloat16
F32 = jnp.float32


def angles(positions):
    half_width = HEAD_DIM // 2
    frequency = THETA ** (-(jnp.arange(half_width, dtype=F32) * 2.0) / HEAD_DIM)
    phase = positions.astype(F32)[:, None] * frequency[None, :]
    return (jnp.cos(phase), jnp.sin(phase))


def rotate(vectors, cosine_table, sine_table):
    half_width = HEAD_DIM // 2
    first_half = vectors[..., :half_width]
    second_half = vectors[..., half_width:]
    cosine_table = cosine_table[:, None, :]
    sine_table = sine_table[:, None, :]
    return jnp.concatenate(
        [
            first_half * cosine_table - second_half * sine_table,
            second_half * cosine_table + first_half * sine_table,
        ],
        axis=-1,
    )


def dot(a, b):
    return jnp.dot(a, b, preferred_element_type=F32)


def dot_t(a, b):
    return lax.dot_general(a, b, (((1,), (1,)), ((), ())), preferred_element_type=F32)


def t_dot(a, b):
    return lax.dot_general(a, b, (((0,), (0,)), ((), ())), preferred_element_type=F32)


def norm_back(vectors, scale, gain, grad_normed):
    weighted = grad_normed * gain
    inner_sum = jnp.sum(weighted * vectors, axis=-1, keepdims=True)
    grad_vectors = (
        scale * weighted - vectors * (scale * scale * scale) * inner_sum / vectors.shape[-1]
    )
    grad_gain = jnp.sum(grad_normed * vectors * scale, axis=0)
    return (grad_vectors, grad_gain)


def masked_scores(query_rot, key_heads, query_places, query_segments, segment_row):
    row_count = query_rot.shape[0]
    grouped = query_rot.reshape(row_count, KV_HEADS, HEADS // KV_HEADS, HEAD_DIM)
    raw = jnp.einsum(
        "qgjd,kgd->gjqk", grouped, key_heads, preferred_element_type=F32
    ) * HEAD_DIM ** (-0.5)
    key_places = jnp.arange(segment_row.shape[0], dtype=jnp.int32)
    allowed = (
        (key_places[None, :] <= query_places[:, None])
        & (query_places[:, None] - key_places[None, :] < WINDOW)
        & (segment_row[None, :] == query_segments[:, None])
    )
    return (jnp.where(allowed[None, None], raw, NEGATIVE), grouped)


def swap(v):
    return lax.ppermute(v, "core", [(0, 1), (1, 0)])


def exchange(v, axis):
    return lax.all_to_all(v, axis, 0, 0, tiled=True)


def spread(v, axis, n):
    copies = lax.optimization_barrier(jnp.broadcast_to(v[None], (n,) + v.shape))
    return lax.all_to_all(copies, axis, 0, 0, tiled=True)


def body(
    inputs,
    segments,
    first_gain,
    query_matrix,
    key_matrix,
    value_matrix,
    output_matrix,
    second_gain,
    expert_ids,
    gate_values,
    priority,
    gate_weight,
    up_weight,
    down_weight,
    cotangent,
):
    tok = inputs.shape[1]
    width = inputs.shape[2]
    rows = query_matrix.shape[0]
    groups = lax.axis_size("fsdp")
    member = lax.axis_index("fsdp")
    core = lax.axis_index("core")
    even = core == 0
    experts = groups
    capacity = 5 * tok * TOP // (4 * experts)
    half = width // 2
    kv_width = key_matrix.shape[1]

    def pick(a, b):
        return jnp.where(even, a, b)

    def sides(own, other):
        return jnp.concatenate([pick(own, other), pick(other, own)], axis=-1)

    gains = jnp.pad(jnp.stack([first_gain, second_gain]), ((0, 14), (0, kv_width - rows)))
    kv_piece = jnp.concatenate([pick(key_matrix, value_matrix), gains], axis=0)
    kv_gathered = spread(kv_piece, "fsdp", groups)
    kv_own = kv_gathered[:, :rows].reshape(width, kv_width)
    gain_one = kv_gathered[:, rows, :rows].reshape(width).astype(F32)
    gain_two = kv_gathered[:, rows + 1, :rows].reshape(width).astype(F32)
    kv_other = swap(kv_own)
    q_own = spread(
        lax.dynamic_slice_in_dim(query_matrix, core * half, half, 1), "fsdp", groups
    ).reshape(width, half)
    q_other = swap(q_own)
    o_own = spread(
        lax.dynamic_slice_in_dim(output_matrix, core * half, half, 1), "fsdp", groups
    ).reshape(width, half)
    o_other = swap(o_own)

    ids = expert_ids[0].reshape(-1)
    order = priority[0, 0]
    earlier = (order[None, :] < order[:, None]) & (ids[None, :] == ids[:, None])
    slots = jnp.sum(earlier.astype(jnp.int32), axis=1)
    kept = slots < capacity
    expert_list = jnp.arange(experts, dtype=jnp.int32)
    chosen = (ids[:, None] == expert_list[None, :]) & kept[:, None]
    place = jnp.sum(
        jnp.where(chosen, slots[:, None] + 1, 0).reshape(tok, TOP, experts), axis=1
    )
    place = place - 1
    gate_table = jnp.sum(
        jnp.where(chosen, gate_values[0].reshape(-1)[:, None], 0.0).reshape(tok, TOP, experts),
        axis=1,
    )
    slot_list = jnp.arange(capacity, dtype=jnp.int32)
    hits = place.T[:, None, :] == slot_list[None, :, None]
    one_hot = hits.astype(BF).reshape(experts * capacity, tok)
    gate_hot = jnp.where(hits, gate_table.T[:, None, :], 0.0).reshape(experts * capacity, tok)
    slot_gate = jnp.sum(gate_hot, axis=1, keepdims=True)
    gate_high = gate_hot.astype(BF)
    gate_low = (gate_hot - gate_high.astype(F32)).astype(BF)

    upstream = cotangent[0].astype(F32)
    send_grad = (dot(one_hot, cotangent[0]) * slot_gate).astype(BF)
    arrived_grad = exchange(send_grad, "fsdp")

    source = inputs[0].astype(F32)
    scale_one = lax.rsqrt(jnp.mean(source * source, axis=-1, keepdims=True) + EPSILON)
    normed = (source * scale_one * gain_one).astype(BF)
    kv_a = dot(normed, kv_own)
    kv_b = dot(normed, kv_other)
    key_pre = pick(kv_a, kv_b)
    value_pre = pick(kv_b, kv_a)
    query_places = member * tok + jnp.arange(tok, dtype=jnp.int32)
    cosine, sine = angles(query_places)
    key_rot = rotate(key_pre.reshape(tok, KV_HEADS, HEAD_DIM), cosine, sine).astype(BF)
    kv_send = jnp.concatenate([key_rot.reshape(tok, kv_width), value_pre.astype(BF)], axis=1)
    kv_all = spread(kv_send, "fsdp", groups).reshape(groups * tok, 2 * kv_width)
    query_pre = sides(dot(normed, q_own), dot(normed, q_other))
    query_rot = rotate(query_pre.reshape(tok, HEADS, HEAD_DIM), cosine, sine).astype(BF)
    seq_length = groups * tok
    segment_row = segments[0]
    query_segments = lax.dynamic_slice_in_dim(segment_row, member * tok, tok)
    key_heads = kv_all[:, :kv_width].reshape(seq_length, KV_HEADS, HEAD_DIM)
    value_heads = kv_all[:, kv_width:].reshape(seq_length, KV_HEADS, HEAD_DIM)
    scores, grouped = masked_scores(query_rot, key_heads, query_places, query_segments, segment_row)
    row_max = jnp.max(scores, axis=-1, keepdims=True)
    weights = jnp.exp(scores - row_max)
    totals = jnp.sum(weights, axis=-1, keepdims=True)
    probs = (weights / totals).astype(BF)
    log_total = row_max + jnp.log(totals)
    mixed = jnp.einsum("gjqk,kgd->qgjd", probs, value_heads, preferred_element_type=F32)
    mixed = mixed.reshape(tok, HEADS * HEAD_DIM).astype(BF)
    residual = source + sides(dot(mixed, o_own), dot(mixed, o_other))
    scale_two = lax.rsqrt(jnp.mean(residual * residual, axis=-1, keepdims=True) + EPSILON)
    second = (residual * scale_two * gain_two).astype(BF)

    arrived = exchange(dot(one_hot, second).astype(BF), "fsdp")
    gate_w, up_w, down_w = gate_weight[0], up_weight[0], down_weight[0]
    gate_pre = dot(arrived, gate_w)
    up_pre = dot(arrived, up_w)
    sigmoid_gate = jax.nn.sigmoid(gate_pre)
    silu_gate = gate_pre * sigmoid_gate
    hidden = (silu_gate * up_pre).astype(BF)
    grad_hidden = dot_t(arrived_grad, down_w)
    grad_gate_pre = (
        grad_hidden * up_pre * (sigmoid_gate * (1.0 + gate_pre * (1.0 - sigmoid_gate)))
    ).astype(BF)
    grad_up_pre = (grad_hidden * silu_gate).astype(BF)
    grad_rows = (dot_t(grad_gate_pre, gate_w) + dot_t(grad_up_pre, up_w)).astype(BF)
    back_rows = exchange(grad_rows, "fsdp")
    grad_down = t_dot(hidden, arrived_grad).astype(BF)
    grad_gate = t_dot(arrived, grad_gate_pre).astype(BF)
    grad_up = t_dot(arrived, grad_up_pre).astype(BF)
    grad_gate, grad_up, grad_down = lax.psum((grad_gate, grad_up, grad_down), REP)
    expert_out = dot(hidden, down_w).astype(BF)
    returned = exchange(expert_out, "fsdp")
    mixture = t_dot(gate_high, returned) + t_dot(gate_low, returned)
    outputs = (residual + mixture).astype(BF)

    grad_second = t_dot(one_hot, back_rows)
    grad_from_two, gain_two_part = norm_back(residual, scale_two, gain_two, grad_second)
    grad_residual = upstream + grad_from_two
    grad_attended = grad_residual.astype(BF)

    def columns(v, which):
        return lax.dynamic_slice_in_dim(v, which * half, half, 1)

    grad_mixed = dot_t(columns(grad_attended, core), o_own) + dot_t(
        columns(grad_attended, 1 - core), o_other
    )
    grad_mixed = grad_mixed.astype(BF).reshape(tok, KV_HEADS, HEADS // KV_HEADS, HEAD_DIM)

    def core_sum(a, b):
        own = t_dot(a, columns(b, core))
        sent = t_dot(a, columns(b, 1 - core)).astype(BF)
        return (own + swap(sent).astype(F32)).astype(BF)

    def x_sum(v):
        piece = rows // (YLO * XS)
        v = v.reshape(groups, YLO, XS, piece, v.shape[-1])
        x = lax.axis_index("x")

        def part(k):
            return lax.dynamic_index_in_dim(v, lax.rem(x + k, XS), 2, keepdims=False)

        total = part(0).astype(F32)
        for k in range(1, XS):
            got = lax.ppermute(part(k), "x", [(i, (i + k) % XS) for i in range(XS)])
            total = total + got.astype(F32)
        return total.astype(BF)

    o_part = x_sum(core_sum(mixed, grad_attended))
    scores, grouped = masked_scores(query_rot, key_heads, query_places, query_segments, segment_row)
    probs_full = jnp.exp(scores - log_total)
    probs_low = probs_full.astype(BF)
    grad_values_all = jnp.einsum(
        "gjqk,qgjd->kgd", probs_low, grad_mixed, preferred_element_type=F32
    )
    grad_probs = jnp.einsum("qgjd,kgd->gjqk", grad_mixed, value_heads, preferred_element_type=F32)
    inner_sum = jnp.sum(probs_full * grad_probs, axis=-1, keepdims=True)
    grad_scores = (probs_full * (grad_probs - inner_sum)).astype(BF)
    grad_query = jnp.einsum(
        "gjqk,kgd->qgjd", grad_scores, key_heads, preferred_element_type=F32
    ) * HEAD_DIM ** (-0.5)
    grad_keys_all = jnp.einsum(
        "gjqk,qgjd->kgd", grad_scores, grouped, preferred_element_type=F32
    ) * HEAD_DIM ** (-0.5)
    kv_back = jnp.concatenate(
        [
            grad_keys_all.reshape(seq_length, kv_width),
            grad_values_all.reshape(seq_length, kv_width),
        ],
        axis=1,
    ).astype(BF)
    kv_back = exchange(kv_back, "fsdp").reshape(groups, tok, 2 * kv_width)
    kv_back = jnp.sum(kv_back.astype(F32), axis=0)
    grad_query_pre = rotate(grad_query.reshape(tok, HEADS, HEAD_DIM), cosine, -sine)
    grad_query_pre = grad_query_pre.reshape(tok, HEADS * HEAD_DIM).astype(BF)
    q_part = x_sum(core_sum(normed, grad_query_pre))
    grad_key_pre = rotate(
        kv_back[:, :kv_width].reshape(tok, KV_HEADS, HEAD_DIM), cosine, -sine
    )
    grad_key_pre = grad_key_pre.reshape(tok, kv_width).astype(BF)
    grad_value_pre = kv_back[:, kv_width:].astype(BF)
    kv_pre_own = pick(grad_key_pre, grad_value_pre)
    kv_pre_other = pick(grad_value_pre, grad_key_pre)
    kv_sent = t_dot(normed, kv_pre_other).astype(BF)
    kv_part = x_sum((t_dot(normed, kv_pre_own) + swap(kv_sent).astype(F32)).astype(BF))
    grad_normed = (
        dot_t(columns(grad_query_pre, core), q_own)
        + dot_t(columns(grad_query_pre, 1 - core), q_other)
        + dot_t(kv_pre_own, kv_own)
        + dot_t(kv_pre_other, kv_other)
    )
    grad_source, gain_one_part = norm_back(source, scale_one, gain_one, grad_normed)
    input_grad = (grad_residual + grad_source).astype(BF)

    piece = rows // (YLO * XS)
    packed = jnp.concatenate([o_part, q_part, kv_part], axis=-1)
    packed_width = packed.shape[-1]
    packed = packed.transpose(1, 0, 2, 3)
    gain_parts = jnp.stack(
        [gain_one_part.reshape(groups, rows), gain_two_part.reshape(groups, rows)], axis=1
    ).astype(BF)
    gain_parts = jnp.pad(gain_parts, ((0, 0), (0, 6), (0, packed_width - rows)))
    gain_parts = jnp.broadcast_to(gain_parts[None], (YLO,) + gain_parts.shape)
    packed = jnp.concatenate([packed, gain_parts], axis=2)
    packed = packed.reshape(YLO * groups, piece + 8, packed_width)
    packed = exchange(packed, ("ylo", "fsdp"))
    packed = jnp.sum(packed.astype(F32), axis=0).astype(BF)
    spreaded = spread(packed, ("ylo", "x"), YLO * XS)
    grads_own = spreaded[:, :piece].reshape(rows, packed_width)
    gains_own = jnp.sum(spreaded[:XS, piece : piece + 2, :rows].astype(F32), axis=0)
    grads_other = swap(grads_own).astype(F32)
    gains_sum = gains_own + swap(gains_own)
    grads_own = grads_own.astype(F32)

    def cut(start, size):
        return sides(grads_own[:, start : start + size], grads_other[:, start : start + size])

    grad_output_w = cut(0, half)
    grad_query_w = cut(half, half)
    grad_kv_w = cut(2 * half, kv_width)
    return (
        outputs[None],
        input_grad[None],
        gains_sum[0],
        grad_query_w,
        grad_kv_w[:, :kv_width],
        grad_kv_w[:, kv_width:],
        grad_output_w,
        gains_sum[1],
        grad_gate.astype(F32)[None],
        grad_up.astype(F32)[None],
        grad_down.astype(F32)[None],
    )


def solution(mesh):
    shape = mesh.devices.shape
    fine = Mesh(
        mesh.devices.reshape(YLO, XS, CORES, shape[1]), ("ylo", "x", "core", "fsdp")
    )
    return jax.shard_map(
        body,
        mesh=fine,
        in_specs=(
            P(REP, "fsdp", None),
            P(REP, None),
            P("fsdp"),
            P("fsdp", None),
            P("fsdp", None),
            P("fsdp", None),
            P("fsdp", None),
            P("fsdp"),
            P(REP, "fsdp", None),
            P(REP, "fsdp", None),
            P(REP, "fsdp", None),
            P("fsdp", None, None),
            P("fsdp", None, None),
            P("fsdp", None, None),
            P(REP, "fsdp", None),
        ),
        out_specs=(
            P(REP, "fsdp", None),
            P(REP, "fsdp", None),
            P("fsdp"),
            P("fsdp", None),
            P("fsdp", None),
            P("fsdp", None),
            P("fsdp", None),
            P("fsdp"),
            P("fsdp", None, None),
            P("fsdp", None, None),
            P("fsdp", None, None),
        ),
        check_vma=False,
    )
```

```python
import jax
import jax.numpy as jnp
from jax import lax
from jax.experimental import pallas as pl
from jax.experimental.pallas import tpu as pltpu
from jax.sharding import Mesh
from jax.sharding import PartitionSpec as P

HEADS = 12
KV_HEADS = 2
HEAD_DIM = 128
TOP = 4
WINDOW = 1024

EPSILON = 1e-06
THETA = 10000.0
NEGATIVE = -1e30

YLO, XS, CORES = 2, 4, 2
REP = ("ylo", "x", "core")
BF = jnp.bfloat16
F32 = jnp.float32


def angles(positions):
    half_width = HEAD_DIM // 2
    frequency = THETA ** (-(jnp.arange(half_width, dtype=F32) * 2.0) / HEAD_DIM)
    phase = positions.astype(F32)[:, None] * frequency[None, :]
    cosine, sine = jnp.cos(phase), jnp.sin(phase)
    return (
        jnp.concatenate([cosine, cosine], axis=1),
        jnp.concatenate([-sine, sine], axis=1),
    )


def dot(a, b):
    return jnp.dot(a, b, preferred_element_type=F32)


def dot_t(a, b):
    return lax.dot_general(a, b, (((1,), (1,)), ((), ())), preferred_element_type=F32)


def t_dot(a, b):
    return lax.dot_general(a, b, (((0,), (0,)), ((), ())), preferred_element_type=F32)


def add(a, b):
    return (a.astype(F32) + b.astype(F32)).astype(BF)


def turn(piece, cosine, sine):
    return piece * cosine + pltpu.roll(piece, HEAD_DIM // 2, 1) * sine


def turn_back(piece, cosine, sine):
    return piece * cosine - pltpu.roll(piece, HEAD_DIM // 2, 1) * sine


def key_kernel(place, src, gain, raw_own, raw_other, cos, sin, normed_o, scale_o, send_o, weight_o):
    core = place[0]
    groups, kv_rows, width = raw_own.shape
    kv_width = weight_o.shape[1] // 2
    parts = width // kv_width
    source = src[...].astype(F32)
    scale = lax.rsqrt(jnp.mean(source * source, axis=-1, keepdims=True) + EPSILON)
    scale_o[...] = jnp.broadcast_to(scale, scale_o.shape)
    normed = (source * scale * gain[...]).astype(BF)
    normed_o[...] = normed
    for raw, which in ((raw_own, core), (raw_other, 1 - core)):
        at = pl.ds(pl.multiple_of(which * kv_width, kv_width), kv_width)
        for f in range(groups):
            for j in range(parts):
                weight_o[pl.ds((f * parts + j) * kv_rows, kv_rows), at] = raw[
                    f, :, pl.ds(j * kv_width, kv_width)
                ]
    pre = dot(normed, weight_o[...])
    for head in range(2 * KV_HEADS):
        low, high = head * HEAD_DIM, (head + 1) * HEAD_DIM
        piece = pre[:, low:high]
        if head < KV_HEADS:
            piece = turn(piece, cos[...], sin[...])
        for f in range(groups):
            send_o[f, :, low:high] = piece.astype(BF)


def put_weight(place, weight_o, pieces, which, spots):
    groups, quarter, half = pieces[0].shape
    at = pl.ds(pl.multiple_of(which * half, half), half)
    for block, (s, t) in zip(pieces, spots):
        for f in range(groups):
            start = (f * XS + 2 * s + t) * quarter
            weight_o[pl.ds(pl.multiple_of(start, quarter), quarter), at] = block[f]


def query_kernel(place, normed, a, b, c, d, e, f, g, h, cos, sin, weight_o, query_o):
    core, s, t = place[0], place[2], place[3]
    spots = ((s, t), (s, 1 - t), (1 - s, t), (1 - s, 1 - t))
    put_weight(place, weight_o, (a, b, c, d), core, spots)
    put_weight(place, weight_o, (e, f, g, h), 1 - core, spots)
    pre = dot(normed[...], weight_o[...])
    for head in range(HEADS):
        low, high = head * HEAD_DIM, (head + 1) * HEAD_DIM
        query_o[:, low:high] = turn(pre[:, low:high], cos[...], sin[...]).astype(BF)


def attend_kernel(place, q, kv, seg_row, seg_col, mixed_o, probs_o, bias):
    base = place[1]
    length, tok = bias.shape
    kv_width = kv.shape[1] // 2
    key_place = lax.broadcasted_iota(jnp.int32, (length, tok), 0)
    query_place = base + lax.broadcasted_iota(jnp.int32, (length, tok), 1)
    allowed = (
        (key_place <= query_place)
        & (query_place - key_place < WINDOW)
        & (seg_col[...] == seg_row[...])
    )
    bias[...] = jnp.where(allowed, 0.0, NEGATIVE)
    for head in range(HEADS):
        group = head // (HEADS // KV_HEADS)
        at = pl.ds(head * HEAD_DIM, HEAD_DIM)
        keys = kv[:, pl.ds(group * HEAD_DIM, HEAD_DIM)]
        values = kv[:, pl.ds(kv_width + group * HEAD_DIM, HEAD_DIM)]
        scores = dot_t(keys, q[:, at]) * HEAD_DIM ** (-0.5) + bias[...]
        weights = jnp.exp(scores - jnp.max(scores, axis=0, keepdims=True))
        probs = (weights * (1.0 / jnp.sum(weights, axis=0, keepdims=True))).astype(BF)
        probs_o[head] = probs
        mixed_o[:, at] = t_dot(probs, values).astype(BF)


def residual_kernel(
    place, mixed, a, b, c, d, e, f, g, h, src, gain, hot, weight_o, resid_o, scale_o, send_o
):
    core, s, t = place[0], place[2], place[3]
    spots = ((s, t), (1 - s, t), (s, 1 - t), (1 - s, 1 - t))
    put_weight(place, weight_o, (a, b, c, d), core, spots)
    put_weight(place, weight_o, (e, f, g, h), 1 - core, spots)
    resid = src[...].astype(F32) + dot(mixed[...], weight_o[...])
    resid_o[...] = resid
    scale = lax.rsqrt(jnp.mean(resid * resid, axis=-1, keepdims=True) + EPSILON)
    scale_o[...] = jnp.broadcast_to(scale, scale_o.shape)
    second = (resid * scale * gain[...]).astype(BF)
    send_o[...] = dot(hot[...], second).astype(BF)


def expert_kernel(place, rows, grad_hidden, gate_w, up_w, hidden_o, pre_o, back_o):
    core = place[0]
    count = rows.shape[0]
    step = count // 2
    for low in range(0, count, step):
        at = pl.ds(low, step)
        block = rows[at, :]
        gate = dot(block, gate_w[...])
        up = dot(block, up_w[...])
        sigmoid = 1.0 / (1.0 + jnp.exp(-gate))
        silu = gate * sigmoid
        hidden_o[at, :] = (silu * up).astype(BF)
        grad = grad_hidden[at, :]
        grad_gate = (grad * up * (sigmoid * (1.0 + gate * (1.0 - sigmoid)))).astype(BF)
        grad_up = (grad * silu).astype(BF)
        pre_o[core, at, :] = grad_gate
        pre_o[1 - core, at, :] = grad_up
        back_o[at, :] = (dot_t(grad_gate, gate_w[...]) + dot_t(grad_up, up_w[...])).astype(BF)


def sent_expert_kernel(place, rows, pre, hidden, arrived, out):
    width, half = rows.shape[1], hidden.shape[1]
    upper = arrived[:, pl.ds(pl.multiple_of((1 - place[0]) * half, half), half)]
    step = 256
    for low in range(0, width, step):
        out[pl.ds(low, step), :] = t_dot(rows[:, pl.ds(low, step)], pre[1]).astype(BF)
    for low in range(0, half, step):
        out[pl.ds(width + low, step), :] = t_dot(hidden[:, pl.ds(low, step)], upper).astype(BF)


def own_expert_kernel(
    place, rows, pre, hidden, arrived, got, down_w, keep_a, send_a, keep_b, send_b, out_o, total
):
    s, t = place[2], place[3]
    width, half = rows.shape[1], hidden.shape[1]
    upper = arrived[:, pl.ds(pl.multiple_of(place[0] * half, half), half)]
    step = 256
    for low in range(0, width, step):
        at = pl.ds(low, step)
        total[at, :] = (t_dot(rows[:, at], pre[0]) + got[at, :].astype(F32)).astype(BF)
    for low in range(0, half, step):
        at = pl.ds(width + low, step)
        part = t_dot(hidden[:, pl.ds(low, step)], upper)
        total[at, :] = (part + got[at, :].astype(F32)).astype(BF)
    big, small = width // 8, half // 8
    for out, side, spots in (
        (send_a, 0, ((1 - s, 0), (1 - s, 1))),
        (keep_a, 0, ((s, 0), (s, 1))),
        (send_b, 1, ((0, 1 - t), (1, 1 - t))),
        (keep_b, 1, ((0, t), (1, t))),
    ):
        for j, (row_s, row_t) in enumerate(spots):
            piece = side * 4 + 2 * row_s + row_t
            out[j, pl.ds(0, big), :] = total[pl.ds(pl.multiple_of(piece * big, big), big), :]
            start = pl.multiple_of(width + piece * small, small)
            out[j, pl.ds(big, small), :] = total[pl.ds(start, small), :]
    out_o[...] = dot(hidden[...], down_w[...]).astype(BF)


def expert_step_kernel(place, keep_a, got_a, keep_b, got_b, keep_ao, send_ao, keep_bo, send_bo):
    s, t = place[2], place[3]
    keep_ao[...] = add(keep_a[t], got_a[t])
    send_ao[...] = add(keep_a[1 - t], got_a[1 - t])
    keep_bo[...] = add(keep_b[s], got_b[s])
    send_bo[...] = add(keep_b[1 - s], got_b[1 - s])


def expert_end_kernel(place, keep_a, got_a, keep_b, got_b, out):
    out[0] = add(keep_a[...], got_a[...])
    out[1] = add(keep_b[...], got_b[...])


def pair_kernel(place, a, b, out):
    out[...] = add(a[...], b[...])


def expert_out_kernel(place, *refs):
    core, s, t = place[0], place[2], place[3]
    gate_o, up_o, down_o = refs[10:]
    width, half = gate_o.shape
    big, small = width // 8, half // 8

    def put(pieces, which, first):
        own, one_a, one_b, two_a, two_b = pieces
        blocks = (
            (0, s, t, own.at[0]),
            (0, s, 1 - t, one_a),
            (0, 1 - s, t, two_a.at[0]),
            (0, 1 - s, 1 - t, two_a.at[1]),
            (1, s, t, own.at[1]),
            (1, 1 - s, t, one_b),
            (1, s, 1 - t, two_b.at[0]),
            (1, 1 - s, 1 - t, two_b.at[1]),
        )
        at = pl.ds(pl.multiple_of(which * half, half), half)
        for side, row_s, row_t, block in blocks:
            piece = side * 4 + 2 * row_s + row_t
            first[pl.ds(pl.multiple_of(piece * big, big), big), :] = block[
                pl.ds(0, big), :
            ].astype(F32)
            down_o[pl.ds(pl.multiple_of(piece * small, small), small), at] = block[
                pl.ds(big, small), :
            ].astype(F32)

    @pl.when(core == 0)
    def _():
        put(refs[:5], 0, gate_o)
        put(refs[5:10], 1, up_o)

    @pl.when(core == 1)
    def _():
        put(refs[:5], 1, up_o)
        put(refs[5:10], 0, gate_o)


def back_kernel(
    place, back, hot_t, resid_i, scale_i, gain, cot, weight, probs_i, kv, q, cos, sin,
    grad_resid_o, attended_o, gain_o, query_o, kv_o,
):
    kv_width = kv.shape[1] // 2
    resid = resid_i[...]
    scale = scale_i[:, :1]
    grad_second = dot(hot_t[...], back[...])
    weighted = grad_second * gain[...]
    inner = jnp.sum(weighted * resid, axis=-1, keepdims=True)
    grad_resid = (
        cot[...].astype(F32)
        + scale * weighted
        - resid * (scale * scale * scale * inner * (1.0 / resid.shape[-1]))
    )
    gain_o[...] = jnp.sum(grad_second * resid * scale, axis=0, keepdims=True)
    grad_resid_o[...] = grad_resid
    attended = grad_resid.astype(BF)
    attended_o[...] = attended
    grad_mixed = dot_t(attended, weight[...]).astype(BF)
    heads = HEADS // KV_HEADS
    for group in range(KV_HEADS):
        keys = kv[:, pl.ds(group * HEAD_DIM, HEAD_DIM)]
        values = kv[:, pl.ds(kv_width + group * HEAD_DIM, HEAD_DIM)]
        grad_keys = jnp.zeros(keys.shape, F32)
        grad_values = jnp.zeros(keys.shape, F32)
        for head in range(group * heads, (group + 1) * heads):
            low, high = head * HEAD_DIM, (head + 1) * HEAD_DIM
            upper = grad_mixed[:, low:high]
            probs = probs_i[head]
            wide = probs.astype(F32)
            grad_probs = dot_t(values, upper)
            total = jnp.sum(wide * grad_probs, axis=0, keepdims=True)
            grad_scores = (wide * (grad_probs - total)).astype(BF)
            grad_values = grad_values + dot(probs, upper)
            grad_keys = grad_keys + dot(grad_scores, q[:, low:high])
            grad_query = t_dot(grad_scores, keys) * HEAD_DIM ** (-0.5)
            query_o[:, low:high] = turn_back(grad_query, cos[...], sin[...]).astype(BF)
        at = pl.ds(group * HEAD_DIM, HEAD_DIM)
        kv_o[:, at] = (grad_keys * HEAD_DIM ** (-0.5)).astype(BF)
        kv_o[:, pl.ds(kv_width + group * HEAD_DIM, HEAD_DIM)] = grad_values.astype(BF)


def square_weight_kernel(own, place, mixed, attended, normed, query, out):
    half = mixed.shape[1] // 2
    which = place[0] if own else 1 - place[0]
    at = pl.ds(pl.multiple_of(which * half, half), half)
    step = 256
    for k, (left, right) in enumerate(((mixed, attended), (normed, query))):
        part = right[:, at]
        for low in range(0, 2 * half, step):
            out[k, pl.ds(low, step), :] = t_dot(left[:, pl.ds(low, step)], part).astype(BF)


def split_kernel(place, own_a, got_a, own_b, got_b, keep_a, send_a, keep_b, send_b):
    s, t = place[2], place[3]
    groups, _, quarter, _ = keep_a.shape
    for f in range(groups):
        for j in range(2):
            for out, own, got, row_s, row_t in (
                (send_a, own_a, got_a, 1 - s, j),
                (keep_a, own_a, got_a, s, j),
                (send_b, own_b, got_b, j, 1 - t),
                (keep_b, own_b, got_b, j, t),
            ):
                start = (f * XS + 2 * row_s + row_t) * quarter
                at = pl.ds(pl.multiple_of(start, quarter), quarter)
                out[f, j] = add(own[at, :], got[at, :])


def step_kernel(
    place, qk_a, qg_a, kk_a, kg_a, qk_b, qg_b, kk_b, kg_b, keep_a, send_a, keep_b, send_b
):
    s, t = place[2], place[3]
    size = qk_a.shape[-1]
    extra = kk_a.shape[-1]
    groups = qk_a.shape[0]
    for f in range(groups):
        for out, which, big, big_got, small, small_got in (
            (send_a, 1 - t, qk_a, qg_a, kk_a, kg_a),
            (keep_a, t, qk_a, qg_a, kk_a, kg_a),
            (send_b, 1 - s, qk_b, qg_b, kk_b, kg_b),
            (keep_b, s, qk_b, qg_b, kk_b, kg_b),
        ):
            out[f, :, pl.ds(0, size)] = add(big[f, which], big_got[f, which])
            out[f, :, pl.ds(size, extra)] = add(small[f, which], small_got[f, which])


def pack_kernel(place, keep_a, got_a, keep_b, got_b, gains, out):
    size = keep_a.shape[-1]
    for y, (keep, got) in enumerate(((keep_a, got_a), (keep_b, got_b))):
        out[y, :, :, pl.ds(0, size)] = add(keep[...], got[...])
        out[y, :, :, pl.ds(size, gains.shape[-1])] = gains[...]


def sum_kernel(place, parts, out):
    total = parts[0].astype(F32)
    for k in range(1, parts.shape[0]):
        total = total + parts[k].astype(F32)
    total = total.astype(BF)
    for k in range(out.shape[0]):
        out[k] = total


def final_kernel(place, own, other, output_o, query_o, key_o, value_o, gains_o):
    core = place[0]
    quarter = own.shape[1]
    half = output_o.shape[1] // 2
    part = key_o.shape[1] // 2
    size = half + part
    for refs, which in ((own, core), (other, 1 - core)):
        at = pl.ds(pl.multiple_of(which * half, half), half)
        for piece, x in enumerate(PLACE):
            rows = pl.ds(piece * quarter, quarter)
            output_o[rows, at] = refs[x, :, pl.ds(0, half)].astype(F32)
            query_o[rows, at] = refs[XS + x, :, pl.ds(0, half)].astype(F32)
    for piece, x in enumerate(PLACE):
        rows = pl.ds(piece * quarter, quarter)
        for y in range(2):
            at = pl.ds(y * part, part)
            mine = own[y * XS + x, :, pl.ds(half, part)].astype(F32)
            others = other[y * XS + x, :, pl.ds(half, part)].astype(F32)
            even = core == 0
            key_o[rows, at] = jnp.where(even, mine, others)
            value_o[rows, at] = jnp.where(even, others, mine)
    total = jnp.zeros(gains_o.shape, F32)
    for refs in (own, other):
        for x in range(XS):
            total = total + refs[x, :, pl.ds(size, gains_o.shape[1])].astype(F32)
    gains_o[...] = total


def key_weight_kernel(place, parts, cos, sin, normed, own_o, sent_o, pre_o):
    core = place[0]
    kv_width = parts.shape[-1] // 2
    total = parts[0].astype(F32)
    for k in range(1, parts.shape[0]):
        total = total + parts[k].astype(F32)
    for head in range(2 * KV_HEADS):
        low, high = head * HEAD_DIM, (head + 1) * HEAD_DIM
        piece = total[:, low:high]
        if head < KV_HEADS:
            piece = turn_back(piece, cos[...], sin[...])
        pre_o[:, low:high] = piece.astype(BF)
    for out, which in ((sent_o, 1 - core), (own_o, core)):
        part = pre_o[:, pl.ds(pl.multiple_of(which * kv_width, kv_width), kv_width)]
        grad = t_dot(normed[...], part).astype(BF)
        out[0] = grad[:, : kv_width // 2]
        out[1] = grad[:, kv_width // 2 :]


def input_kernel(
    place, query, pre, src, scale_i, gain, query_w, kv_w, grad_resid, input_o, gain_o
):
    grad_normed = dot_t(query[...], query_w[...]) + dot_t(pre[...], kv_w[...])
    source = src[...].astype(F32)
    scale = scale_i[:, :1]
    weighted = grad_normed * gain[...]
    inner = jnp.sum(weighted * source, axis=-1, keepdims=True)
    input_o[...] = (
        grad_resid[...]
        + scale * weighted
        - source * (scale * scale * scale * inner * (1.0 / source.shape[-1]))
    ).astype(BF)
    gain_o[...] = jnp.sum(grad_normed * source * scale, axis=0, keepdims=True)


def call(kernel, args, outs, scratch=(), micros=0):
    return pl.pallas_call(
        kernel,
        out_shape=[jax.ShapeDtypeStruct(shape, kind) for shape, kind in outs],
        in_specs=[pl.BlockSpec(memory_space=pltpu.SMEM)]
        + [pl.BlockSpec(memory_space=pltpu.VMEM)] * (len(args) - 1),
        out_specs=[pl.BlockSpec(memory_space=pltpu.VMEM)] * len(outs),
        scratch_shapes=list(scratch),
        compiler_params=pltpu.CompilerParams(vmem_limit_bytes=48 * 1024 * 1024),
        cost_estimate=pl.CostEstimate(flops=int(micros * 1e9), bytes_accessed=0, transcendentals=0),
    )(*args)


def swap(v):
    return lax.ppermute(v, "core", [(0, 1), (1, 0)])


def swap_y(v):
    return lax.ppermute(v, "ylo", [(0, 1), (1, 0)])


def exchange(v, axis):
    return lax.all_to_all(v, axis, 0, 0, tiled=True)


def copies(v, n):
    return lax.optimization_barrier(jnp.broadcast_to(v[None], (n,) + v.shape))


def tie(*values):
    return lax.optimization_barrier(values)


PAIRS_S = [(0, 1), (1, 0), (2, 3), (3, 2)]
PAIRS_T = [(0, 3), (3, 0), (1, 2), (2, 1)]
PLACE = (0, 3, 1, 2)


def x_bits():
    x = lax.axis_index("x")
    return ((x + 1) // 2) % 2, x // 2


def flip(v, pairs):
    return lax.ppermute(v, "x", pairs)


def body(
    inputs,
    segments,
    first_gain,
    query_matrix,
    key_matrix,
    value_matrix,
    output_matrix,
    second_gain,
    expert_ids,
    gate_values,
    priority,
    gate_weight,
    up_weight,
    down_weight,
    cotangent,
):
    tok = inputs.shape[1]
    width = inputs.shape[2]
    rows = query_matrix.shape[0]
    groups = lax.axis_size("fsdp")
    member = lax.axis_index("fsdp")
    core = lax.axis_index("core")
    even = core == 0
    experts = groups
    capacity = 5 * tok * TOP // (4 * experts)
    slots_all = experts * capacity
    half = width // 2
    kv_width = key_matrix.shape[1]
    length = groups * tok
    quarter = rows // XS
    bit_s, bit_t = x_bits()
    place_at = jnp.stack([core, member * tok, bit_s, bit_t]).astype(jnp.int32)

    def pick(a, b):
        return jnp.where(even, a, b)

    def qo_blocks(q_spot, o_spot):
        return jnp.concatenate(
            [
                lax.dynamic_slice(
                    matrix, ((2 * spot[0] + spot[1]) * quarter, core * half), (quarter, half)
                )
                for matrix, spot in ((query_matrix, q_spot), (output_matrix, o_spot))
            ],
            axis=1,
        )

    parts = width // kv_width
    kv_rows = rows // parts
    kv_half = pick(key_matrix, value_matrix).reshape(parts, kv_rows, kv_width)
    kv_piece = jnp.concatenate([kv_half[j] for j in range(parts)], axis=1)
    gains = jnp.pad(jnp.stack([first_gain, second_gain]), ((0, 6), (0, width - rows)))
    qo_first = qo_blocks((bit_s, bit_t), (bit_s, bit_t))
    qo_second = qo_blocks((bit_s, 1 - bit_t), (1 - bit_s, bit_t))
    gathered = exchange(
        copies(jnp.concatenate([kv_piece, gains, qo_first], axis=0), groups), "fsdp"
    )

    ids = expert_ids[0].reshape(-1)
    order = priority[0, 0]
    earlier = (order[None, :] < order[:, None]) & (ids[None, :] == ids[:, None])
    slots = jnp.sum(earlier.astype(jnp.int32), axis=1)
    kept = slots < capacity
    expert_list = jnp.arange(experts, dtype=jnp.int32)
    chosen = (ids[:, None] == expert_list[None, :]) & kept[:, None]
    slot_of = jnp.sum(
        jnp.where(chosen, slots[:, None] + 1, 0).reshape(tok, TOP, experts), axis=1
    )
    slot_of = slot_of - 1
    gate_table = jnp.sum(
        jnp.where(chosen, gate_values[0].reshape(-1)[:, None], 0.0).reshape(tok, TOP, experts),
        axis=1,
    )
    slot_list = jnp.arange(capacity, dtype=jnp.int32)
    hits = slot_of.T[:, None, :] == slot_list[None, :, None]
    one_hot = hits.astype(BF).reshape(slots_all, tok)
    gate_hot = jnp.where(hits, gate_table.T[:, None, :], 0.0).reshape(slots_all, tok)
    slot_gate = jnp.sum(gate_hot, axis=1, keepdims=True)
    gate_high = gate_hot.astype(BF)
    gate_low = (gate_hot - gate_high.astype(F32)).astype(BF)
    send_grad = (dot(one_hot, cotangent[0]) * slot_gate).astype(BF)

    cosine, sine = angles(member * tok + jnp.arange(tok, dtype=jnp.int32))
    segment_row = segments[0]
    query_segments = lax.dynamic_slice_in_dim(segment_row, member * tok, tok)
    segment_column = segment_row[:, None]
    one_hot_t = one_hot.T
    qo_second = copies(qo_second, groups)
    (gathered, qo_second, one_hot, one_hot_t, gate_high, gate_low, send_grad, cosine, sine,
     segment_column, place_at) = tie(
        gathered, qo_second, one_hot, one_hot_t, gate_high, gate_low, send_grad, cosine, sine,
        segment_column, place_at)
    kv_raw = gathered[:, :kv_rows]
    gain_one = gathered[:, kv_rows, :rows].reshape(1, width).astype(F32)
    gain_two = gathered[:, kv_rows + 1, :rows].reshape(1, width).astype(F32)
    second_blocks = exchange(qo_second, "fsdp")
    kv_raw_other = swap(kv_raw)
    q_first, o_first = gathered[:, kv_rows + 8 :, :half], gathered[:, kv_rows + 8 :, half:]

    square = (width, width)
    normed, scale_one, kv_send, kv_weight = call(
        key_kernel,
        [place_at, inputs[0], gain_one, kv_raw, kv_raw_other, cosine, sine],
        [((tok, width), BF), ((tok, HEAD_DIM), F32), ((groups, tok, 2 * kv_width), BF),
         ((width, 2 * kv_width), BF)],
    )
    kv_send, second_blocks = tie(kv_send, second_blocks)
    q_second, o_second = second_blocks[..., :half], second_blocks[..., half:]
    kv_all = exchange(kv_send, "fsdp").reshape(length, 2 * kv_width)
    send_grad, kv_all = tie(send_grad, kv_all)
    arrived_grad = exchange(send_grad, "fsdp")
    q_own = (q_first, q_second, flip(q_first, PAIRS_S), flip(q_second, PAIRS_S))
    o_own = (o_first, o_second, flip(o_first, PAIRS_T), flip(o_second, PAIRS_T))
    q_other = tuple(swap(v) for v in q_own)
    o_other = tuple(swap(v) for v in o_own)
    query_weight, query_rot = call(
        query_kernel,
        [place_at, normed, *q_own, *q_other, cosine, sine],
        [(square, BF), ((tok, width), BF)],
    )
    mixed, probs = call(
        attend_kernel,
        [place_at, query_rot, kv_all, query_segments[None], segment_column],
        [((tok, width), BF), ((HEADS, length, tok), BF)],
        [pltpu.VMEM((length, tok), F32)],
    )
    output_weight, residual, scale_two, send_rows = call(
        residual_kernel,
        [place_at, mixed, *o_own, *o_other, inputs[0], gain_two, one_hot],
        [(square, BF), ((tok, width), F32), ((tok, HEAD_DIM), F32), ((slots_all, width), BF)],
    )

    send_rows, arrived_grad = tie(send_rows, arrived_grad)
    arrived = exchange(send_rows, "fsdp")
    grad_hidden = dot_t(arrived_grad, down_weight[0])
    arrived, grad_hidden = tie(arrived, grad_hidden)
    hidden, grad_pre, grad_rows = call(
        expert_kernel,
        [place_at, arrived, grad_hidden, gate_weight[0], up_weight[0]],
        [((slots_all, half), BF), ((2, slots_all, half), BF), ((slots_all, width), BF)],
    )
    back_rows = exchange(grad_rows, "fsdp")
    expert_rows = width + half

    e_sent = call(
        sent_expert_kernel,
        [place_at, arrived, grad_pre, hidden, arrived_grad],
        [((expert_rows, half), BF)],
        micros=40,
    )[0]
    e_part = (2, expert_rows // 8, half)
    e_keep_a, e_send_a, e_keep_b, e_send_b, expert_out = call(
        own_expert_kernel,
        [place_at, arrived, grad_pre, hidden, arrived_grad, swap(e_sent), down_weight[0]],
        [(e_part, BF)] * 4 + [((slots_all, width), BF)],
        [pltpu.VMEM((expert_rows, half), BF)],
    )
    e_got_a, e_got_b = flip(e_send_a, PAIRS_S), flip(e_send_b, PAIRS_T)
    back_rows, expert_out, e_keep_a, e_keep_b = tie(back_rows, expert_out, e_keep_a, e_keep_b)

    grad_residual, grad_attended, gain_two_part, grad_query_pre, kv_back = call(
        back_kernel,
        [place_at, back_rows, one_hot_t, residual, scale_two, gain_two, cotangent[0],
         output_weight, probs, kv_all, query_rot, cosine, sine],
        [((tok, width), F32), ((tok, width), BF), ((1, width), F32), ((tok, width), BF),
         ((length, 2 * kv_width), BF)],
    )
    kv_back, e_got_a, e_got_b = tie(kv_back, e_got_a, e_got_b)
    kv_got = exchange(kv_back, "fsdp")
    e_keep_a, e_send_a, e_keep_b, e_send_b = call(
        expert_step_kernel,
        [place_at, e_keep_a, e_got_a, e_keep_b, e_got_b],
        [(e_part[1:], BF)] * 4,
    )
    e_got_a, e_got_b = flip(e_send_a, PAIRS_T), flip(e_send_b, PAIRS_S)

    def square_weights(own, micros):
        def kernel(*refs):
            square_weight_kernel(own, *refs)

        return call(
            kernel,
            [place_at, mixed, grad_attended, normed, grad_query_pre],
            [((2, width, half), BF)],
            micros=micros,
        )[0]

    qo_got = swap(square_weights(False, 30))
    qo_own = square_weights(True, 0)
    big_part, small_part = (groups, 2, quarter, half), (groups, 2, quarter, kv_width // 2)
    qo_keep_a, qo_send_a, qo_keep_b, qo_send_b = call(
        split_kernel,
        [place_at, qo_own[0], qo_got[0], qo_own[1], qo_got[1]],
        [(big_part, BF)] * 4,
    )
    kv_got, expert_out, qo_send_a, qo_send_b, e_got_a, e_got_b = tie(
        kv_got, expert_out, qo_send_a, qo_send_b, e_got_a, e_got_b
    )
    qo_got_a, qo_got_b = flip(qo_send_a, PAIRS_S), flip(qo_send_b, PAIRS_T)
    returned = exchange(expert_out, "fsdp")
    kv_grad_own, kv_grad_sent, grad_kv_pre = call(
        key_weight_kernel,
        [place_at, kv_got.reshape(groups, tok, 2 * kv_width), cosine, sine, normed],
        [((2, width, kv_width // 2), BF)] * 2 + [((tok, 2 * kv_width), BF)],
        micros=30,
    )
    kv_grad_got = swap(kv_grad_sent)
    kv_keep_a, kv_send_a, kv_keep_b, kv_send_b = call(
        split_kernel,
        [place_at, kv_grad_own[0], kv_grad_got[0], kv_grad_own[1], kv_grad_got[1]],
        [(small_part, BF)] * 4,
    )
    kv_got_a, kv_got_b = flip(kv_send_a, PAIRS_S), flip(kv_send_b, PAIRS_T)
    e_sum = call(
        expert_end_kernel,
        [place_at, e_keep_a, e_got_a, e_keep_b, e_got_b],
        [(e_part, BF)],
    )[0]
    e_other_y = swap_y(e_sum)
    input_grad, gain_one_part = call(
        input_kernel,
        [place_at, grad_query_pre, grad_kv_pre, inputs[0], scale_one, gain_one, query_weight,
         kv_weight, grad_residual],
        [((tok, width), BF), ((1, width), F32)],
    )

    both_part = (groups, quarter, half + kv_width // 2)
    keep_a, send_a, keep_b, send_b = call(
        step_kernel,
        [place_at, qo_keep_a, qo_got_a, kv_keep_a, kv_got_a, qo_keep_b, qo_got_b, kv_keep_b,
         kv_got_b],
        [(both_part, BF)] * 4,
    )
    got_a, got_b = flip(send_a, PAIRS_T), flip(send_b, PAIRS_S)
    spare = HEAD_DIM
    gain_parts = jnp.stack([gain_one_part, gain_two_part]).reshape(2, groups, quarter, XS)
    gain_parts = gain_parts.transpose(1, 2, 0, 3).reshape(groups, quarter, 2 * XS).astype(BF)
    gain_parts = jnp.pad(gain_parts, ((0, 0), (0, 0), (0, spare - 2 * XS)))
    packed_width = both_part[-1] + spare
    packed = call(
        pack_kernel,
        [place_at, keep_a, got_a, keep_b, got_b, gain_parts],
        [((YLO, groups, quarter, packed_width), BF)],
    )[0]
    packed, returned, e_sum, e_other_y = tie(packed, returned, e_sum, e_other_y)
    packed = exchange(packed.reshape(YLO * groups, quarter, packed_width), ("ylo", "fsdp"))
    e_sum = call(pair_kernel, [place_at, e_sum, e_other_y], [(e_part, BF)])[0]
    e_one_a, e_one_b = flip(e_sum[0], PAIRS_T), flip(e_sum[1], PAIRS_S)
    e_two_a = flip(jnp.stack([e_sum[0], e_one_a]), PAIRS_S)
    e_two_b = flip(jnp.stack([e_sum[1], e_one_b]), PAIRS_T)
    e_pieces = [e_sum, e_one_a, e_one_b, e_two_a, e_two_b]
    grad_gate, grad_up, grad_down = call(
        expert_out_kernel,
        [place_at, *e_pieces, *[swap(v) for v in e_pieces]],
        [((width, half), F32), ((width, half), F32), ((half, width), F32)],
    )
    mixture = t_dot(gate_high, returned) + t_dot(gate_low, returned)
    outputs = (residual + mixture).astype(BF)
    packed = call(sum_kernel, [place_at, packed], [((YLO * XS, quarter, packed_width), BF)])[0]
    spreaded = exchange(packed, ("ylo", "x"))
    grad_output_w, grad_query_w, grad_key_w, grad_value_w, gains_sum = call(
        final_kernel,
        [place_at, spreaded, swap(spreaded)],
        [((rows, width), F32), ((rows, width), F32), ((rows, kv_width), F32),
         ((rows, kv_width), F32), ((quarter, spare), F32)],
    )
    gains_sum = gains_sum[:, : 2 * XS].reshape(quarter, 2, XS).transpose(1, 0, 2)
    gains_sum = gains_sum.reshape(2, rows)
    return (
        outputs[None],
        input_grad[None],
        gains_sum[0],
        grad_query_w,
        grad_key_w,
        grad_value_w,
        grad_output_w,
        gains_sum[1],
        grad_gate[None],
        grad_up[None],
        grad_down[None],
    )


def solution(mesh):
    shape = mesh.devices.shape
    fine = Mesh(
        mesh.devices.reshape(YLO, XS, CORES, shape[1]), ("ylo", "x", "core", "fsdp")
    )
    return jax.shard_map(
        body,
        mesh=fine,
        in_specs=(
            P(REP, "fsdp", None),
            P(REP, None),
            P("fsdp"),
            P("fsdp", None),
            P("fsdp", None),
            P("fsdp", None),
            P("fsdp", None),
            P("fsdp"),
            P(REP, "fsdp", None),
            P(REP, "fsdp", None),
            P(REP, "fsdp", None),
            P("fsdp", None, None),
            P("fsdp", None, None),
            P("fsdp", None, None),
            P(REP, "fsdp", None),
        ),
        out_specs=(
            P(REP, "fsdp", None),
            P(REP, "fsdp", None),
            P("fsdp"),
            P("fsdp", None),
            P("fsdp", None),
            P("fsdp", None),
            P("fsdp", None),
            P("fsdp"),
            P("fsdp", None, None),
            P("fsdp", None, None),
            P("fsdp", None, None),
        ),
        check_vma=False,
    )
```

```python
import jax
import jax.numpy as jnp
from jax import lax
from jax.experimental import pallas as pl
from jax.experimental.pallas import tpu as pltpu
from jax.sharding import Mesh
from jax.sharding import PartitionSpec as P

HEADS = 12
KV_HEADS = 2
HEAD_DIM = 128
TOP = 4
WINDOW = 1024

EPSILON = 1e-06
THETA = 10000.0
NEGATIVE = -1e30

YLO, XS, CORES = 2, 4, 2
REP = ("ylo", "x", "core")
BF = jnp.bfloat16
F32 = jnp.float32


def angles(positions):
    half_width = HEAD_DIM // 2
    frequency = THETA ** (-(jnp.arange(half_width, dtype=F32) * 2.0) / HEAD_DIM)
    phase = positions.astype(F32)[:, None] * frequency[None, :]
    cosine, sine = jnp.cos(phase), jnp.sin(phase)
    return (
        jnp.concatenate([cosine, cosine], axis=1),
        jnp.concatenate([-sine, sine], axis=1),
    )


def dot(a, b):
    return jnp.dot(a, b, preferred_element_type=F32)


def dot_t(a, b):
    return lax.dot_general(a, b, (((1,), (1,)), ((), ())), preferred_element_type=F32)


def t_dot(a, b):
    return lax.dot_general(a, b, (((0,), (0,)), ((), ())), preferred_element_type=F32)


def add(a, b):
    return (a.astype(F32) + b.astype(F32)).astype(BF)


def turn(piece, cosine, sine):
    return piece * cosine + pltpu.roll(piece, HEAD_DIM // 2, 1) * sine


def turn_back(piece, cosine, sine):
    return piece * cosine - pltpu.roll(piece, HEAD_DIM // 2, 1) * sine


def stacked(ref, pair):
    low = 2 * pair * HEAD_DIM
    return jnp.concatenate(
        [ref[:, pl.ds(low, HEAD_DIM)], ref[:, pl.ds(low + HEAD_DIM, HEAD_DIM)]], axis=0
    )


def unstack(ref, pair, value):
    low, rows = 2 * pair * HEAD_DIM, value.shape[0] // 2
    ref[:, pl.ds(low, HEAD_DIM)] = value[:rows]
    ref[:, pl.ds(low + HEAD_DIM, HEAD_DIM)] = value[rows:]


def key_kernel(place, src, gain, raw_own, raw_other, cos, sin, normed_o, scale_o, send_o, weight_o):
    core = place[0]
    groups, kv_rows, width = raw_own.shape
    kv_width = weight_o.shape[1] // 2
    parts = width // kv_width
    source = src[...].astype(F32)
    scale = lax.rsqrt(jnp.mean(source * source, axis=-1, keepdims=True) + EPSILON)
    scale_o[...] = jnp.broadcast_to(scale, scale_o.shape)
    normed = (source * scale * gain[...]).astype(BF)
    normed_o[...] = normed
    send(scale_o, normed_o)
    for raw, which in ((raw_own, core), (raw_other, 1 - core)):
        at = pl.ds(pl.multiple_of(which * kv_width, kv_width), kv_width)
        for f in range(groups):
            for j in range(parts):
                weight_o[pl.ds((f * parts + j) * kv_rows, kv_rows), at] = raw[
                    f, :, pl.ds(j * kv_width, kv_width)
                ]
    send(weight_o)
    pre = dot(normed, weight_o[...])
    for head in range(2 * KV_HEADS):
        low, high = head * HEAD_DIM, (head + 1) * HEAD_DIM
        piece = pre[:, low:high]
        if head < KV_HEADS:
            piece = turn(piece, cos[...], sin[...])
        for f in range(groups):
            send_o[f, :, low:high] = piece.astype(BF)


def front_kernel(place, normed, kv, bias, src, gain, hot_t, cos, sin, *refs):
    pieces = refs[:8]
    query_w, output_w, query_o, mixed_o, probs_o, resid_o, scale_o, send_o, sems = refs[8:]
    core, s, t = place[0], place[2], place[3]
    _, rows, half = pieces[0].shape
    copies = []
    for n, block in enumerate(pieces):
        weight, bit = ((query_w, s), (output_w, t))[n // 4]
        which = core if n % 4 < 2 else 1 - core
        part = bit if n % 2 == 0 else 1 - bit
        at = pl.ds(pl.multiple_of(part * rows, rows), rows)
        cols = pl.ds(pl.multiple_of(which * half, half), half)
        copy = pltpu.make_async_copy(block, weight.ref.at[:, at, cols], sems.at[n])
        copy.start()
        copies.append(copy)
    width = 2 * half
    for copy in copies[:4]:
        copy.wait()
    query_w.send()
    pre = dot(normed[...], query_w[...].reshape(width, width))
    for head in range(HEADS):
        low, high = head * HEAD_DIM, (head + 1) * HEAD_DIM
        query_o[:, low:high] = turn(pre[:, low:high], cos[...], sin[...]).astype(BF)
    query_o.send()
    kv_width = kv.shape[1] // 2
    for pair in range(HEADS // 2):
        group = 2 * pair // (HEADS // KV_HEADS)
        keys = kv[:, pl.ds(group * HEAD_DIM, HEAD_DIM)]
        values = kv[:, pl.ds(kv_width + group * HEAD_DIM, HEAD_DIM)]
        scores = dot_t(keys, stacked(query_o, pair)) * HEAD_DIM ** (-0.5) + bias[...]
        weights = jnp.exp(scores - jnp.max(scores, axis=0, keepdims=True))
        probs = (weights * (1.0 / jnp.sum(weights, axis=0, keepdims=True))).astype(BF)
        probs_o[pair] = probs
        unstack(mixed_o, pair, t_dot(probs, values).astype(BF))
    send(probs_o, mixed_o)
    for copy in copies[4:]:
        copy.wait()
    output_w.send()
    resid = src[...].astype(F32) + dot(mixed_o[...], output_w[...].reshape(width, width))
    resid_o[...] = resid
    resid_o.send()
    scale = lax.rsqrt(jnp.mean(resid * resid, axis=-1, keepdims=True) + EPSILON)
    scale_o[...] = jnp.broadcast_to(scale, scale_o.shape)
    second = (resid * scale * gain[...]).astype(BF)
    send_o[...] = t_dot(hot_t[...], second).astype(BF)


def expert_kernel(place, rows, grad_hidden, gate_w, up_w, hidden_o, own_o, sent_o, back_o):
    core = place[0]
    count = rows.shape[0]
    step = count // 2
    for n, low in enumerate(range(0, count, step)):
        at = pl.ds(low, step)
        block = rows[at, :]
        gate = dot(block, gate_w[...])
        up = dot(block, up_w[...])
        sigmoid = 1.0 / (1.0 + jnp.exp(-gate))
        silu = gate * sigmoid
        hidden_o[at, :] = (silu * up).astype(BF)
        grad = grad_hidden[at, :]
        grad_gate = (grad * up * (sigmoid * (1.0 + gate * (1.0 - sigmoid)))).astype(BF)
        grad_up = (grad * silu).astype(BF)
        own_o[at, :] = jnp.where(core == 0, grad_gate, grad_up)
        sent_o[at, :] = jnp.where(core == 0, grad_up, grad_gate)
        for result in (sent_o, hidden_o, own_o):
            result.send(n + 1)
        back_o[at, :] = (dot_t(grad_gate, gate_w[...]) + dot_t(grad_up, up_w[...])).astype(BF)
        back_o.send(n + 1)


def expert_weight_kernel(
    place, rows, rows_got, pre, pre_got, hidden, hidden_got, arrived, upper_got,
    keep_a, send_a, keep_b, send_b, total,
):
    s, t = place[2], place[3]
    width, half = rows.shape[1], hidden.shape[1]
    upper = arrived[:, pl.ds(pl.multiple_of(place[0] * half, half), half)]
    step = 256
    for low in range(0, width, step):
        at = pl.ds(low, step)
        total[at, :] = (t_dot(rows[:, at], pre[...]) + t_dot(rows_got[:, at], pre_got[...])).astype(
            BF
        )
    for low in range(0, half, step):
        at = pl.ds(low, step)
        total[pl.ds(width + low, step), :] = (
            t_dot(hidden[:, at], upper) + t_dot(hidden_got[:, at], upper_got[...])
        ).astype(BF)
    big, small = width // 8, half // 8
    for out, side, spots in (
        (send_a, 0, ((1 - s, 0), (1 - s, 1))),
        (send_b, 1, ((0, 1 - t), (1, 1 - t))),
        (keep_a, 0, ((s, 0), (s, 1))),
        (keep_b, 1, ((0, t), (1, t))),
    ):
        for j, (row_s, row_t) in enumerate(spots):
            piece = side * 4 + 2 * row_s + row_t
            out[j, pl.ds(0, big), :] = total[pl.ds(pl.multiple_of(piece * big, big), big), :]
            start = pl.multiple_of(width + piece * small, small)
            out[j, pl.ds(big, small), :] = total[pl.ds(start, small), :]
        out.send()


def expert_step_kernel(place, keep_a, got_a, keep_b, got_b, keep_ao, send_ao, keep_bo, send_bo):
    s, t = place[2], place[3]
    send_ao[...] = add(keep_a[1 - t], got_a[1 - t])
    send_ao.send()
    send_bo[...] = add(keep_b[1 - s], got_b[1 - s])
    send_bo.send()
    keep_ao[...] = add(keep_a[t], got_a[t])
    keep_ao.send()
    keep_bo[...] = add(keep_b[s], got_b[s])


def expert_end_kernel(place, keep_a, got_a, keep_b, got_b, out):
    out[0] = add(keep_a[...], got_a[...])
    out[1] = add(keep_b[...], got_b[...])


def pair_kernel(place, a, b, one, two):
    one[...] = add(a[0], b[0])
    one.send()
    two[...] = add(a[1], b[1])


def place_experts(place, blocks, outs, stage, sems):
    core = place[0]
    gate_o, up_o, down_o = outs
    half = stage.shape[2]
    big = gate_o.shape[0] // 8
    small = stage.shape[1] - big
    moves = []
    for n, (side, row_s, row_t, which, block) in enumerate(blocks):
        stage[n] = block[...].astype(F32)
        piece = side * 4 + 2 * row_s + row_t
        at = pl.ds(pl.multiple_of(piece * big, big), big)
        cols = pl.ds(pl.multiple_of(which * half, half), half)
        to_gate = pltpu.make_async_copy(stage.at[n, pl.ds(0, big)], gate_o.at[at], sems.at[2 * n])
        to_up = pltpu.make_async_copy(stage.at[n, pl.ds(0, big)], up_o.at[at], sems.at[2 * n])
        to_down = pltpu.make_async_copy(
            stage.at[n, pl.ds(big, small)],
            down_o.at[pl.ds(pl.multiple_of(piece * small, small), small), cols],
            sems.at[2 * n + 1],
        )

        @pl.when(which == 0)
        def _():
            to_gate.start()

        @pl.when(which == 1)
        def _():
            to_up.start()

        to_down.start()
        moves.append((which, to_gate, to_up, to_down))
    for which, to_gate, to_up, to_down in moves:

        @pl.when(which == 0)
        def _():
            to_gate.wait()

        @pl.when(which == 1)
        def _():
            to_up.wait()

        to_down.wait()


def expert_most_kernel(place, *refs):
    core, s, t = place[0], place[2], place[3]
    gate_o, up_o, down_o, mark_o, stage, sems = refs[12:]
    mark_o[...] = jnp.zeros(mark_o.shape, F32)
    blocks = []
    for first, which in ((0, core), (6, 1 - core)):
        zero_a, zero_b, one_a, one_b, two_a, two_b = refs[first : first + 6]
        blocks += [
            (0, s, t, which, zero_a),
            (1, s, t, which, zero_b),
            (0, s, 1 - t, which, one_a),
            (1, 1 - s, t, which, one_b),
            (0, 1 - s, t, which, two_a),
            (1, s, 1 - t, which, two_b),
        ]
    place_experts(place, blocks, (gate_o, up_o, down_o), stage, sems)


def expert_rest_kernel(place, *refs):
    core, s, t = place[0], place[2], place[3]
    gate_o, up_o, down_o, mark_o, stage, sems = refs[9:]
    mark_o[...] = jnp.zeros(mark_o.shape, F32)
    blocks = []
    for first, which in ((0, core), (2, 1 - core)):
        for side in range(2):
            blocks.append((side, 1 - s, 1 - t, which, refs[first + side]))
    place_experts(place, blocks, (gate_o, up_o, down_o), stage, sems)


def expert_outputs(kernel, args, before, part, width, half):
    near = pl.BlockSpec(memory_space=pltpu.VMEM)
    away = pl.BlockSpec(memory_space=pl.ANY)
    shapes = [
        jax.ShapeDtypeStruct(shape, F32)
        for shape in ((width, half), (width, half), (half, width), (8, HEAD_DIM))
    ]
    blocks = 12 if not before else 4
    return pl.pallas_call(
        kernel,
        out_shape=shapes,
        in_specs=[pl.BlockSpec(memory_space=pltpu.SMEM)]
        + [near] * (len(args) - 1)
        + [away] * len(before),
        out_specs=[away] * 3 + [near],
        scratch_shapes=[
            pltpu.VMEM((blocks,) + part, F32),
            pltpu.SemaphoreType.DMA((2 * blocks,)),
        ],
        input_output_aliases={len(args) + n: n for n in range(len(before))},
        compiler_params=pltpu.CompilerParams(vmem_limit_bytes=56 * 1024 * 1024),
        cost_estimate=pl.CostEstimate(flops=0, bytes_accessed=0, transcendentals=0),
    )(*args, *before)


def back_kernel(
    place, back, hot_t, resid_i, scale_i, gain, cot, weight, probs_i, kv, q, cos, sin,
    grad_resid_o, attended_o, gain_o, query_o, kv_o, sent_o,
):
    kv_width = kv.shape[1] // 2
    resid = resid_i[...]
    scale = scale_i[:, :1]
    grad_second = dot(hot_t[...], back[...])
    weighted = grad_second * gain[...]
    inner = jnp.sum(weighted * resid, axis=-1, keepdims=True)
    grad_resid = (
        cot[...].astype(F32)
        + scale * weighted
        - resid * (scale * scale * scale * inner * (1.0 / resid.shape[-1]))
    )
    gain_o[...] = jnp.sum(grad_second * resid * scale, axis=0, keepdims=True)
    grad_resid_o[...] = grad_resid
    grad_resid_o.send()
    attended = grad_resid.astype(BF)
    attended_o[...] = attended
    grad_mixed = dot_t(attended, weight[...]).astype(BF)
    pairs = HEADS // KV_HEADS // 2
    rows = resid.shape[0]
    for group in range(KV_HEADS):
        keys = kv[:, pl.ds(group * HEAD_DIM, HEAD_DIM)]
        values = kv[:, pl.ds(kv_width + group * HEAD_DIM, HEAD_DIM)]
        grad_keys = jnp.zeros(keys.shape, F32)
        grad_values = jnp.zeros(keys.shape, F32)
        for pair in range(group * pairs, (group + 1) * pairs):
            low, high = 2 * pair * HEAD_DIM, (2 * pair + 1) * HEAD_DIM
            upper = jnp.concatenate(
                [grad_mixed[:, low:high], grad_mixed[:, high : high + HEAD_DIM]], axis=0
            )
            probs = probs_i[pair]
            wide = probs.astype(F32)
            grad_probs = dot_t(values, upper)
            total = jnp.sum(wide * grad_probs, axis=0, keepdims=True)
            grad_scores = (wide * (grad_probs - total)).astype(BF)
            grad_values = grad_values + dot(probs, upper)
            grad_keys = grad_keys + dot(grad_scores, stacked(q, pair))
            grad_query = t_dot(grad_scores, keys) * HEAD_DIM ** (-0.5)
            for at, part in ((low, grad_query[:rows]), (high, grad_query[rows:])):
                turned = turn_back(part, cos[...], sin[...])
                query_o[:, pl.ds(at, HEAD_DIM)] = turned.astype(BF)
        at = pl.ds(group * HEAD_DIM, HEAD_DIM)
        kv_o[:, at] = (grad_keys * HEAD_DIM ** (-0.5)).astype(BF)
        kv_o[:, pl.ds(kv_width + group * HEAD_DIM, HEAD_DIM)] = grad_values.astype(BF)
    kv_o.send()
    half = resid.shape[1] // 2
    at = pl.ds(pl.multiple_of((1 - place[0]) * half, half), half)
    sent_o[0] = attended_o[:, at]
    sent_o[1] = query_o[:, at]


def put_split(s, t, total, keep_a, send_a, keep_b, send_b, which=(0, 1)):
    groups, _, quarter, _ = keep_a.shape
    outs = (
        (send_a, 0, ((1 - s, 0), (1 - s, 1))),
        (send_b, 1, ((0, 1 - t), (1, 1 - t))),
        (keep_a, 0, ((s, 0), (s, 1))),
        (keep_b, 1, ((0, t), (1, t))),
    )
    for out, k, spots in outs:
        if k not in which:
            continue
        for f in range(groups):
            for j, (row_s, row_t) in enumerate(spots):
                start = (f * XS + 2 * row_s + row_t) * quarter
                out[f, j] = total[k, pl.ds(pl.multiple_of(start, quarter), quarter), :]
        out.send()


def square_weight_kernel(
    place, mixed, mixed_got, attended, normed, normed_got, query, got,
    keep_a, send_a, keep_b, send_b, total,
):
    half = mixed.shape[1] // 2
    at = pl.ds(pl.multiple_of(place[0] * half, half), half)
    step = 256
    for k, (left, left_got, right) in enumerate(
        ((mixed, mixed_got, attended), (normed, normed_got, query))
    ):
        part = right[:, at]
        for low in range(0, 2 * half, step):
            cols = pl.ds(low, step)
            total[k, cols, :] = (
                t_dot(left[:, cols], part) + t_dot(left_got[:, cols], got[k])
            ).astype(BF)
        put_split(place[2], place[3], total, keep_a, send_a, keep_b, send_b, (k,))


def step_kernel(
    place, qk_a, qg_a, kk_a, kg_a, qk_b, qg_b, kk_b, kg_b, keep_a, send_a, keep_b, send_b
):
    s, t = place[2], place[3]
    size = qk_a.shape[-1]
    extra = kk_a.shape[-1]
    groups = qk_a.shape[0]
    for out, which, big, big_got, small, small_got in (
        (send_a, 1 - t, qk_a, qg_a, kk_a, kg_a),
        (send_b, 1 - s, qk_b, qg_b, kk_b, kg_b),
        (keep_a, t, qk_a, qg_a, kk_a, kg_a),
        (keep_b, s, qk_b, qg_b, kk_b, kg_b),
    ):
        for f in range(groups):
            out[f, :, pl.ds(0, size)] = add(big[f, which], big_got[f, which])
            out[f, :, pl.ds(size, extra)] = add(small[f, which], small_got[f, which])
        out.send()


def pack_kernel(place, keep_a, got_a, keep_b, got_b, gains, out):
    size = keep_a.shape[-1]
    for y, (keep, got) in enumerate(((keep_a, got_a), (keep_b, got_b))):
        out[y, :, :, pl.ds(0, size)] = add(keep[...], got[...])
        out[y, :, :, pl.ds(size, gains.shape[-1])] = gains[...]
        out.send(y + 1)


def sum_kernel(place, parts, out):
    total = parts[0].astype(F32)
    for k in range(1, parts.shape[0]):
        total = total + parts[k].astype(F32)
    total = total.astype(BF)
    for k in range(out.shape[0]):
        out[k] = total


def final_kernel(place, own, other, mark, output_o, query_o, key_o, value_o, gains_o):
    core = place[0]
    quarter = own.shape[1]
    half = output_o.shape[1] // 2
    part = key_o.shape[1] // 2
    size = half + part
    for refs, which in ((own, core), (other, 1 - core)):
        at = pl.ds(pl.multiple_of(which * half, half), half)
        for piece, x in enumerate(PLACE):
            rows = pl.ds(piece * quarter, quarter)
            output_o[rows, at] = refs[x, :, pl.ds(0, half)].astype(F32)
            query_o[rows, at] = refs[XS + x, :, pl.ds(0, half)].astype(F32)
    send(output_o, query_o)
    for piece, x in enumerate(PLACE):
        rows = pl.ds(piece * quarter, quarter)
        for y in range(2):
            at = pl.ds(y * part, part)
            mine = own[y * XS + x, :, pl.ds(half, part)].astype(F32)
            others = other[y * XS + x, :, pl.ds(half, part)].astype(F32)
            even = core == 0
            key_o[rows, at] = jnp.where(even, mine, others)
            value_o[rows, at] = jnp.where(even, others, mine)
    total = jnp.zeros(gains_o.shape, F32)
    for refs in (own, other):
        for x in range(XS):
            total = total + refs[x, :, pl.ds(size, gains_o.shape[1])].astype(F32)
    gains_o[...] = total


def key_back_kernel(place, parts, cos, sin, pre_o, sent_o):
    kv_width = parts.shape[-1] // 2
    total = parts[0].astype(F32)
    for k in range(1, parts.shape[0]):
        total = total + parts[k].astype(F32)
    for head in range(2 * KV_HEADS):
        low, high = head * HEAD_DIM, (head + 1) * HEAD_DIM
        piece = total[:, low:high]
        if head < KV_HEADS:
            piece = turn_back(piece, cos[...], sin[...])
        pre_o[:, low:high] = piece.astype(BF)
    sent_o[...] = pre_o[:, pl.ds(pl.multiple_of((1 - place[0]) * kv_width, kv_width), kv_width)]


def key_weight_kernel(
    place, normed, normed_got, pre, pre_got, keep_a, send_a, keep_b, send_b, total
):
    kv_width = pre_got.shape[1]
    part = pre[:, pl.ds(pl.multiple_of(place[0] * kv_width, kv_width), kv_width)]
    grad = (t_dot(normed[...], part) + t_dot(normed_got[...], pre_got[...])).astype(BF)
    total[0] = grad[:, : kv_width // 2]
    total[1] = grad[:, kv_width // 2 :]
    put_split(place[2], place[3], total, keep_a, send_a, keep_b, send_b)


def input_kernel(
    place, query, pre, src, scale_i, gain, query_w, kv_w, grad_resid, input_o, gain_o
):
    grad_normed = dot_t(query[...], query_w[...]) + dot_t(pre[...], kv_w[...])
    source = src[...].astype(F32)
    scale = scale_i[:, :1]
    weighted = grad_normed * gain[...]
    inner = jnp.sum(weighted * source, axis=-1, keepdims=True)
    input_o[...] = (
        grad_resid[...]
        + scale * weighted
        - source * (scale * scale * scale * inner * (1.0 / source.shape[-1]))
    ).astype(BF)
    gain_o[...] = jnp.sum(grad_normed * source * scale, axis=0, keepdims=True)


class Far:
    def __init__(self, value, kind=None, parts=1):
        self.value, self.kind, self.parts = value, kind, parts


class Coming:
    def __init__(self, source, ref, sem):
        self.copy, self.ref, self.waits = pltpu.make_async_copy(source, ref, sem), ref, True
        self.shape = ref.shape
        self.copy.start()

    def now(self):
        if self.waits:
            self.copy.wait()
            self.waits = False
        return self.ref

    def __getitem__(self, index):
        return self.now()[index]

    @property
    def at(self):
        return self.now().at


class Going:
    def __init__(self, ref, target, sems, parts):
        self.ref, self.target, self.shape, self.sent = ref, target, ref.shape, 0
        rows = ref.shape[0] // parts
        self.copies = [
            pltpu.make_async_copy(
                ref.at[pl.ds(n * rows, rows)], target.at[pl.ds(n * rows, rows)], sem
            )
            for n, sem in enumerate(sems)
        ]

    def __getitem__(self, index):
        return self.ref[index]

    def __setitem__(self, index, value):
        self.ref[index] = value

    def send(self, upto=None):
        upto = len(self.copies) if upto is None else upto
        for copy in self.copies[self.sent : upto]:
            copy.start()
        self.sent = max(self.sent, upto)


def send(self):
        if not self.sent:
            self.copy.start()
            self.sent = True


def send(*results):
    for result in results:
        result.send()


def call(kernel, args, outs, scratch=(), micros=0, raw=()):
    outs = [out if isinstance(out, Far) else Far(*out) for out in outs]
    values = [a.value if isinstance(a, Far) else a for a in args]
    far = [i for i, a in enumerate(args) if isinstance(a, Far) and i not in raw]
    count, made = len(args), len(outs)

    def whole(*refs):
        ins, results = list(refs[:count]), refs[count : count + made]
        own = refs[count + made : count + made + len(scratch)]
        rest = refs[count + made + len(scratch) :]
        landing, leaving, sems = rest[: len(far)], rest[len(far) : len(far) + made], rest[-1]
        for n, i in enumerate(far):
            ins[i] = Coming(ins[i], landing[n], sems.at[n])
        going, used = [], len(far)
        for out, ref, target in zip(outs, leaving, results):
            going.append(
                Going(ref, target, [sems.at[used + n] for n in range(out.parts)], out.parts)
            )
            used += out.parts
        kernel(*ins, *going, *own)
        for i in far:
            ins[i].now()
        send(*going)
        for result in going:
            for copy in result.copies:
                copy.wait()

    near = pl.BlockSpec(memory_space=pltpu.VMEM)
    away = pl.BlockSpec(memory_space=pl.ANY)
    specs = [away if isinstance(a, Far) else near for a in args]
    specs[0] = pl.BlockSpec(memory_space=pltpu.SMEM)
    return pl.pallas_call(
        whole,
        out_shape=[jax.ShapeDtypeStruct(out.value, out.kind) for out in outs],
        in_specs=specs,
        out_specs=[away] * made,
        scratch_shapes=[
            *scratch,
            *[pltpu.VMEM(values[i].shape, values[i].dtype) for i in far],
            *[pltpu.VMEM(out.value, out.kind) for out in outs],
            pltpu.SemaphoreType.DMA((len(far) + sum(out.parts for out in outs),)),
        ],
        compiler_params=pltpu.CompilerParams(vmem_limit_bytes=56 * 1024 * 1024),
        cost_estimate=pl.CostEstimate(
            flops=int(micros * 1e9), bytes_accessed=0, transcendentals=0
        ),
    )(*values)


def swap(v):
    return lax.ppermute(v, "core", [(0, 1), (1, 0)])


def swap_y(v):
    return lax.ppermute(v, "ylo", [(0, 1), (1, 0)])


def exchange(v, axis):
    return lax.all_to_all(v, axis, 0, 0, tiled=True)


def copies(v, n):
    return lax.optimization_barrier(jnp.broadcast_to(v[None], (n,) + v.shape))


def tie(*values):
    return lax.optimization_barrier(values)


PAIRS_S = [(0, 1), (1, 0), (2, 3), (3, 2)]
PAIRS_T = [(0, 3), (3, 0), (1, 2), (2, 1)]
PLACE = (0, 3, 1, 2)


def x_bits():
    x = lax.axis_index("x")
    return ((x + 1) // 2) % 2, x // 2


def flip(v, pairs):
    return lax.ppermute(v, "x", pairs)


def body(
    inputs,
    segments,
    first_gain,
    query_matrix,
    key_matrix,
    value_matrix,
    output_matrix,
    second_gain,
    expert_ids,
    gate_values,
    priority,
    gate_weight,
    up_weight,
    down_weight,
    cotangent,
):
    tok = inputs.shape[1]
    width = inputs.shape[2]
    rows = query_matrix.shape[0]
    groups = lax.axis_size("fsdp")
    member = lax.axis_index("fsdp")
    core = lax.axis_index("core")
    even = core == 0
    experts = groups
    capacity = 5 * tok * TOP // (4 * experts)
    slots_all = experts * capacity
    half = width // 2
    kv_width = key_matrix.shape[1]
    length = groups * tok
    quarter = rows // XS
    bit_s, bit_t = x_bits()
    place_at = jnp.stack([core, member * tok, bit_s, bit_t]).astype(jnp.int32)

    def pick(a, b):
        return jnp.where(even, a, b)

    parts = width // kv_width
    kv_rows = rows // parts
    kv_half = pick(key_matrix, value_matrix).reshape(parts, kv_rows, kv_width)
    kv_piece = jnp.concatenate([kv_half[j] for j in range(parts)], axis=1)
    gains = jnp.pad(jnp.stack([first_gain, second_gain]), ((0, 6), (0, width - rows)))
    square_piece = jnp.concatenate(
        [
            lax.dynamic_slice(matrix, (bit * (rows // 2), core * half), (rows // 2, half))
            for matrix, bit in ((query_matrix, bit_s), (output_matrix, bit_t))
        ],
        axis=1,
    )
    weights = jnp.concatenate([kv_piece, gains, square_piece], axis=0)
    gathered = exchange(copies(weights, groups), "fsdp")

    ids = expert_ids[0].reshape(-1)
    order = priority[0, 0]
    earlier = (order[None, :] < order[:, None]) & (ids[None, :] == ids[:, None])
    slots = jnp.sum(earlier.astype(jnp.int32), axis=1)
    kept = slots < capacity
    expert_list = jnp.arange(experts, dtype=jnp.int32)
    chosen = (ids[:, None] == expert_list[None, :]) & kept[:, None]
    slot_of = jnp.sum(
        jnp.where(chosen, slots[:, None] + 1, 0).reshape(tok, TOP, experts), axis=1
    )
    slot_of = slot_of - 1
    gate_table = jnp.sum(
        jnp.where(chosen, gate_values[0].reshape(-1)[:, None], 0.0).reshape(tok, TOP, experts),
        axis=1,
    )
    slot_list = jnp.arange(capacity, dtype=jnp.int32)
    hits = slot_of.T[:, None, :] == slot_list[None, :, None]
    one_hot = hits.astype(BF).reshape(slots_all, tok)
    one_hot_t = (slot_of[:, :, None] == slot_list[None, None, :]).astype(BF)
    one_hot_t = one_hot_t.reshape(tok, slots_all)
    gate_hot = jnp.where(hits, gate_table.T[:, None, :], 0.0).reshape(slots_all, tok)
    slot_gate = jnp.sum(gate_hot, axis=1, keepdims=True)
    gate_high = gate_hot.astype(BF)
    gate_low = (gate_hot - gate_high.astype(F32)).astype(BF)
    send_grad = (dot(one_hot, cotangent[0]) * slot_gate).astype(BF)

    cosine, sine = angles(member * tok + jnp.arange(tok, dtype=jnp.int32))
    segment_row = segments[0]
    query_segments = lax.dynamic_slice_in_dim(segment_row, member * tok, tok)
    key_place = jnp.arange(length, dtype=jnp.int32)[:, None]
    query_place = (member * tok + jnp.arange(tok, dtype=jnp.int32))[None, :]
    allowed = (
        (key_place <= query_place)
        & (query_place - key_place < WINDOW)
        & (segment_row[:, None] == query_segments[None, :])
    )
    bias = jnp.where(allowed, 0.0, NEGATIVE).astype(F32)
    bias = jnp.concatenate([bias, bias], axis=1)
    gathered, cosine, sine, place_at, one_hot_t, gate_high, gate_low, send_grad, bias = tie(
        gathered, cosine, sine, place_at, one_hot_t, gate_high, gate_low, send_grad, bias
    )
    kv_raw = gathered[:, :kv_rows]
    gain_one = gathered[:, kv_rows, :rows].reshape(1, width).astype(F32)
    gain_two = gathered[:, kv_rows + 1, :rows].reshape(1, width).astype(F32)
    kv_raw_other = swap(kv_raw)

    square = (width, width)
    normed, scale_one, kv_send, kv_weight = call(
        key_kernel,
        [place_at, Far(inputs[0]), gain_one, Far(kv_raw), Far(kv_raw_other), cosine, sine],
        [((tok, width), BF), ((tok, HEAD_DIM), F32), ((groups, tok, 2 * kv_width), BF),
         ((width, 2 * kv_width), BF)],
    )
    q_own, o_own = gathered[:, kv_rows + 8 :, :half], gathered[:, kv_rows + 8 :, half:]
    kv_all = exchange(kv_send, "fsdp").reshape(length, 2 * kv_width)
    q_got, o_got = flip(q_own, PAIRS_S), flip(o_own, PAIRS_T)
    send_grad, kv_all = tie(send_grad, kv_all)
    arrived_grad = exchange(send_grad, "fsdp")
    normed_other = swap(normed)
    far_pieces = [
        Far(v)
        for v in (q_own, q_got, swap(q_own), swap(q_got), o_own, o_got, swap(o_own), swap(o_got))
    ]
    weight_parts = (groups, rows, width)
    (query_weight, output_weight, query_rot, mixed, probs, residual, scale_two,
     send_rows) = call(
        front_kernel,
        [place_at, Far(normed), Far(kv_all), Far(bias), Far(inputs[0]), gain_two, Far(one_hot_t),
         cosine, sine, *far_pieces],
        [(weight_parts, BF), (weight_parts, BF), ((tok, width), BF), ((tok, width), BF),
         ((HEADS // 2, length, 2 * tok), BF), ((tok, width), F32), ((tok, HEAD_DIM), F32),
         ((slots_all, width), BF)],
        [pltpu.SemaphoreType.DMA((8,))],
        raw=range(9, 17),
    )
    query_weight = query_weight.reshape(square)
    output_weight = output_weight.reshape(square)

    send_rows, arrived_grad = tie(send_rows, arrived_grad)
    arrived = exchange(send_rows, "fsdp")
    mixed_other = swap(mixed)
    upper_other = swap(lax.dynamic_slice_in_dim(arrived_grad, (1 - core) * half, half, 1))
    grad_hidden = dot_t(arrived_grad, down_weight[0])
    arrived, grad_hidden, mixed_other, upper_other = tie(
        arrived, grad_hidden, mixed_other, upper_other
    )
    arrived_other = swap(arrived)
    hidden, own_pre, sent_pre, grad_rows = call(
        expert_kernel,
        [place_at, Far(arrived), Far(grad_hidden), gate_weight[0], up_weight[0]],
        [Far((slots_all, half), BF, 2)] * 3 + [Far((slots_all, width), BF, 2)],
    )
    back_rows = exchange(grad_rows, "fsdp")
    expert_rows = width + half

    e_part = (2, expert_rows // 8, half)
    e_keep_a, e_send_a, e_keep_b, e_send_b = call(
        expert_weight_kernel,
        [place_at] + [Far(v) for v in (arrived, arrived_other, own_pre, swap(sent_pre), hidden,
                                       swap(hidden), arrived_grad, upper_other)],
        [(e_part, BF)] * 4,
        [pltpu.VMEM((expert_rows, half), BF)],
    )
    expert_out = dot(hidden, down_weight[0]).astype(BF)
    e_got_a, e_got_b = flip(e_send_a, PAIRS_S), flip(e_send_b, PAIRS_T)
    back_rows, expert_out, e_keep_a, e_keep_b = tie(back_rows, expert_out, e_keep_a, e_keep_b)

    grad_residual, grad_attended, gain_two_part, grad_query_pre, kv_back, qo_sent = call(
        back_kernel,
        [place_at, Far(back_rows), Far(one_hot_t), Far(residual), Far(scale_two), gain_two,
         Far(cotangent[0]), Far(output_weight), Far(probs), Far(kv_all), Far(query_rot), cosine,
         sine],
        [((tok, width), F32), ((tok, width), BF), ((1, width), F32), ((tok, width), BF),
         ((length, 2 * kv_width), BF), ((2, tok, half), BF)],
    )
    kv_got = exchange(kv_back, "fsdp")
    e_keep_a, e_send_a, e_keep_b, e_send_b = call(
        expert_step_kernel,
        [place_at, Far(e_keep_a), Far(e_got_a), Far(e_keep_b), Far(e_got_b)],
        [(e_part[1:], BF)] * 4,
    )
    qo_got, e_send_a, e_send_b = tie(swap(qo_sent), e_send_a, e_send_b)
    e_got_a, e_got_b = flip(e_send_a, PAIRS_T), flip(e_send_b, PAIRS_S)

    big_part, small_part = (groups, 2, quarter, half), (groups, 2, quarter, kv_width // 2)
    qo_keep_a, qo_send_a, qo_keep_b, qo_send_b = call(
        square_weight_kernel,
        [place_at] + [Far(v) for v in (mixed, mixed_other, grad_attended, normed, normed_other,
                                       grad_query_pre, qo_got)],
        [(big_part, BF)] * 4,
        [pltpu.VMEM((2, width, half), BF)],
    )
    kv_got, expert_out = tie(kv_got, expert_out)
    qo_got_a, qo_got_b = flip(qo_send_a, PAIRS_S), flip(qo_send_b, PAIRS_T)
    returned = exchange(expert_out, "fsdp")
    grad_kv_pre, kv_pre_sent = call(
        key_back_kernel,
        [place_at, Far(kv_got.reshape(groups, tok, 2 * kv_width)), cosine, sine],
        [((tok, 2 * kv_width), BF), ((tok, kv_width), BF)],
        micros=30,
    )
    kv_keep_a, kv_send_a, kv_keep_b, kv_send_b = call(
        key_weight_kernel,
        [place_at, Far(normed), Far(normed_other), Far(grad_kv_pre), Far(swap(kv_pre_sent))],
        [(small_part, BF)] * 4,
        [pltpu.VMEM((2, width, kv_width // 2), BF)],
    )
    kv_got_a, kv_got_b = flip(kv_send_a, PAIRS_S), flip(kv_send_b, PAIRS_T)
    e_sum = call(
        expert_end_kernel,
        [place_at, Far(e_keep_a), Far(e_got_a), Far(e_keep_b), Far(e_got_b)],
        [(e_part, BF)],
    )[0]
    e_other_y = swap_y(e_sum)
    input_grad, gain_one_part = call(
        input_kernel,
        [place_at, Far(grad_query_pre), Far(grad_kv_pre), Far(inputs[0]), Far(scale_one), gain_one,
         Far(query_weight), Far(kv_weight), Far(grad_residual)],
        [((tok, width), BF), ((1, width), F32)],
    )

    e_other_y, gain_one_part = tie(e_other_y, gain_one_part)
    e_zero_a, e_zero_b = call(pair_kernel, [place_at, Far(e_sum), Far(e_other_y)], [(e_part[1:], BF)] * 2)
    e_one_a, e_one_b = flip(e_zero_a, PAIRS_T), flip(e_zero_b, PAIRS_S)
    e_two_a, e_two_b = flip(e_zero_a, PAIRS_S), flip(e_zero_b, PAIRS_T)

    both_part = (groups, quarter, half + kv_width // 2)
    keep_a, send_a, keep_b, send_b = call(
        step_kernel,
        [place_at] + [Far(v) for v in (qo_keep_a, qo_got_a, kv_keep_a, kv_got_a, qo_keep_b,
                                       qo_got_b, kv_keep_b, kv_got_b)],
        [(both_part, BF)] * 4,
    )
    got_a, got_b = flip(send_a, PAIRS_T), flip(send_b, PAIRS_S)
    spare = HEAD_DIM
    gain_parts = jnp.stack([gain_one_part, gain_two_part]).reshape(2, groups, quarter, XS)
    gain_parts = gain_parts.transpose(1, 2, 0, 3).reshape(groups, quarter, 2 * XS).astype(BF)
    gain_parts = jnp.pad(gain_parts, ((0, 0), (0, 0), (0, spare - 2 * XS)))
    packed_width = both_part[-1] + spare
    packed = call(
        pack_kernel,
        [place_at, Far(keep_a), Far(got_a), Far(keep_b), Far(got_b), gain_parts],
        [Far((YLO, groups, quarter, packed_width), BF, 2)],
    )[0]
    packed, returned = tie(packed, returned)
    packed = exchange(packed.reshape(YLO * groups, quarter, packed_width), ("ylo", "fsdp"))
    mixture = t_dot(gate_high, returned) + t_dot(gate_low, returned)
    outputs = (residual + mixture).astype(BF)
    packed, outputs = tie(packed, outputs)
    packed = call(sum_kernel, [place_at, Far(packed)], [((YLO * XS, quarter, packed_width), BF)])[0]
    spreaded = exchange(packed, ("ylo", "x"))
    most = [e_zero_a, e_zero_b, e_one_a, e_one_b, e_two_a, e_two_b]
    *e_grads, most_mark = expert_outputs(
        expert_most_kernel, [place_at, *most, *[swap(v) for v in most]], [], e_part[1:], width, half
    )
    e_one_a, e_one_b, packed = tie(e_one_a, e_one_b, packed)
    e_three_a, e_three_b = flip(e_one_a, PAIRS_S), flip(e_one_b, PAIRS_T)
    e_three_a, e_three_b, most_mark = tie(e_three_a, e_three_b, most_mark)
    grad_gate, grad_up, grad_down, e_mark = expert_outputs(
        expert_rest_kernel,
        [place_at, e_three_a, e_three_b, swap(e_three_a), swap(e_three_b), most_mark,
         packed[0, :16, :HEAD_DIM]],
        e_grads,
        e_part[1:],
        width,
        half,
    )
    spreaded, e_mark = tie(spreaded, e_mark)
    grad_output_w, grad_query_w, grad_key_w, grad_value_w, gains_sum = call(
        final_kernel,
        [place_at, Far(spreaded), Far(swap(spreaded)), e_mark],
        [((rows, width), F32), ((rows, width), F32), ((rows, kv_width), F32),
         ((rows, kv_width), F32), ((quarter, spare), F32)],
    )
    gains_sum = gains_sum[:, : 2 * XS].reshape(quarter, 2, XS).transpose(1, 0, 2)
    gains_sum = gains_sum.reshape(2, rows)
    return (
        outputs[None],
        input_grad[None],
        gains_sum[0],
        grad_query_w,
        grad_key_w,
        grad_value_w,
        grad_output_w,
        gains_sum[1],
        grad_gate[None],
        grad_up[None],
        grad_down[None],
    )


def solution(mesh):
    shape = mesh.devices.shape
    fine = Mesh(
        mesh.devices.reshape(YLO, XS, CORES, shape[1]), ("ylo", "x", "core", "fsdp")
    )
    return jax.shard_map(
        body,
        mesh=fine,
        in_specs=(
            P(REP, "fsdp", None),
            P(REP, None),
            P("fsdp"),
            P("fsdp", None),
            P("fsdp", None),
            P("fsdp", None),
            P("fsdp", None),
            P("fsdp"),
            P(REP, "fsdp", None),
            P(REP, "fsdp", None),
            P(REP, "fsdp", None),
            P("fsdp", None, None),
            P("fsdp", None, None),
            P("fsdp", None, None),
            P(REP, "fsdp", None),
        ),
        out_specs=(
            P(REP, "fsdp", None),
            P(REP, "fsdp", None),
            P("fsdp"),
            P("fsdp", None),
            P("fsdp", None),
            P("fsdp", None),
            P("fsdp", None),
            P("fsdp"),
            P("fsdp", None, None),
            P("fsdp", None, None),
            P("fsdp", None, None),
        ),
        check_vma=False,
    )
```

```python
import jax
import jax.numpy as jnp
from jax import lax
from jax.experimental import pallas as pl
from jax.experimental.pallas import tpu as pltpu
from jax.sharding import Mesh
from jax.sharding import PartitionSpec as P

HEADS = 12
KV_HEADS = 2
HEAD_DIM = 128
TOP = 4
WINDOW = 1024

EPSILON = 1e-06
THETA = 10000.0
NEGATIVE = -1e30

YLO, XS, CORES = 2, 4, 2
REP = ("ylo", "x", "core")
BF = jnp.bfloat16
F32 = jnp.float32


def angles(positions):
    half_width = HEAD_DIM // 2
    frequency = THETA ** (-(jnp.arange(half_width, dtype=F32) * 2.0) / HEAD_DIM)
    phase = positions.astype(F32)[:, None] * frequency[None, :]
    cosine, sine = jnp.cos(phase), jnp.sin(phase)
    return (
        jnp.concatenate([cosine, cosine], axis=1),
        jnp.concatenate([-sine, sine], axis=1),
    )


def dot(a, b):
    return jnp.dot(a, b, preferred_element_type=F32)


def dot_t(a, b):
    return lax.dot_general(a, b, (((1,), (1,)), ((), ())), preferred_element_type=F32)


def t_dot(a, b):
    return lax.dot_general(a, b, (((0,), (0,)), ((), ())), preferred_element_type=F32)


def fan(pieces):
    return [
        pieces[0],
        flip(pieces[1], PAIRS_S),
        flip(pieces[2], PAIRS_T),
        flip(pieces[3], PAIRS_ST),
    ]


def add(a, b):
    return (a.astype(F32) + b.astype(F32)).astype(BF)


def turn(piece, cosine, sine):
    return piece * cosine + pltpu.roll(piece, HEAD_DIM // 2, 1) * sine


def turn_back(piece, cosine, sine):
    return piece * cosine - pltpu.roll(piece, HEAD_DIM // 2, 1) * sine


def stacked(ref, pair):
    low = 2 * pair * HEAD_DIM
    return jnp.concatenate(
        [ref[:, pl.ds(low, HEAD_DIM)], ref[:, pl.ds(low + HEAD_DIM, HEAD_DIM)]], axis=0
    )


def unstack(ref, pair, value):
    low, rows = 2 * pair * HEAD_DIM, value.shape[0] // 2
    ref[:, pl.ds(low, HEAD_DIM)] = value[:rows]
    ref[:, pl.ds(low + HEAD_DIM, HEAD_DIM)] = value[rows:]


def key_kernel(place, src, gain, raw_own, raw_other, cos, sin, normed_o, scale_o, send_o, weight_o):
    core = place[0]
    groups, kv_rows, width = raw_own.shape
    kv_width = weight_o.shape[1] // 2
    parts = width // kv_width
    source = src[...].astype(F32)
    scale = lax.rsqrt(jnp.mean(source * source, axis=-1, keepdims=True) + EPSILON)
    scale_o[...] = jnp.broadcast_to(scale, scale_o.shape)
    normed = (source * scale * gain[...]).astype(BF)
    normed_o[...] = normed
    send(scale_o, normed_o)
    for raw, which in ((raw_own, core), (raw_other, 1 - core)):
        at = pl.ds(pl.multiple_of(which * kv_width, kv_width), kv_width)
        for f in range(groups):
            for j in range(parts):
                weight_o[pl.ds((f * parts + j) * kv_rows, kv_rows), at] = raw[
                    f, :, pl.ds(j * kv_width, kv_width)
                ]
    send(weight_o)
    pre = dot(normed, weight_o[...])
    for head in range(2 * KV_HEADS):
        low, high = head * HEAD_DIM, (head + 1) * HEAD_DIM
        piece = pre[:, low:high]
        if head < KV_HEADS:
            piece = turn(piece, cos[...], sin[...])
        for f in range(groups):
            send_o[f, :, low:high] = piece.astype(BF)


def front_kernel(place, normed, kv, bias, src, gain, hot_t, cos, sin, *refs):
    pieces = refs[:8]
    query_w, output_w, query_o, mixed_o, probs_o, resid_o, scale_o, send_o, sems = refs[8:]
    core, s, t = place[0], place[2], place[3]
    _, rows, half = pieces[0].shape
    copies = []
    for n, block in enumerate(pieces):
        weight, bit = ((query_w, s), (output_w, t))[n // 4]
        which = core if n % 4 < 2 else 1 - core
        part = bit if n % 2 == 0 else 1 - bit
        at = pl.ds(pl.multiple_of(part * rows, rows), rows)
        cols = pl.ds(pl.multiple_of(which * half, half), half)
        copy = pltpu.make_async_copy(block, weight.ref.at[:, at, cols], sems.at[n])
        copy.start()
        copies.append(copy)
    width = 2 * half
    for copy in copies[:4]:
        copy.wait()
    query_w.send()
    pre = dot(normed[...], query_w[...].reshape(width, width))
    for head in range(HEADS):
        low, high = head * HEAD_DIM, (head + 1) * HEAD_DIM
        query_o[:, low:high] = turn(pre[:, low:high], cos[...], sin[...]).astype(BF)
    query_o.send()
    kv_width = kv.shape[1] // 2
    for pair in range(HEADS // 2):
        group = 2 * pair // (HEADS // KV_HEADS)
        keys = kv[:, pl.ds(group * HEAD_DIM, HEAD_DIM)]
        values = kv[:, pl.ds(kv_width + group * HEAD_DIM, HEAD_DIM)]
        scores = dot_t(keys, stacked(query_o, pair)) * HEAD_DIM ** (-0.5) + bias[...]
        weights = jnp.exp(scores - jnp.max(scores, axis=0, keepdims=True))
        probs = (weights * (1.0 / jnp.sum(weights, axis=0, keepdims=True))).astype(BF)
        probs_o[pair] = probs
        unstack(mixed_o, pair, t_dot(probs, values).astype(BF))
    send(probs_o, mixed_o)
    for copy in copies[4:]:
        copy.wait()
    output_w.send()
    resid = src[...].astype(F32) + dot(mixed_o[...], output_w[...].reshape(width, width))
    resid_o[...] = resid
    resid_o.send()
    scale = lax.rsqrt(jnp.mean(resid * resid, axis=-1, keepdims=True) + EPSILON)
    scale_o[...] = jnp.broadcast_to(scale, scale_o.shape)
    second = (resid * scale * gain[...]).astype(BF)
    send_o[...] = t_dot(hot_t[...], second).astype(BF)


def expert_kernel(place, rows, grad_hidden, gate_w, up_w, hidden_o, own_o, sent_o, back_o):
    core = place[0]
    count = rows.shape[0]
    step = count // 2
    for n, low in enumerate(range(0, count, step)):
        at = pl.ds(low, step)
        block = rows[at, :]
        gate = dot(block, gate_w[...])
        up = dot(block, up_w[...])
        sigmoid = 1.0 / (1.0 + jnp.exp(-gate))
        silu = gate * sigmoid
        hidden_o[at, :] = (silu * up).astype(BF)
        grad = grad_hidden[at, :]
        grad_gate = (grad * up * (sigmoid * (1.0 + gate * (1.0 - sigmoid)))).astype(BF)
        grad_up = (grad * silu).astype(BF)
        own_o[at, :] = jnp.where(core == 0, grad_gate, grad_up)
        sent_o[at, :] = jnp.where(core == 0, grad_up, grad_gate)
        for result in (sent_o, hidden_o, own_o):
            result.send(n + 1)
        back_o[at, :] = (dot_t(grad_gate, gate_w[...]) + dot_t(grad_up, up_w[...])).astype(BF)
        back_o.send(n + 1)


def expert_weight_kernel(
    place, rows, rows_got, pre, pre_got, hidden, hidden_got, arrived, upper_got,
    keep_a, send_a, keep_b, send_b, total,
):
    s, t = place[2], place[3]
    width, half = rows.shape[1], hidden.shape[1]
    upper = arrived[:, pl.ds(pl.multiple_of(place[0] * half, half), half)]
    step = 256
    for low in range(0, width, step):
        at = pl.ds(low, step)
        total[at, :] = (t_dot(rows[:, at], pre[...]) + t_dot(rows_got[:, at], pre_got[...])).astype(
            BF
        )
    for low in range(0, half, step):
        at = pl.ds(low, step)
        total[pl.ds(width + low, step), :] = (
            t_dot(hidden[:, at], upper) + t_dot(hidden_got[:, at], upper_got[...])
        ).astype(BF)
    big, small = width // 8, half // 8
    for out, side, spots in (
        (send_a, 0, ((1 - s, 0), (1 - s, 1))),
        (send_b, 1, ((0, 1 - t), (1, 1 - t))),
        (keep_a, 0, ((s, 0), (s, 1))),
        (keep_b, 1, ((0, t), (1, t))),
    ):
        for j, (row_s, row_t) in enumerate(spots):
            piece = side * 4 + 2 * row_s + row_t
            out[j, pl.ds(0, big), :] = total[pl.ds(pl.multiple_of(piece * big, big), big), :]
            start = pl.multiple_of(width + piece * small, small)
            out[j, pl.ds(big, small), :] = total[pl.ds(start, small), :]
        out.send()


def expert_step_kernel(place, keep_a, got_a, keep_b, got_b, keep_ao, send_ao, keep_bo, send_bo):
    s, t = place[2], place[3]
    send_ao[...] = add(keep_a[1 - t], got_a[1 - t])
    send_ao.send()
    send_bo[...] = add(keep_b[1 - s], got_b[1 - s])
    send_bo.send()
    keep_ao[...] = add(keep_a[t], got_a[t])
    keep_ao.send()
    keep_bo[...] = add(keep_b[s], got_b[s])


def expert_end_kernel(place, keep_a, got_a, keep_b, got_b, out):
    out[0] = add(keep_a[...], got_a[...])
    out[1] = add(keep_b[...], got_b[...])


def pair_kernel(place, a, b, one, two):
    one[...] = add(a[0], b[0])
    one.send()
    two[...] = add(a[1], b[1])


def place_experts(place, blocks, outs, stage, sems):
    core = place[0]
    gate_o, up_o, down_o = outs
    half = stage.shape[2]
    big = gate_o.shape[0] // 8
    small = stage.shape[1] - big
    moves = []
    for n, (side, row_s, row_t, which, block) in enumerate(blocks):
        stage[n] = block[...].astype(F32)
        piece = side * 4 + 2 * row_s + row_t
        at = pl.ds(pl.multiple_of(piece * big, big), big)
        cols = pl.ds(pl.multiple_of(which * half, half), half)
        to_gate = pltpu.make_async_copy(stage.at[n, pl.ds(0, big)], gate_o.at[at], sems.at[2 * n])
        to_up = pltpu.make_async_copy(stage.at[n, pl.ds(0, big)], up_o.at[at], sems.at[2 * n])
        to_down = pltpu.make_async_copy(
            stage.at[n, pl.ds(big, small)],
            down_o.at[pl.ds(pl.multiple_of(piece * small, small), small), cols],
            sems.at[2 * n + 1],
        )

        @pl.when(which == 0)
        def _():
            to_gate.start()

        @pl.when(which == 1)
        def _():
            to_up.start()

        to_down.start()
        moves.append((which, to_gate, to_up, to_down))
    for which, to_gate, to_up, to_down in moves:

        @pl.when(which == 0)
        def _():
            to_gate.wait()

        @pl.when(which == 1)
        def _():
            to_up.wait()

        to_down.wait()


def expert_most_kernel(place, *refs):
    core, s, t = place[0], place[2], place[3]
    gate_o, up_o, down_o, mark_o, stage, sems = refs[12:]
    mark_o[...] = jnp.zeros(mark_o.shape, F32)
    blocks = []
    for first, which in ((0, core), (6, 1 - core)):
        zero_a, zero_b, one_a, one_b, two_a, two_b = refs[first : first + 6]
        blocks += [
            (0, s, t, which, zero_a),
            (1, s, t, which, zero_b),
            (0, s, 1 - t, which, one_a),
            (1, 1 - s, t, which, one_b),
            (0, 1 - s, t, which, two_a),
            (1, s, 1 - t, which, two_b),
        ]
    place_experts(place, blocks, (gate_o, up_o, down_o), stage, sems)


def expert_rest_kernel(place, *refs):
    core, s, t = place[0], place[2], place[3]
    gate_o, up_o, down_o, mark_o, stage, sems = refs[9:]
    mark_o[...] = jnp.zeros(mark_o.shape, F32)
    blocks = []
    for first, which in ((0, core), (2, 1 - core)):
        for side in range(2):
            blocks.append((side, 1 - s, 1 - t, which, refs[first + side]))
    place_experts(place, blocks, (gate_o, up_o, down_o), stage, sems)


def expert_outputs(kernel, args, before, part, width, half):
    near = pl.BlockSpec(memory_space=pltpu.VMEM)
    away = pl.BlockSpec(memory_space=pl.ANY)
    shapes = [
        jax.ShapeDtypeStruct(shape, F32)
        for shape in ((width, half), (width, half), (half, width), (8, HEAD_DIM))
    ]
    blocks = 12 if not before else 4
    return pl.pallas_call(
        kernel,
        out_shape=shapes,
        in_specs=[pl.BlockSpec(memory_space=pltpu.SMEM)]
        + [near] * (len(args) - 1)
        + [away] * len(before),
        out_specs=[away] * 3 + [near],
        scratch_shapes=[
            pltpu.VMEM((blocks,) + part, F32),
            pltpu.SemaphoreType.DMA((2 * blocks,)),
        ],
        input_output_aliases={len(args) + n: n for n in range(len(before))},
        compiler_params=pltpu.CompilerParams(vmem_limit_bytes=56 * 1024 * 1024),
        cost_estimate=pl.CostEstimate(flops=0, bytes_accessed=0, transcendentals=0),
    )(*args, *before)


def back_kernel(
    place, back, hot_t, resid_i, scale_i, gain, cot, weight, probs_i, kv, q, cos, sin,
    grad_resid_o, attended_o, gain_o, query_o, kv_o, *sent_o,
):
    kv_width = kv.shape[1] // 2
    resid = resid_i[...]
    scale = scale_i[:, :1]
    grad_second = dot(hot_t[...], back[...])
    weighted = grad_second * gain[...]
    inner = jnp.sum(weighted * resid, axis=-1, keepdims=True)
    grad_resid = (
        cot[...].astype(F32)
        + scale * weighted
        - resid * (scale * scale * scale * inner * (1.0 / resid.shape[-1]))
    )
    gain_o[...] = jnp.sum(grad_second * resid * scale, axis=0, keepdims=True)
    grad_resid_o[...] = grad_resid
    grad_resid_o.send()
    attended = grad_resid.astype(BF)
    attended_o[...] = attended
    grad_mixed = dot_t(attended, weight[...]).astype(BF)
    pairs = HEADS // KV_HEADS // 2
    rows = resid.shape[0]
    for group in range(KV_HEADS):
        keys = kv[:, pl.ds(group * HEAD_DIM, HEAD_DIM)]
        values = kv[:, pl.ds(kv_width + group * HEAD_DIM, HEAD_DIM)]
        grad_keys = jnp.zeros(keys.shape, F32)
        grad_values = jnp.zeros(keys.shape, F32)
        for pair in range(group * pairs, (group + 1) * pairs):
            low, high = 2 * pair * HEAD_DIM, (2 * pair + 1) * HEAD_DIM
            upper = jnp.concatenate(
                [grad_mixed[:, low:high], grad_mixed[:, high : high + HEAD_DIM]], axis=0
            )
            probs = probs_i[pair]
            wide = probs.astype(F32)
            grad_probs = dot_t(values, upper)
            total = jnp.sum(wide * grad_probs, axis=0, keepdims=True)
            grad_scores = (wide * (grad_probs - total)).astype(BF)
            grad_values = grad_values + dot(probs, upper)
            grad_keys = grad_keys + dot(grad_scores, stacked(q, pair))
            grad_query = t_dot(grad_scores, keys) * HEAD_DIM ** (-0.5)
            for at, part in ((low, grad_query[:rows]), (high, grad_query[rows:])):
                turned = turn_back(part, cos[...], sin[...])
                query_o[:, pl.ds(at, HEAD_DIM)] = turned.astype(BF)
        at = pl.ds(group * HEAD_DIM, HEAD_DIM)
        kv_o[:, at] = (grad_keys * HEAD_DIM ** (-0.5)).astype(BF)
        kv_o[:, pl.ds(kv_width + group * HEAD_DIM, HEAD_DIM)] = grad_values.astype(BF)
    kv_o.send()
    size = resid.shape[1] // XS
    for out, part in zip(sent_o, x_parts(place)):
        at = pl.ds(pl.multiple_of(part * size, size), size)
        one, two = attended_o[:, at], query_o[:, at]
        out[:, pl.ds(0, size)] = jnp.where(place[0] == 0, one, two)
        out[:, pl.ds(size, size)] = jnp.where(place[0] == 0, two, one)


def x_parts(place):
    s, t = place[2], place[3]
    return [
        a + 3 * b - 2 * a * b for a, b in ((s, t), (1 - s, t), (s, 1 - t), (1 - s, 1 - t))
    ]


def collect(pieces, whole, sems, first):
    rows = pieces[0].shape[0]
    copies = []
    for n, piece in enumerate(pieces):
        copy = pltpu.make_async_copy(
            piece, whole.at[pl.ds(n * rows, rows)], sems.at[first + n]
        )
        copy.start()
        copies.append(copy)
    return copies


def interleave(own, other):
    return [piece for pair in zip(own, other) for piece in pair]


def square_weight_kernel(place, *refs):
    own, other, left = refs[:4], refs[4:8], refs[8:16]
    out, all_grads, all_left, sems = refs[16:]
    size = out.shape[1]
    copies = collect(
        interleave(
            [ref.at[:, pl.ds(0, size)] for ref in own],
            [ref.at[:, pl.ds(size, size)] for ref in other],
        ),
        all_grads, sems, 0,
    )
    copies += collect(left, all_left, sems, 8)
    for copy in copies:
        copy.wait()
    step = 256
    for low in range(0, all_left.shape[1], step):
        at = pl.ds(low, step)
        out[at, :] = t_dot(all_left[:, at], all_grads[...]).astype(BF)


def pack_kernel(place, square, gains, *refs):
    grads, left = refs[:8], refs[8:16]
    out, all_grads, all_left, total, sems = refs[16:]
    copies = collect(interleave(grads[:4], grads[4:]), all_grads, sems, 0)
    copies += collect(left, all_left, sems, 8)
    for copy in copies:
        copy.wait()
    total[...] = t_dot(all_left[...], all_grads[...]).astype(BF)
    size, small = square.shape[1], total.shape[1]
    count, groups, part, _ = out.shape
    even = place[0] == 0
    for y in range(count):
        for f in range(groups):
            at = pl.ds((f * count + y) * part, part)
            out[y, f, :, pl.ds(0, size)] = square[at, :]
            out[y, f, :, pl.ds(size, small)] = jnp.where(even, gains[f], total[at, :])
        out.send(y + 1)


def sum_kernel(place, parts, out):
    total = parts[0].astype(F32)
    for k in range(1, parts.shape[0]):
        total = total + parts[k].astype(F32)
    total = total.astype(BF)
    for k in range(out.shape[0]):
        out[k] = total


def final_kernel(place, own, other, mark, output_o, query_o, key_o, value_o, gains_o):
    even = place[0] == 0
    part = own.shape[1]
    size = output_o.shape[1] // XS
    small = key_o.shape[1] * 2 // XS
    total = jnp.zeros(gains_o.shape, F32)
    for y in range(YLO):
        rows = pl.ds(y * part, part)
        for x in range(XS):
            mine, theirs = own[y * XS + x], other[y * XS + x]
            first = jnp.where(even, mine, theirs).astype(F32)
            second = jnp.where(even, theirs, mine).astype(F32)
            at = pl.ds(x * size, size)
            output_o[rows, at] = first[:, :size]
            query_o[rows, at] = second[:, :size]
            into = key_o if x < XS // 2 else value_o
            into[rows, pl.ds(x % (XS // 2) * small, small)] = second[:, size:]
            if y == 0:
                total = total + first[:, size:]
    gains_o[...] = total


def key_back_kernel(place, parts, cos, sin, pre_o, *sent_o):
    kv_width = parts.shape[-1] // 2
    total = parts[0].astype(F32)
    for k in range(1, parts.shape[0]):
        total = total + parts[k].astype(F32)
    for head in range(2 * KV_HEADS):
        low, high = head * HEAD_DIM, (head + 1) * HEAD_DIM
        piece = total[:, low:high]
        if head < KV_HEADS:
            piece = turn_back(piece, cos[...], sin[...])
        pre_o[:, low:high] = piece.astype(BF)
    size = 2 * kv_width // XS
    for out, part in zip(sent_o, x_parts(place)):
        out[...] = pre_o[:, pl.ds(pl.multiple_of(part * size, size), size)]


def input_kernel(
    place, query, pre, src, scale_i, gain, query_w, kv_w, grad_resid, input_o, gain_o
):
    grad_normed = dot_t(query[...], query_w[...]) + dot_t(pre[...], kv_w[...])
    source = src[...].astype(F32)
    scale = scale_i[:, :1]
    weighted = grad_normed * gain[...]
    inner = jnp.sum(weighted * source, axis=-1, keepdims=True)
    input_o[...] = (
        grad_resid[...]
        + scale * weighted
        - source * (scale * scale * scale * inner * (1.0 / source.shape[-1]))
    ).astype(BF)
    gain_o[...] = jnp.sum(grad_normed * source * scale, axis=0, keepdims=True)


class Far:
    def __init__(self, value, kind=None, parts=1):
        self.value, self.kind, self.parts = value, kind, parts


class Coming:
    def __init__(self, source, ref, sem):
        self.copy, self.ref, self.waits = pltpu.make_async_copy(source, ref, sem), ref, True
        self.shape = ref.shape
        self.copy.start()

    def now(self):
        if self.waits:
            self.copy.wait()
            self.waits = False
        return self.ref

    def __getitem__(self, index):
        return self.now()[index]

    @property
    def at(self):
        return self.now().at


class Going:
    def __init__(self, ref, target, sems, parts):
        self.ref, self.target, self.shape, self.sent = ref, target, ref.shape, 0
        rows = ref.shape[0] // parts
        self.copies = [
            pltpu.make_async_copy(
                ref.at[pl.ds(n * rows, rows)], target.at[pl.ds(n * rows, rows)], sem
            )
            for n, sem in enumerate(sems)
        ]

    def __getitem__(self, index):
        return self.ref[index]

    def __setitem__(self, index, value):
        self.ref[index] = value

    def send(self, upto=None):
        upto = len(self.copies) if upto is None else upto
        for copy in self.copies[self.sent : upto]:
            copy.start()
        self.sent = max(self.sent, upto)


def send(self):
        if not self.sent:
            self.copy.start()
            self.sent = True


def send(*results):
    for result in results:
        result.send()


def call(kernel, args, outs, scratch=(), micros=0, raw=()):
    outs = [out if isinstance(out, Far) else Far(*out) for out in outs]
    values = [a.value if isinstance(a, Far) else a for a in args]
    far = [i for i, a in enumerate(args) if isinstance(a, Far) and i not in raw]
    count, made = len(args), len(outs)

    def whole(*refs):
        ins, results = list(refs[:count]), refs[count : count + made]
        own = refs[count + made : count + made + len(scratch)]
        rest = refs[count + made + len(scratch) :]
        landing, leaving, sems = rest[: len(far)], rest[len(far) : len(far) + made], rest[-1]
        for n, i in enumerate(far):
            ins[i] = Coming(ins[i], landing[n], sems.at[n])
        going, used = [], len(far)
        for out, ref, target in zip(outs, leaving, results):
            going.append(
                Going(ref, target, [sems.at[used + n] for n in range(out.parts)], out.parts)
            )
            used += out.parts
        kernel(*ins, *going, *own)
        for i in far:
            ins[i].now()
        send(*going)
        for result in going:
            for copy in result.copies:
                copy.wait()

    near = pl.BlockSpec(memory_space=pltpu.VMEM)
    away = pl.BlockSpec(memory_space=pl.ANY)
    specs = [away if isinstance(a, Far) else near for a in args]
    specs[0] = pl.BlockSpec(memory_space=pltpu.SMEM)
    return pl.pallas_call(
        whole,
        out_shape=[jax.ShapeDtypeStruct(out.value, out.kind) for out in outs],
        in_specs=specs,
        out_specs=[away] * made,
        scratch_shapes=[
            *scratch,
            *[pltpu.VMEM(values[i].shape, values[i].dtype) for i in far],
            *[pltpu.VMEM(out.value, out.kind) for out in outs],
            pltpu.SemaphoreType.DMA((len(far) + sum(out.parts for out in outs),)),
        ],
        compiler_params=pltpu.CompilerParams(vmem_limit_bytes=56 * 1024 * 1024),
        cost_estimate=pl.CostEstimate(
            flops=int(micros * 1e9), bytes_accessed=0, transcendentals=0
        ),
    )(*values)


def swap(v):
    return lax.ppermute(v, "core", [(0, 1), (1, 0)])


def swap_y(v):
    return lax.ppermute(v, "ylo", [(0, 1), (1, 0)])


def exchange(v, axis):
    return lax.all_to_all(v, axis, 0, 0, tiled=True)


def copies(v, n):
    return lax.optimization_barrier(jnp.broadcast_to(v[None], (n,) + v.shape))


def tie(*values):
    return lax.optimization_barrier(values)


PAIRS_S = [(0, 1), (1, 0), (2, 3), (3, 2)]
PAIRS_T = [(0, 3), (3, 0), (1, 2), (2, 1)]
PAIRS_ST = [(0, 2), (2, 0), (1, 3), (3, 1)]


def x_bits():
    x = lax.axis_index("x")
    return ((x + 1) // 2) % 2, x // 2


def flip(v, pairs):
    return lax.ppermute(v, "x", pairs)


def body(
    inputs,
    segments,
    first_gain,
    query_matrix,
    key_matrix,
    value_matrix,
    output_matrix,
    second_gain,
    expert_ids,
    gate_values,
    priority,
    gate_weight,
    up_weight,
    down_weight,
    cotangent,
):
    tok = inputs.shape[1]
    width = inputs.shape[2]
    rows = query_matrix.shape[0]
    groups = lax.axis_size("fsdp")
    member = lax.axis_index("fsdp")
    core = lax.axis_index("core")
    even = core == 0
    experts = groups
    capacity = 5 * tok * TOP // (4 * experts)
    slots_all = experts * capacity
    half = width // 2
    kv_width = key_matrix.shape[1]
    length = groups * tok
    quarter = rows // XS
    bit_s, bit_t = x_bits()
    place_at = jnp.stack([core, member * tok, bit_s, bit_t]).astype(jnp.int32)

    def pick(a, b):
        return jnp.where(even, a, b)

    parts = width // kv_width
    kv_rows = rows // parts
    kv_half = pick(key_matrix, value_matrix).reshape(parts, kv_rows, kv_width)
    kv_piece = jnp.concatenate([kv_half[j] for j in range(parts)], axis=1)
    gains = jnp.pad(jnp.stack([first_gain, second_gain]), ((0, 6), (0, width - rows)))
    square_piece = jnp.concatenate(
        [
            lax.dynamic_slice(matrix, (bit * (rows // 2), core * half), (rows // 2, half))
            for matrix, bit in ((query_matrix, bit_s), (output_matrix, bit_t))
        ],
        axis=1,
    )
    kv_piece = jnp.concatenate([kv_piece, gains], axis=0)
    gathered = exchange(copies(kv_piece, groups), "fsdp")
    square_piece = copies(square_piece, groups)
    gathered, square_piece, place_at = tie(gathered, square_piece, place_at)
    squares = exchange(square_piece, "fsdp")

    ids = expert_ids[0].reshape(-1)
    order = priority[0, 0]
    earlier = (order[None, :] < order[:, None]) & (ids[None, :] == ids[:, None])
    slots = jnp.sum(earlier.astype(jnp.int32), axis=1)
    kept = slots < capacity
    expert_list = jnp.arange(experts, dtype=jnp.int32)
    chosen = (ids[:, None] == expert_list[None, :]) & kept[:, None]
    slot_of = jnp.sum(
        jnp.where(chosen, slots[:, None] + 1, 0).reshape(tok, TOP, experts), axis=1
    )
    slot_of = slot_of - 1
    gate_table = jnp.sum(
        jnp.where(chosen, gate_values[0].reshape(-1)[:, None], 0.0).reshape(tok, TOP, experts),
        axis=1,
    )
    slot_list = jnp.arange(capacity, dtype=jnp.int32)
    hits = slot_of.T[:, None, :] == slot_list[None, :, None]
    one_hot = hits.astype(BF).reshape(slots_all, tok)
    one_hot_t = (slot_of[:, :, None] == slot_list[None, None, :]).astype(BF)
    one_hot_t = one_hot_t.reshape(tok, slots_all)
    gate_hot = jnp.where(hits, gate_table.T[:, None, :], 0.0).reshape(slots_all, tok)
    slot_gate = jnp.sum(gate_hot, axis=1, keepdims=True)
    gate_high = gate_hot.astype(BF)
    gate_low = (gate_hot - gate_high.astype(F32)).astype(BF)
    send_grad = (dot(one_hot, cotangent[0]) * slot_gate).astype(BF)

    cosine, sine = angles(member * tok + jnp.arange(tok, dtype=jnp.int32))
    segment_row = segments[0]
    query_segments = lax.dynamic_slice_in_dim(segment_row, member * tok, tok)
    key_place = jnp.arange(length, dtype=jnp.int32)[:, None]
    query_place = (member * tok + jnp.arange(tok, dtype=jnp.int32))[None, :]
    allowed = (
        (key_place <= query_place)
        & (query_place - key_place < WINDOW)
        & (segment_row[:, None] == query_segments[None, :])
    )
    bias = jnp.where(allowed, 0.0, NEGATIVE).astype(F32)
    bias = jnp.concatenate([bias, bias], axis=1)
    gathered, cosine, sine = tie(gathered, cosine, sine)
    kv_raw = gathered[:, :kv_rows]
    gain_one = gathered[:, kv_rows, :rows].reshape(1, width).astype(F32)
    gain_two = gathered[:, kv_rows + 1, :rows].reshape(1, width).astype(F32)
    kv_raw_other = swap(kv_raw)

    square = (width, width)
    normed, scale_one, kv_send, kv_weight = call(
        key_kernel,
        [place_at, Far(inputs[0]), gain_one, Far(kv_raw), Far(kv_raw_other), cosine, sine],
        [((tok, width), BF), ((tok, HEAD_DIM), F32), ((groups, tok, 2 * kv_width), BF),
         ((width, 2 * kv_width), BF)],
    )
    kv_send, squares, one_hot_t, gate_high, gate_low, send_grad, bias = tie(
        kv_send, squares, one_hot_t, gate_high, gate_low, send_grad, bias
    )
    q_own, o_own = squares[..., :half], squares[..., half:]
    kv_all = exchange(kv_send, "fsdp").reshape(length, 2 * kv_width)
    q_got, o_got = flip(q_own, PAIRS_S), flip(o_own, PAIRS_T)
    send_grad, kv_all = tie(send_grad, kv_all)
    arrived_grad = exchange(send_grad, "fsdp")
    far_pieces = [
        Far(v)
        for v in (q_own, q_got, swap(q_own), swap(q_got), o_own, o_got, swap(o_own), swap(o_got))
    ]
    weight_parts = (groups, rows, width)
    (query_weight, output_weight, query_rot, mixed, probs, residual, scale_two,
     send_rows) = call(
        front_kernel,
        [place_at, Far(normed), Far(kv_all), Far(bias), Far(inputs[0]), gain_two, Far(one_hot_t),
         cosine, sine, *far_pieces],
        [(weight_parts, BF), (weight_parts, BF), ((tok, width), BF), ((tok, width), BF),
         ((HEADS // 2, length, 2 * tok), BF), ((tok, width), F32), ((tok, HEAD_DIM), F32),
         ((slots_all, width), BF)],
        [pltpu.SemaphoreType.DMA((8,))],
        raw=range(9, 17),
    )
    query_weight = query_weight.reshape(square)
    output_weight = output_weight.reshape(square)

    send_rows, arrived_grad = tie(send_rows, arrived_grad)
    arrived = exchange(send_rows, "fsdp")

    left_a = pick(mixed, normed)
    left_b = swap(pick(normed, mixed))
    left_one_a, left_two_a = flip(left_a, PAIRS_S), flip(left_a, PAIRS_T)
    left_one_b, left_two_b = flip(left_b, PAIRS_T), flip(left_b, PAIRS_S)
    upper_other = swap(lax.dynamic_slice_in_dim(arrived_grad, (1 - core) * half, half, 1))
    grad_hidden = dot_t(arrived_grad, down_weight[0])
    arrived, grad_hidden, upper_other, left_one_a, left_two_a, left_one_b, left_two_b = tie(
        arrived, grad_hidden, upper_other, left_one_a, left_two_a, left_one_b, left_two_b
    )
    left_three_a, left_three_b = flip(left_one_a, PAIRS_T), flip(left_one_b, PAIRS_S)
    arrived_other = swap(arrived)
    hidden, own_pre, sent_pre, grad_rows = call(
        expert_kernel,
        [place_at, Far(arrived), Far(grad_hidden), gate_weight[0], up_weight[0]],
        [Far((slots_all, half), BF, 2)] * 3 + [Far((slots_all, width), BF, 2)],
    )
    back_rows = exchange(grad_rows, "fsdp")
    expert_rows = width + half

    e_part = (2, expert_rows // 8, half)
    e_keep_a, e_send_a, e_keep_b, e_send_b = call(
        expert_weight_kernel,
        [place_at] + [Far(v) for v in (arrived, arrived_other, own_pre, swap(sent_pre), hidden,
                                       swap(hidden), arrived_grad, upper_other)],
        [(e_part, BF)] * 4,
        [pltpu.VMEM((expert_rows, half), BF)],
    )
    expert_out = dot(hidden, down_weight[0]).astype(BF)
    e_got_a, e_got_b = flip(e_send_a, PAIRS_S), flip(e_send_b, PAIRS_T)
    back_rows, expert_out, e_keep_a, e_keep_b, left_three_a, left_three_b = tie(
        back_rows, expert_out, e_keep_a, e_keep_b, left_three_a, left_three_b
    )
    left = [left_a, left_b, left_one_a, left_two_b, left_two_a, left_one_b, left_three_a,
            left_three_b]

    grad_residual, grad_attended, gain_two_part, grad_query_pre, kv_back, *qo_sent = call(
        back_kernel,
        [place_at, Far(back_rows), Far(one_hot_t), Far(residual), Far(scale_two), gain_two,
         Far(cotangent[0]), Far(output_weight), Far(probs), Far(kv_all), Far(query_rot), cosine,
         sine],
        [((tok, width), F32), ((tok, width), BF), ((1, width), F32), ((tok, width), BF),
         ((length, 2 * kv_width), BF)] + [((tok, half), BF)] * XS,
    )
    kv_got = exchange(kv_back, "fsdp")
    e_keep_a, e_send_a, e_keep_b, e_send_b = call(
        expert_step_kernel,
        [place_at, Far(e_keep_a), Far(e_got_a), Far(e_keep_b), Far(e_got_b)],
        [(e_part[1:], BF)] * 4,
    )
    e_got_a, e_got_b = flip(e_send_a, PAIRS_T), flip(e_send_b, PAIRS_S)
    qo_set = fan(qo_sent)
    whole = 2 * XS * tok
    square_grad = call(
        square_weight_kernel,
        [place_at] + [Far(v) for v in (*qo_set, *[swap(v) for v in qo_set], *left)],
        [((width, width // XS), BF)],
        [pltpu.VMEM((whole, width // XS), BF), pltpu.VMEM((whole, width), BF),
         pltpu.SemaphoreType.DMA((16,))],
        raw=range(1, 17),
    )[0]
    kv_got, square_grad = tie(kv_got, square_grad)
    grad_kv_pre, *kv_sent = call(
        key_back_kernel,
        [place_at, Far(kv_got.reshape(groups, tok, 2 * kv_width)), cosine, sine],
        [((tok, 2 * kv_width), BF)] + [((tok, 2 * kv_width // XS), BF)] * XS,
    )
    kv_sent[0], expert_out = tie(kv_sent[0], expert_out)
    returned = exchange(expert_out, "fsdp")
    kv_set = fan(kv_sent)
    e_sum = call(
        expert_end_kernel,
        [place_at, Far(e_keep_a), Far(e_got_a), Far(e_keep_b), Far(e_got_b)],
        [(e_part, BF)],
    )[0]
    e_other_y = swap_y(e_sum)
    input_grad, gain_one_part = call(
        input_kernel,
        [place_at, Far(grad_query_pre), Far(grad_kv_pre), Far(inputs[0]), Far(scale_one), gain_one,
         Far(query_weight), Far(kv_weight), Far(grad_residual)],
        [((tok, width), BF), ((1, width), F32)],
    )

    e_zero_a, e_zero_b = call(pair_kernel, [place_at, Far(e_sum), Far(e_other_y)], [(e_part[1:], BF)] * 2)
    e_one_a, e_one_b = flip(e_zero_a, PAIRS_T), flip(e_zero_b, PAIRS_S)
    e_two_a, e_two_b = flip(e_zero_a, PAIRS_S), flip(e_zero_b, PAIRS_T)

    spare = 2 * kv_width // XS
    part = rows // YLO
    gain_parts = jnp.concatenate([gain_one_part, gain_two_part])
    gain_parts = gain_parts + swap(gain_parts)
    gain_parts = gain_parts.reshape(2, groups, part, YLO).transpose(1, 2, 0, 3)
    gain_parts = gain_parts.reshape(groups, part, 2 * YLO).astype(BF)
    gain_parts = jnp.pad(gain_parts, ((0, 0), (0, 0), (0, spare - 2 * YLO)))
    packed_width = width // XS + spare
    packed = call(
        pack_kernel,
        [place_at, Far(square_grad), gain_parts]
        + [Far(v) for v in (*kv_set, *[swap(v) for v in kv_set], *left)],
        [Far((YLO, groups, part, packed_width), BF, 2)],
        [pltpu.VMEM((whole, spare), BF), pltpu.VMEM((whole, width), BF),
         pltpu.VMEM((width, spare), BF), pltpu.SemaphoreType.DMA((16,))],
        raw=range(3, 19),
    )[0]
    packed, returned = tie(packed, returned)
    packed = exchange(packed.reshape(YLO * groups, part, packed_width), ("ylo", "fsdp"))
    mixture = t_dot(gate_high, returned) + t_dot(gate_low, returned)
    outputs = (residual + mixture).astype(BF)
    packed, outputs = tie(packed, outputs)
    packed = call(sum_kernel, [place_at, Far(packed)], [((YLO * XS, part, packed_width), BF)])[0]
    spreaded = exchange(packed, ("ylo", "x"))
    most = [e_zero_a, e_zero_b, e_one_a, e_one_b, e_two_a, e_two_b]
    *e_grads, most_mark = expert_outputs(
        expert_most_kernel, [place_at, *most, *[swap(v) for v in most]], [], e_part[1:], width, half
    )
    e_one_a, e_one_b, packed = tie(e_one_a, e_one_b, packed)
    e_three_a, e_three_b = flip(e_one_a, PAIRS_S), flip(e_one_b, PAIRS_T)
    e_three_a, e_three_b, most_mark = tie(e_three_a, e_three_b, most_mark)
    grad_gate, grad_up, grad_down, e_mark = expert_outputs(
        expert_rest_kernel,
        [place_at, e_three_a, e_three_b, swap(e_three_a), swap(e_three_b), most_mark,
         packed[0, :16, :HEAD_DIM]],
        e_grads,
        e_part[1:],
        width,
        half,
    )
    spreaded, e_mark = tie(spreaded, e_mark)
    grad_output_w, grad_query_w, grad_key_w, grad_value_w, gains_sum = call(
        final_kernel,
        [place_at, Far(spreaded), Far(swap(spreaded)), e_mark],
        [((rows, width), F32), ((rows, width), F32), ((rows, kv_width), F32),
         ((rows, kv_width), F32), ((part, spare), F32)],
    )
    gains_sum = gains_sum[:, : 2 * YLO].reshape(part, 2, YLO).transpose(1, 0, 2)
    gains_sum = gains_sum.reshape(2, rows)
    return (
        outputs[None],
        input_grad[None],
        gains_sum[0],
        grad_query_w,
        grad_key_w,
        grad_value_w,
        grad_output_w,
        gains_sum[1],
        grad_gate[None],
        grad_up[None],
        grad_down[None],
    )


def solution(mesh):
    shape = mesh.devices.shape
    fine = Mesh(
        mesh.devices.reshape(YLO, XS, CORES, shape[1]), ("ylo", "x", "core", "fsdp")
    )
    return jax.shard_map(
        body,
        mesh=fine,
        in_specs=(
            P(REP, "fsdp", None),
            P(REP, None),
            P("fsdp"),
            P("fsdp", None),
            P("fsdp", None),
            P("fsdp", None),
            P("fsdp", None),
            P("fsdp"),
            P(REP, "fsdp", None),
            P(REP, "fsdp", None),
            P(REP, "fsdp", None),
            P("fsdp", None, None),
            P("fsdp", None, None),
            P("fsdp", None, None),
            P(REP, "fsdp", None),
        ),
        out_specs=(
            P(REP, "fsdp", None),
            P(REP, "fsdp", None),
            P("fsdp"),
            P("fsdp", None),
            P("fsdp", None),
            P("fsdp", None),
            P("fsdp", None),
            P("fsdp"),
            P("fsdp", None, None),
            P("fsdp", None, None),
            P("fsdp", None, None),
        ),
        check_vma=False,
    )
```

```python
import jax
import jax.numpy as jnp
from jax import lax
from jax.experimental import pallas as pl
from jax.experimental.pallas import tpu as pltpu
from jax.sharding import Mesh
from jax.sharding import PartitionSpec as P

HEADS = 12
KV_HEADS = 2
HEAD_DIM = 128
TOP = 4
WINDOW = 1024

EPSILON = 1e-06
THETA = 10000.0
NEGATIVE = -1e30

YLO, XS, CORES = 2, 4, 2
REP = ("ylo", "x", "core")
BF = jnp.bfloat16
F32 = jnp.float32


def angles(positions):
    half_width = HEAD_DIM // 2
    frequency = THETA ** (-(jnp.arange(half_width, dtype=F32) * 2.0) / HEAD_DIM)
    phase = positions.astype(F32)[:, None] * frequency[None, :]
    cosine, sine = jnp.cos(phase), jnp.sin(phase)
    return (
        jnp.concatenate([cosine, cosine], axis=1),
        jnp.concatenate([-sine, sine], axis=1),
    )


def dot(a, b):
    return jnp.dot(a, b, preferred_element_type=F32)


def dot_t(a, b):
    return lax.dot_general(a, b, (((1,), (1,)), ((), ())), preferred_element_type=F32)


def t_dot(a, b):
    return lax.dot_general(a, b, (((0,), (0,)), ((), ())), preferred_element_type=F32)


def fan(pieces):
    return [
        pieces[0],
        flip(pieces[1], PAIRS_S),
        flip(pieces[2], PAIRS_T),
        flip(pieces[3], PAIRS_ST),
    ]


def add(a, b):
    return (a.astype(F32) + b.astype(F32)).astype(BF)


def turn(piece, cosine, sine):
    return piece * cosine + pltpu.roll(piece, HEAD_DIM // 2, 1) * sine


def turn_back(piece, cosine, sine):
    return piece * cosine - pltpu.roll(piece, HEAD_DIM // 2, 1) * sine


def stacked(ref, pair):
    low = 2 * pair * HEAD_DIM
    return jnp.concatenate(
        [ref[:, pl.ds(low, HEAD_DIM)], ref[:, pl.ds(low + HEAD_DIM, HEAD_DIM)]], axis=0
    )


def unstack(ref, pair, value):
    low, rows = 2 * pair * HEAD_DIM, value.shape[0] // 2
    ref[:, pl.ds(low, HEAD_DIM)] = value[:rows]
    ref[:, pl.ds(low + HEAD_DIM, HEAD_DIM)] = value[rows:]


def put_gain(out, total):
    groups, _, lanes = out.shape
    size = total.shape[1] // groups
    for f in range(groups):
        row = total[:, f * size : (f + 1) * size]
        out[f, 0:1, :] = row[:, :lanes]
        out[f, 1:2, pl.ds(0, size - lanes)] = row[:, lanes:]


def key_kernel(place, src, gain, raw_own, raw_other, cos, sin, normed_o, scale_o, send_o, weight_o):
    core = place[0]
    groups, kv_rows, width = raw_own.shape
    kv_width = weight_o.shape[1] // 2
    parts = width // kv_width
    source = src[...].astype(F32)
    scale = lax.rsqrt(jnp.mean(source * source, axis=-1, keepdims=True) + EPSILON)
    scale_o[...] = jnp.broadcast_to(scale, scale_o.shape)
    normed = (source * scale * gain[...]).astype(BF)
    normed_o[...] = normed
    send(scale_o, normed_o)
    for raw, which in ((raw_own, core), (raw_other, 1 - core)):
        at = pl.ds(pl.multiple_of(which * kv_width, kv_width), kv_width)
        for f in range(groups):
            for j in range(parts):
                weight_o[pl.ds((f * parts + j) * kv_rows, kv_rows), at] = raw[
                    f, :, pl.ds(j * kv_width, kv_width)
                ]
    send(weight_o)
    pre = dot(normed, weight_o[...])
    for head in range(2 * KV_HEADS):
        low, high = head * HEAD_DIM, (head + 1) * HEAD_DIM
        piece = pre[:, low:high]
        if head < KV_HEADS:
            piece = turn(piece, cos[...], sin[...])
        for f in range(groups):
            send_o[f, :, low:high] = piece.astype(BF)


def front_kernel(place, normed, kv, bias, src, gain, hot_t, cos, sin, *refs):
    pieces = refs[:8]
    query_w, output_w, query_o, mixed_o, probs_o, resid_o, scale_o, send_o, sems = refs[8:]
    core, s, t = place[0], place[2], place[3]
    _, rows, half = pieces[0].shape
    copies = []
    for n, block in enumerate(pieces):
        weight, bit = ((query_w, s), (output_w, t))[n // 4]
        which = core if n % 4 < 2 else 1 - core
        part = bit if n % 2 == 0 else 1 - bit
        at = pl.ds(pl.multiple_of(part * rows, rows), rows)
        cols = pl.ds(pl.multiple_of(which * half, half), half)
        copy = pltpu.make_async_copy(block, weight.ref.at[:, at, cols], sems.at[n])
        copy.start()
        copies.append(copy)
    width = 2 * half
    for copy in copies[:4]:
        copy.wait()
    query_w.send()
    pre = dot(normed[...], query_w[...].reshape(width, width))
    for head in range(HEADS):
        low, high = head * HEAD_DIM, (head + 1) * HEAD_DIM
        query_o[:, low:high] = turn(pre[:, low:high], cos[...], sin[...]).astype(BF)
    query_o.send()
    kv_width = kv.shape[1] // 2
    for pair in range(HEADS // 2):
        group = 2 * pair // (HEADS // KV_HEADS)
        keys = kv[:, pl.ds(group * HEAD_DIM, HEAD_DIM)]
        values = kv[:, pl.ds(kv_width + group * HEAD_DIM, HEAD_DIM)]
        scores = dot_t(keys, stacked(query_o, pair)) * HEAD_DIM ** (-0.5) + bias[...]
        weights = jnp.exp(scores - jnp.max(scores, axis=0, keepdims=True))
        probs = (weights * (1.0 / jnp.sum(weights, axis=0, keepdims=True))).astype(BF)
        probs_o[pair] = probs
        unstack(mixed_o, pair, t_dot(probs, values).astype(BF))
    send(probs_o, mixed_o)
    for copy in copies[4:]:
        copy.wait()
    output_w.send()
    resid = src[...].astype(F32) + dot(mixed_o[...], output_w[...].reshape(width, width))
    resid_o[...] = resid
    resid_o.send()
    scale = lax.rsqrt(jnp.mean(resid * resid, axis=-1, keepdims=True) + EPSILON)
    scale_o[...] = jnp.broadcast_to(scale, scale_o.shape)
    second = (resid * scale * gain[...]).astype(BF)
    send_o[...] = t_dot(hot_t[...], second).astype(BF)


def expert_kernel(place, rows, grad_hidden, gate_w, up_w, hidden_o, own_o, sent_o, back_o):
    core = place[0]
    count = rows.shape[0]
    step = count // 2
    for n, low in enumerate(range(0, count, step)):
        at = pl.ds(low, step)
        block = rows[at, :]
        gate = dot(block, gate_w[...])
        up = dot(block, up_w[...])
        sigmoid = 1.0 / (1.0 + jnp.exp(-gate))
        silu = gate * sigmoid
        hidden_o[at, :] = (silu * up).astype(BF)
        grad = grad_hidden[at, :]
        grad_gate = (grad * up * (sigmoid * (1.0 + gate * (1.0 - sigmoid)))).astype(BF)
        grad_up = (grad * silu).astype(BF)
        own_o[at, :] = jnp.where(core == 0, grad_gate, grad_up)
        sent_o[at, :] = jnp.where(core == 0, grad_up, grad_gate)
        for result in (sent_o, hidden_o, own_o):
            result.send(n + 1)
        back_o[at, :] = (dot_t(grad_gate, gate_w[...]) + dot_t(grad_up, up_w[...])).astype(BF)
        back_o.send(n + 1)


def expert_weight_kernel(
    place, rows, rows_got, pre, pre_got, hidden, hidden_got, arrived, upper_got,
    keep_a, send_a, keep_b, send_b, total,
):
    s, t = place[2], place[3]
    width, half = rows.shape[1], hidden.shape[1]
    upper = arrived[:, pl.ds(pl.multiple_of(place[0] * half, half), half)]
    step = 256
    for low in range(0, width, step):
        at = pl.ds(low, step)
        total[at, :] = (t_dot(rows[:, at], pre[...]) + t_dot(rows_got[:, at], pre_got[...])).astype(
            BF
        )
    for low in range(0, half, step):
        at = pl.ds(low, step)
        total[pl.ds(width + low, step), :] = (
            t_dot(hidden[:, at], upper) + t_dot(hidden_got[:, at], upper_got[...])
        ).astype(BF)
    big, small = width // 8, half // 8
    for out, side, spots in (
        (send_a, 0, ((1 - s, 0), (1 - s, 1))),
        (send_b, 1, ((0, 1 - t), (1, 1 - t))),
        (keep_a, 0, ((s, 0), (s, 1))),
        (keep_b, 1, ((0, t), (1, t))),
    ):
        for j, (row_s, row_t) in enumerate(spots):
            piece = side * 4 + 2 * row_s + row_t
            out[j, pl.ds(0, big), :] = total[pl.ds(pl.multiple_of(piece * big, big), big), :]
            start = pl.multiple_of(width + piece * small, small)
            out[j, pl.ds(big, small), :] = total[pl.ds(start, small), :]
        out.send()


def expert_step_kernel(place, keep_a, got_a, keep_b, got_b, keep_ao, send_ao, keep_bo, send_bo):
    s, t = place[2], place[3]
    send_ao[...] = add(keep_a[1 - t], got_a[1 - t])
    send_ao.send()
    send_bo[...] = add(keep_b[1 - s], got_b[1 - s])
    send_bo.send()
    keep_ao[...] = add(keep_a[t], got_a[t])
    keep_ao.send()
    keep_bo[...] = add(keep_b[s], got_b[s])


def expert_end_kernel(place, keep_a, got_a, keep_b, got_b, mark, out):
    out[0] = add(keep_a[...], got_a[...])
    out[1] = add(keep_b[...], got_b[...])


def pair_kernel(place, a, b, one, two):
    one[...] = add(a[0], b[0])
    one.send()
    two[...] = add(a[1], b[1])


def place_experts(place, blocks, outs, stage, sems):
    core = place[0]
    gate_o, up_o, down_o = outs
    half = stage.shape[2]
    big = gate_o.shape[0] // 8
    small = stage.shape[1] - big
    moves = []
    for n, (side, row_s, row_t, which, block) in enumerate(blocks):
        stage[n] = block[...].astype(F32)
        piece = side * 4 + 2 * row_s + row_t
        at = pl.ds(pl.multiple_of(piece * big, big), big)
        cols = pl.ds(pl.multiple_of(which * half, half), half)
        to_gate = pltpu.make_async_copy(stage.at[n, pl.ds(0, big)], gate_o.at[at], sems.at[2 * n])
        to_up = pltpu.make_async_copy(stage.at[n, pl.ds(0, big)], up_o.at[at], sems.at[2 * n])
        to_down = pltpu.make_async_copy(
            stage.at[n, pl.ds(big, small)],
            down_o.at[pl.ds(pl.multiple_of(piece * small, small), small), cols],
            sems.at[2 * n + 1],
        )

        @pl.when(which == 0)
        def _():
            to_gate.start()

        @pl.when(which == 1)
        def _():
            to_up.start()

        to_down.start()
        moves.append((which, to_gate, to_up, to_down))
    for which, to_gate, to_up, to_down in moves:

        @pl.when(which == 0)
        def _():
            to_gate.wait()

        @pl.when(which == 1)
        def _():
            to_up.wait()

        to_down.wait()


def expert_most_kernel(place, *refs):
    core, s, t = place[0], place[2], place[3]
    gate_o, up_o, down_o, mark_o, stage, sems = refs[12:]
    mark_o[...] = jnp.zeros(mark_o.shape, F32)
    blocks = []
    for first, which in ((0, core), (6, 1 - core)):
        zero_a, zero_b, one_a, one_b, two_a, two_b = refs[first : first + 6]
        blocks += [
            (0, s, t, which, zero_a),
            (1, s, t, which, zero_b),
            (0, s, 1 - t, which, one_a),
            (1, 1 - s, t, which, one_b),
            (0, 1 - s, t, which, two_a),
            (1, s, 1 - t, which, two_b),
        ]
    place_experts(place, blocks, (gate_o, up_o, down_o), stage, sems)


def expert_rest_kernel(place, *refs):
    core, s, t = place[0], place[2], place[3]
    gate_o, up_o, down_o, mark_o, stage, sems = refs[9:]
    mark_o[...] = jnp.zeros(mark_o.shape, F32)
    blocks = []
    for first, which in ((0, core), (2, 1 - core)):
        for side in range(2):
            blocks.append((side, 1 - s, 1 - t, which, refs[first + side]))
    place_experts(place, blocks, (gate_o, up_o, down_o), stage, sems)


def expert_outputs(kernel, args, before, part, width, half):
    near = pl.BlockSpec(memory_space=pltpu.VMEM)
    away = pl.BlockSpec(memory_space=pl.ANY)
    shapes = [
        jax.ShapeDtypeStruct(shape, F32)
        for shape in ((width, half), (width, half), (half, width), (8, HEAD_DIM))
    ]
    blocks = 12 if not before else 4
    return pl.pallas_call(
        kernel,
        out_shape=shapes,
        in_specs=[pl.BlockSpec(memory_space=pltpu.SMEM)]
        + [near] * (len(args) - 1)
        + [away] * len(before),
        out_specs=[away] * 3 + [near],
        scratch_shapes=[
            pltpu.VMEM((blocks,) + part, F32),
            pltpu.SemaphoreType.DMA((2 * blocks,)),
        ],
        input_output_aliases={len(args) + n: n for n in range(len(before))},
        compiler_params=pltpu.CompilerParams(vmem_limit_bytes=56 * 1024 * 1024),
        cost_estimate=pl.CostEstimate(flops=0, bytes_accessed=0, transcendentals=0),
    )(*args, *before)


def back_kernel(
    place, back, hot_t, resid_i, scale_i, gain, cot, weight, probs_i, kv, q, cos, sin,
    grad_resid_o, attended_o, gain_o, query_o, kv_o, *sent_o,
):
    kv_width = kv.shape[1] // 2
    resid = resid_i[...]
    scale = scale_i[:, :1]
    grad_second = dot(hot_t[...], back[...])
    weighted = grad_second * gain[...]
    inner = jnp.sum(weighted * resid, axis=-1, keepdims=True)
    grad_resid = (
        cot[...].astype(F32)
        + scale * weighted
        - resid * (scale * scale * scale * inner * (1.0 / resid.shape[-1]))
    )
    put_gain(gain_o, jnp.sum(grad_second * resid * scale, axis=0, keepdims=True))
    grad_resid_o[...] = grad_resid
    grad_resid_o.send()
    attended = grad_resid.astype(BF)
    attended_o[...] = attended
    grad_mixed = dot_t(attended, weight[...]).astype(BF)
    pairs = HEADS // KV_HEADS // 2
    rows = resid.shape[0]
    for group in range(KV_HEADS):
        keys = kv[:, pl.ds(group * HEAD_DIM, HEAD_DIM)]
        values = kv[:, pl.ds(kv_width + group * HEAD_DIM, HEAD_DIM)]
        grad_keys = jnp.zeros(keys.shape, F32)
        grad_values = jnp.zeros(keys.shape, F32)
        for pair in range(group * pairs, (group + 1) * pairs):
            low, high = 2 * pair * HEAD_DIM, (2 * pair + 1) * HEAD_DIM
            upper = jnp.concatenate(
                [grad_mixed[:, low:high], grad_mixed[:, high : high + HEAD_DIM]], axis=0
            )
            probs = probs_i[pair]
            wide = probs.astype(F32)
            grad_probs = dot_t(values, upper)
            total = jnp.sum(wide * grad_probs, axis=0, keepdims=True)
            grad_scores = (wide * (grad_probs - total)).astype(BF)
            grad_values = grad_values + dot(probs, upper)
            grad_keys = grad_keys + dot(grad_scores, stacked(q, pair))
            grad_query = t_dot(grad_scores, keys) * HEAD_DIM ** (-0.5)
            for at, part in ((low, grad_query[:rows]), (high, grad_query[rows:])):
                turned = turn_back(part, cos[...], sin[...])
                query_o[:, pl.ds(at, HEAD_DIM)] = turned.astype(BF)
        at = pl.ds(group * HEAD_DIM, HEAD_DIM)
        kv_o[:, at] = (grad_keys * HEAD_DIM ** (-0.5)).astype(BF)
        kv_o[:, pl.ds(kv_width + group * HEAD_DIM, HEAD_DIM)] = grad_values.astype(BF)
    kv_o.send()
    size = resid.shape[1] // XS
    for out, part in zip(sent_o, x_parts(place)):
        at = pl.ds(pl.multiple_of(part * size, size), size)
        one, two = attended_o[:, at], query_o[:, at]
        out[:, pl.ds(0, size)] = jnp.where(place[0] == 0, one, two)
        out[:, pl.ds(size, size)] = jnp.where(place[0] == 0, two, one)


def x_parts(place):
    s, t = place[2], place[3]
    return [
        a + 3 * b - 2 * a * b for a, b in ((s, t), (1 - s, t), (s, 1 - t), (1 - s, 1 - t))
    ]


def collect(pieces, whole, sems, first):
    rows = pieces[0].shape[0]
    copies = []
    for n, piece in enumerate(pieces):
        copy = pltpu.make_async_copy(
            piece, whole.at[pl.ds(n * rows, rows)], sems.at[first + n]
        )
        copy.start()
        copies.append(copy)
    return copies


def interleave(own, other):
    return [piece for pair in zip(own, other) for piece in pair]


def square_weight_kernel(place, *refs):
    own, other, left = refs[:4], refs[4:8], refs[8:16]
    out, all_grads, all_left, sems = refs[16:]
    size = out.shape[1]
    copies = collect(
        interleave(
            [ref.at[:, pl.ds(0, size)] for ref in own],
            [ref.at[:, pl.ds(size, size)] for ref in other],
        ),
        all_grads, sems, 0,
    )
    copies += collect(left, all_left, sems, 8)
    for copy in copies:
        copy.wait()
    step = 256
    for low in range(0, all_left.shape[1], step):
        at = pl.ds(low, step)
        out[at, :] = t_dot(all_left[:, at], all_grads[...]).astype(BF)


def pack_kernel(place, square, one_own, one_got, two_own, two_got, *refs):
    grads, left = refs[:8], refs[8:16]
    out, all_grads, all_left, total, sems = refs[16:]
    copies = collect(interleave(grads[:4], grads[4:]), all_grads, sems, 0)
    copies += collect(left, all_left, sems, 8)
    size, small = square.shape[1], total.shape[1]
    count, groups, part, _ = out.shape
    row = lax.broadcasted_iota(jnp.int32, (part, small), 0)
    lane = lax.broadcasted_iota(jnp.int32, (part, small), 1)
    short = lane < square.shape[0] // groups - small
    gains = []
    for f in range(groups):
        one, two = one_own[f] + one_got[f], two_own[f] + two_got[f]
        block = jnp.where(row == 0, one[0:1], 0.0)
        block = jnp.where((row == 1) & short, one[1:2], block)
        block = jnp.where(row == 2, two[0:1], block)
        gains.append(jnp.where((row == 3) & short, two[1:2], block).astype(BF))
        for y in range(count):
            out[y, f, :, pl.ds(0, size)] = square[pl.ds((f * count + y) * part, part), :]
    for copy in copies:
        copy.wait()
    total[...] = t_dot(all_left[...], all_grads[...]).astype(BF)
    even = place[0] == 0
    for y in range(count):
        for f in range(groups):
            at = pl.ds((f * count + y) * part, part)
            out[y, f, :, pl.ds(size, small)] = jnp.where(even, gains[f], total[at, :])
        out.send(y + 1)


def sum_kernel(place, parts, out):
    total = parts[0].astype(F32)
    for k in range(1, parts.shape[0]):
        total = total + parts[k].astype(F32)
    total = total.astype(BF)
    for k in range(out.shape[0]):
        out[k] = total


def final_kernel(
    place, own, other, mark, output_o, query_o, key_o, value_o, gain_one_o, gain_two_o
):
    even = place[0] == 0
    part = own.shape[1]
    size = output_o.shape[1] // XS
    small = key_o.shape[1] * 2 // XS
    total = jnp.zeros((8, small), F32)
    for y in range(YLO):
        rows = pl.ds(y * part, part)
        for x in range(XS):
            mine, theirs = own[y * XS + x], other[y * XS + x]
            first = jnp.where(even, mine, theirs).astype(F32)
            second = jnp.where(even, theirs, mine).astype(F32)
            at = pl.ds(x * size, size)
            output_o[rows, at] = first[:, :size]
            query_o[rows, at] = second[:, :size]
            into = key_o if x < XS // 2 else value_o
            into[rows, pl.ds(x % (XS // 2) * small, small)] = second[:, size:]
            if y == 0:
                total = total + first[:8, size:]
    for ref, row in ((gain_one_o, 0), (gain_two_o, 2)):
        ref[:, pl.ds(0, small)] = total[row : row + 1]
        ref[:, pl.ds(small, ref.shape[1] - small)] = total[
            row + 1 : row + 2, : ref.shape[1] - small
        ]


def key_back_kernel(place, parts, cos, sin, pre_o, *sent_o):
    kv_width = parts.shape[-1] // 2
    total = parts[0].astype(F32)
    for k in range(1, parts.shape[0]):
        total = total + parts[k].astype(F32)
    for head in range(2 * KV_HEADS):
        low, high = head * HEAD_DIM, (head + 1) * HEAD_DIM
        piece = total[:, low:high]
        if head < KV_HEADS:
            piece = turn_back(piece, cos[...], sin[...])
        pre_o[:, low:high] = piece.astype(BF)
    size = 2 * kv_width // XS
    for out, part in zip(sent_o, x_parts(place)):
        out[...] = pre_o[:, pl.ds(pl.multiple_of(part * size, size), size)]


def query_back_kernel(place, query, query_w, out):
    out[...] = dot_t(query[...], query_w[...])


def input_kernel(
    place, partial, pre, src, scale_i, gain, kv_w, grad_resid, input_o, gain_o, mark_o
):
    mark_o[...] = jnp.zeros(mark_o.shape, F32)
    grad_normed = partial[...] + dot_t(pre[...], kv_w[...])
    source = src[...].astype(F32)
    scale = scale_i[:, :1]
    put_gain(gain_o, jnp.sum(grad_normed * source * scale, axis=0, keepdims=True))
    send(gain_o)
    weighted = grad_normed * gain[...]
    inner = jnp.sum(weighted * source, axis=-1, keepdims=True)
    input_o[...] = (
        grad_resid[...]
        + scale * weighted
        - source * (scale * scale * scale * inner * (1.0 / source.shape[-1]))
    ).astype(BF)


class Far:
    def __init__(self, value, kind=None, parts=1):
        self.value, self.kind, self.parts = value, kind, parts


class Coming:
    def __init__(self, source, ref, sem):
        self.copy, self.ref, self.waits = pltpu.make_async_copy(source, ref, sem), ref, True
        self.shape = ref.shape
        self.copy.start()

    def now(self):
        if self.waits:
            self.copy.wait()
            self.waits = False
        return self.ref

    def __getitem__(self, index):
        return self.now()[index]

    @property
    def at(self):
        return self.now().at


class Going:
    def __init__(self, ref, target, sems, parts):
        self.ref, self.target, self.shape, self.sent = ref, target, ref.shape, 0
        rows = ref.shape[0] // parts
        self.copies = [
            pltpu.make_async_copy(
                ref.at[pl.ds(n * rows, rows)], target.at[pl.ds(n * rows, rows)], sem
            )
            for n, sem in enumerate(sems)
        ]

    def __getitem__(self, index):
        return self.ref[index]

    def __setitem__(self, index, value):
        self.ref[index] = value

    def send(self, upto=None):
        upto = len(self.copies) if upto is None else upto
        for copy in self.copies[self.sent : upto]:
            copy.start()
        self.sent = max(self.sent, upto)


def send(self):
        if not self.sent:
            self.copy.start()
            self.sent = True


def send(*results):
    for result in results:
        result.send()


def call(kernel, args, outs, scratch=(), micros=0, raw=()):
    outs = [out if isinstance(out, Far) else Far(*out) for out in outs]
    values = [a.value if isinstance(a, Far) else a for a in args]
    far = [i for i, a in enumerate(args) if isinstance(a, Far) and i not in raw]
    count, made = len(args), len(outs)

    def whole(*refs):
        ins, results = list(refs[:count]), refs[count : count + made]
        own = refs[count + made : count + made + len(scratch)]
        rest = refs[count + made + len(scratch) :]
        landing, leaving, sems = rest[: len(far)], rest[len(far) : len(far) + made], rest[-1]
        for n, i in enumerate(far):
            ins[i] = Coming(ins[i], landing[n], sems.at[n])
        going, used = [], len(far)
        for out, ref, target in zip(outs, leaving, results):
            going.append(
                Going(ref, target, [sems.at[used + n] for n in range(out.parts)], out.parts)
            )
            used += out.parts
        kernel(*ins, *going, *own)
        for i in far:
            ins[i].now()
        send(*going)
        for result in going:
            for copy in result.copies:
                copy.wait()

    near = pl.BlockSpec(memory_space=pltpu.VMEM)
    away = pl.BlockSpec(memory_space=pl.ANY)
    specs = [away if isinstance(a, Far) else near for a in args]
    specs[0] = pl.BlockSpec(memory_space=pltpu.SMEM)
    return pl.pallas_call(
        whole,
        out_shape=[jax.ShapeDtypeStruct(out.value, out.kind) for out in outs],
        in_specs=specs,
        out_specs=[away] * made,
        scratch_shapes=[
            *scratch,
            *[pltpu.VMEM(values[i].shape, values[i].dtype) for i in far],
            *[pltpu.VMEM(out.value, out.kind) for out in outs],
            pltpu.SemaphoreType.DMA((len(far) + sum(out.parts for out in outs),)),
        ],
        compiler_params=pltpu.CompilerParams(vmem_limit_bytes=56 * 1024 * 1024),
        cost_estimate=pl.CostEstimate(
            flops=int(micros * 1e9), bytes_accessed=0, transcendentals=0
        ),
    )(*values)


def swap(v):
    return lax.ppermute(v, "core", [(0, 1), (1, 0)])


def swap_y(v):
    return lax.ppermute(v, "ylo", [(0, 1), (1, 0)])


def exchange(v, axis):
    return lax.all_to_all(v, axis, 0, 0, tiled=True)


def copies(v, n):
    return lax.optimization_barrier(jnp.broadcast_to(v[None], (n,) + v.shape))


def tie(*values):
    return lax.optimization_barrier(values)


PAIRS_S = [(0, 1), (1, 0), (2, 3), (3, 2)]
PAIRS_T = [(0, 3), (3, 0), (1, 2), (2, 1)]
PAIRS_ST = [(0, 2), (2, 0), (1, 3), (3, 1)]


def x_bits():
    x = lax.axis_index("x")
    return ((x + 1) // 2) % 2, x // 2


def flip(v, pairs):
    return lax.ppermute(v, "x", pairs)


def body(
    inputs,
    segments,
    first_gain,
    query_matrix,
    key_matrix,
    value_matrix,
    output_matrix,
    second_gain,
    expert_ids,
    gate_values,
    priority,
    gate_weight,
    up_weight,
    down_weight,
    cotangent,
):
    tok = inputs.shape[1]
    width = inputs.shape[2]
    rows = query_matrix.shape[0]
    groups = lax.axis_size("fsdp")
    member = lax.axis_index("fsdp")
    core = lax.axis_index("core")
    even = core == 0
    experts = groups
    capacity = 5 * tok * TOP // (4 * experts)
    slots_all = experts * capacity
    half = width // 2
    kv_width = key_matrix.shape[1]
    length = groups * tok
    quarter = rows // XS
    bit_s, bit_t = x_bits()
    place_at = jnp.stack([core, member * tok, bit_s, bit_t]).astype(jnp.int32)

    def pick(a, b):
        return jnp.where(even, a, b)

    parts = width // kv_width
    kv_rows = rows // parts
    kv_half = pick(key_matrix, value_matrix).reshape(parts, kv_rows, kv_width)
    kv_piece = jnp.concatenate([kv_half[j] for j in range(parts)], axis=1)
    gains = jnp.pad(jnp.stack([first_gain, second_gain]), ((0, 6), (0, width - rows)))
    square_piece = jnp.concatenate(
        [
            lax.dynamic_slice(matrix, (bit * (rows // 2), core * half), (rows // 2, half))
            for matrix, bit in ((query_matrix, bit_s), (output_matrix, bit_t))
        ],
        axis=1,
    )
    kv_piece = jnp.concatenate([kv_piece, gains], axis=0)
    gathered = exchange(copies(kv_piece, groups), "fsdp")
    square_piece = copies(square_piece, groups)
    gathered, square_piece, place_at = tie(gathered, square_piece, place_at)
    squares = exchange(square_piece, "fsdp")

    ids = expert_ids[0].reshape(-1)
    order = priority[0, 0]
    earlier = (order[None, :] < order[:, None]) & (ids[None, :] == ids[:, None])
    slots = jnp.sum(earlier.astype(jnp.int32), axis=1)
    kept = slots < capacity
    expert_list = jnp.arange(experts, dtype=jnp.int32)
    chosen = (ids[:, None] == expert_list[None, :]) & kept[:, None]
    slot_of = jnp.sum(
        jnp.where(chosen, slots[:, None] + 1, 0).reshape(tok, TOP, experts), axis=1
    )
    slot_of = slot_of - 1
    gate_table = jnp.sum(
        jnp.where(chosen, gate_values[0].reshape(-1)[:, None], 0.0).reshape(tok, TOP, experts),
        axis=1,
    )
    slot_list = jnp.arange(capacity, dtype=jnp.int32)
    hits = slot_of.T[:, None, :] == slot_list[None, :, None]
    one_hot = hits.astype(BF).reshape(slots_all, tok)
    one_hot_t = (slot_of[:, :, None] == slot_list[None, None, :]).astype(BF)
    one_hot_t = one_hot_t.reshape(tok, slots_all)
    gate_hot = jnp.where(hits, gate_table.T[:, None, :], 0.0).reshape(slots_all, tok)
    slot_gate = jnp.sum(gate_hot, axis=1, keepdims=True)
    gate_high = gate_hot.astype(BF)
    gate_low = (gate_hot - gate_high.astype(F32)).astype(BF)
    send_grad = (dot(one_hot, cotangent[0]) * slot_gate).astype(BF)

    cosine, sine = angles(member * tok + jnp.arange(tok, dtype=jnp.int32))
    segment_row = segments[0]
    query_segments = lax.dynamic_slice_in_dim(segment_row, member * tok, tok)
    key_place = jnp.arange(length, dtype=jnp.int32)[:, None]
    query_place = (member * tok + jnp.arange(tok, dtype=jnp.int32))[None, :]
    allowed = (
        (key_place <= query_place)
        & (query_place - key_place < WINDOW)
        & (segment_row[:, None] == query_segments[None, :])
    )
    bias = jnp.where(allowed, 0.0, NEGATIVE).astype(F32)
    bias = jnp.concatenate([bias, bias], axis=1)
    gathered, cosine, sine = tie(gathered, cosine, sine)
    kv_raw = gathered[:, :kv_rows]
    gain_one = gathered[:, kv_rows, :rows].reshape(1, width).astype(F32)
    gain_two = gathered[:, kv_rows + 1, :rows].reshape(1, width).astype(F32)
    kv_raw_other = swap(kv_raw)

    square = (width, width)
    normed, scale_one, kv_send, kv_weight = call(
        key_kernel,
        [place_at, Far(inputs[0]), gain_one, Far(kv_raw), Far(kv_raw_other), cosine, sine],
        [((tok, width), BF), ((tok, HEAD_DIM), F32), ((groups, tok, 2 * kv_width), BF),
         ((width, 2 * kv_width), BF)],
    )
    kv_send, squares, one_hot_t, gate_high, gate_low, send_grad, bias = tie(
        kv_send, squares, one_hot_t, gate_high, gate_low, send_grad, bias
    )
    q_own, o_own = squares[..., :half], squares[..., half:]
    kv_all = exchange(kv_send, "fsdp").reshape(length, 2 * kv_width)
    q_got, o_got = flip(q_own, PAIRS_S), flip(o_own, PAIRS_T)
    send_grad, kv_all = tie(send_grad, kv_all)
    arrived_grad = exchange(send_grad, "fsdp")
    far_pieces = [
        Far(v)
        for v in (q_own, q_got, swap(q_own), swap(q_got), o_own, o_got, swap(o_own), swap(o_got))
    ]
    weight_parts = (groups, rows, width)
    (query_weight, output_weight, query_rot, mixed, probs, residual, scale_two,
     send_rows) = call(
        front_kernel,
        [place_at, Far(normed), Far(kv_all), Far(bias), Far(inputs[0]), gain_two, Far(one_hot_t),
         cosine, sine, *far_pieces],
        [(weight_parts, BF), (weight_parts, BF), ((tok, width), BF), ((tok, width), BF),
         ((HEADS // 2, length, 2 * tok), BF), ((tok, width), F32), ((tok, HEAD_DIM), F32),
         ((slots_all, width), BF)],
        [pltpu.SemaphoreType.DMA((8,))],
        raw=range(9, 17),
    )
    query_weight = query_weight.reshape(square)
    output_weight = output_weight.reshape(square)

    send_rows, arrived_grad = tie(send_rows, arrived_grad)
    arrived = exchange(send_rows, "fsdp")

    left_a = pick(mixed, normed)
    left_b = swap(pick(normed, mixed))
    left_one_a, left_two_a = flip(left_a, PAIRS_S), flip(left_a, PAIRS_T)
    left_one_b, left_two_b = flip(left_b, PAIRS_T), flip(left_b, PAIRS_S)
    upper_other = swap(lax.dynamic_slice_in_dim(arrived_grad, (1 - core) * half, half, 1))
    grad_hidden = dot_t(arrived_grad, down_weight[0])
    arrived, grad_hidden, upper_other, left_one_a, left_two_a, left_one_b, left_two_b = tie(
        arrived, grad_hidden, upper_other, left_one_a, left_two_a, left_one_b, left_two_b
    )
    left_three_a, left_three_b = flip(left_one_a, PAIRS_T), flip(left_one_b, PAIRS_S)
    arrived_other = swap(arrived)
    hidden, own_pre, sent_pre, grad_rows = call(
        expert_kernel,
        [place_at, Far(arrived), Far(grad_hidden), gate_weight[0], up_weight[0]],
        [Far((slots_all, half), BF, 2)] * 3 + [Far((slots_all, width), BF, 2)],
    )
    back_rows = exchange(grad_rows, "fsdp")
    expert_rows = width + half

    e_part = (2, expert_rows // 8, half)
    e_keep_a, e_send_a, e_keep_b, e_send_b = call(
        expert_weight_kernel,
        [place_at] + [Far(v) for v in (arrived, arrived_other, own_pre, swap(sent_pre), hidden,
                                       swap(hidden), arrived_grad, upper_other)],
        [(e_part, BF)] * 4,
        [pltpu.VMEM((expert_rows, half), BF)],
    )
    expert_out = dot(hidden, down_weight[0]).astype(BF)
    e_got_a, e_got_b = flip(e_send_a, PAIRS_S), flip(e_send_b, PAIRS_T)
    back_rows, expert_out, e_keep_a, e_keep_b, left_three_a, left_three_b = tie(
        back_rows, expert_out, e_keep_a, e_keep_b, left_three_a, left_three_b
    )
    left = [left_a, left_b, left_one_a, left_two_b, left_two_a, left_one_b, left_three_a,
            left_three_b]

    grad_residual, grad_attended, gain_two_part, grad_query_pre, kv_back, *qo_sent = call(
        back_kernel,
        [place_at, Far(back_rows), Far(one_hot_t), Far(residual), Far(scale_two), gain_two,
         Far(cotangent[0]), Far(output_weight), Far(probs), Far(kv_all), Far(query_rot), cosine,
         sine],
        [((tok, width), F32), ((tok, width), BF), ((groups, 2, HEAD_DIM), F32), ((tok, width), BF),
         ((length, 2 * kv_width), BF)] + [((tok, half), BF)] * XS,
    )
    kv_got = exchange(kv_back, "fsdp")
    e_keep_a, e_send_a, e_keep_b, e_send_b = call(
        expert_step_kernel,
        [place_at, Far(e_keep_a), Far(e_got_a), Far(e_keep_b), Far(e_got_b)],
        [(e_part[1:], BF)] * 4,
    )
    e_got_a, e_got_b = flip(e_send_a, PAIRS_T), flip(e_send_b, PAIRS_S)
    qo_set = fan(qo_sent)
    partial = call(
        query_back_kernel,
        [place_at, Far(grad_query_pre), Far(query_weight)],
        [((tok, width), F32)],
    )[0]
    qo_set[1], qo_set[2], qo_set[3], partial = tie(qo_set[1], qo_set[2], qo_set[3], partial)
    whole = 2 * XS * tok
    square_grad = call(
        square_weight_kernel,
        [place_at] + [Far(v) for v in (*qo_set, *[swap(v) for v in qo_set], *left)],
        [((width, width // XS), BF)],
        [pltpu.VMEM((whole, width // XS), BF), pltpu.VMEM((whole, width), BF),
         pltpu.SemaphoreType.DMA((16,))],
        raw=range(1, 17),
    )[0]
    kv_got, expert_out, square_grad = tie(kv_got, expert_out, square_grad)
    returned = exchange(expert_out, "fsdp")
    grad_kv_pre, *kv_sent = call(
        key_back_kernel,
        [place_at, Far(kv_got.reshape(groups, tok, 2 * kv_width)), cosine, sine],
        [((tok, 2 * kv_width), BF)] + [((tok, 2 * kv_width // XS), BF)] * XS,
    )
    kv_set = fan(kv_sent)
    input_grad, gain_one_part, mark = call(
        input_kernel,
        [place_at, Far(partial), Far(grad_kv_pre), Far(inputs[0]), Far(scale_one), gain_one,
         Far(kv_weight), Far(grad_residual)],
        [((tok, width), BF), ((groups, 2, HEAD_DIM), F32), ((8, HEAD_DIM), F32)],
        micros=6,
    )

    kv_set[1], kv_set[2], kv_set[3], mark = tie(kv_set[1], kv_set[2], kv_set[3], mark)
    e_got_a, e_got_b, mark = tie(e_got_a, e_got_b, mark)
    e_sum = call(
        expert_end_kernel,
        [place_at, Far(e_keep_a), Far(e_got_a), Far(e_keep_b), Far(e_got_b), mark],
        [(e_part, BF)],
    )[0]
    e_other_y = swap_y(e_sum)
    e_zero_a, e_zero_b = call(pair_kernel, [place_at, Far(e_sum), Far(e_other_y)], [(e_part[1:], BF)] * 2)
    e_one_a, e_one_b = flip(e_zero_a, PAIRS_T), flip(e_zero_b, PAIRS_S)
    e_two_a, e_two_b = flip(e_zero_a, PAIRS_S), flip(e_zero_b, PAIRS_T)

    spare = 2 * kv_width // XS
    part = rows // YLO
    packed_width = width // XS + spare
    packed = call(
        pack_kernel,
        [place_at]
        + [Far(v) for v in (square_grad, gain_one_part, swap(gain_one_part), gain_two_part,
                            swap(gain_two_part))]
        + [Far(v) for v in (*kv_set, *[swap(v) for v in kv_set], *left)],
        [Far((YLO, groups, part, packed_width), BF, 2)],
        [pltpu.VMEM((whole, spare), BF), pltpu.VMEM((whole, width), BF),
         pltpu.VMEM((width, spare), BF), pltpu.SemaphoreType.DMA((16,))],
        raw=range(6, 22),
    )[0]
    packed, returned = tie(packed, returned)
    packed = exchange(packed.reshape(YLO * groups, part, packed_width), ("ylo", "fsdp"))
    mixture = t_dot(gate_high, returned) + t_dot(gate_low, returned)
    outputs = (residual + mixture).astype(BF)
    packed, outputs = tie(packed, outputs)
    packed = call(sum_kernel, [place_at, Far(packed)], [((YLO * XS, part, packed_width), BF)])[0]
    spreaded = exchange(packed, ("ylo", "x"))
    most = [e_zero_a, e_zero_b, e_one_a, e_one_b, e_two_a, e_two_b]
    *e_grads, most_mark = expert_outputs(
        expert_most_kernel, [place_at, *most, *[swap(v) for v in most]], [], e_part[1:], width, half
    )
    e_one_a, e_one_b, packed = tie(e_one_a, e_one_b, packed)
    e_three_a, e_three_b = flip(e_one_a, PAIRS_S), flip(e_one_b, PAIRS_T)
    e_three_a, e_three_b, most_mark = tie(e_three_a, e_three_b, most_mark)
    grad_gate, grad_up, grad_down, e_mark = expert_outputs(
        expert_rest_kernel,
        [place_at, e_three_a, e_three_b, swap(e_three_a), swap(e_three_b), most_mark,
         packed[0, :16, :HEAD_DIM]],
        e_grads,
        e_part[1:],
        width,
        half,
    )
    spreaded, e_mark = tie(spreaded, e_mark)
    grad_output_w, grad_query_w, grad_key_w, grad_value_w, grad_one, grad_two = call(
        final_kernel,
        [place_at, Far(spreaded), Far(swap(spreaded)), e_mark],
        [((rows, width), F32), ((rows, width), F32), ((rows, kv_width), F32),
         ((rows, kv_width), F32), ((1, rows), F32), ((1, rows), F32)],
    )
    return (
        outputs[None],
        input_grad[None],
        grad_one[0],
        grad_query_w,
        grad_key_w,
        grad_value_w,
        grad_output_w,
        grad_two[0],
        grad_gate[None],
        grad_up[None],
        grad_down[None],
    )


def solution(mesh):
    shape = mesh.devices.shape
    fine = Mesh(
        mesh.devices.reshape(YLO, XS, CORES, shape[1]), ("ylo", "x", "core", "fsdp")
    )
    return jax.shard_map(
        body,
        mesh=fine,
        in_specs=(
            P(REP, "fsdp", None),
            P(REP, None),
            P("fsdp"),
            P("fsdp", None),
            P("fsdp", None),
            P("fsdp", None),
            P("fsdp", None),
            P("fsdp"),
            P(REP, "fsdp", None),
            P(REP, "fsdp", None),
            P(REP, "fsdp", None),
            P("fsdp", None, None),
            P("fsdp", None, None),
            P("fsdp", None, None),
            P(REP, "fsdp", None),
        ),
        out_specs=(
            P(REP, "fsdp", None),
            P(REP, "fsdp", None),
            P("fsdp"),
            P("fsdp", None),
            P("fsdp", None),
            P("fsdp", None),
            P("fsdp", None),
            P("fsdp"),
            P("fsdp", None, None),
            P("fsdp", None, None),
            P("fsdp", None, None),
        ),
        check_vma=False,
    )
```

```python
import jax
import jax.numpy as jnp
from jax import lax
from jax.experimental import pallas as pl
from jax.experimental.pallas import tpu as pltpu
from jax.sharding import Mesh
from jax.sharding import PartitionSpec as P

HEADS = 12
KV_HEADS = 2
HEAD_DIM = 128
TOP = 4
WINDOW = 1024

EPSILON = 1e-06
THETA = 10000.0
NEGATIVE = -1e30

YLO, XS, CORES = 2, 4, 2
REP = ("ylo", "x", "core")
BF = jnp.bfloat16
F32 = jnp.float32


def angles(positions):
    half_width = HEAD_DIM // 2
    frequency = THETA ** (-(jnp.arange(half_width, dtype=F32) * 2.0) / HEAD_DIM)
    phase = positions.astype(F32)[:, None] * frequency[None, :]
    cosine, sine = jnp.cos(phase), jnp.sin(phase)
    return (
        jnp.concatenate([cosine, cosine], axis=1),
        jnp.concatenate([-sine, sine], axis=1),
    )


def dot(a, b):
    return jnp.dot(a, b, preferred_element_type=F32)


def dot_t(a, b):
    return lax.dot_general(a, b, (((1,), (1,)), ((), ())), preferred_element_type=F32)


def t_dot(a, b):
    return lax.dot_general(a, b, (((0,), (0,)), ((), ())), preferred_element_type=F32)


def fan(pieces):
    return [
        pieces[0],
        flip(pieces[1], PAIRS_S),
        flip(pieces[2], PAIRS_T),
        flip(pieces[3], PAIRS_ST),
    ]


def add(a, b):
    return (a.astype(F32) + b.astype(F32)).astype(BF)


def turn(piece, cosine, sine):
    return piece * cosine + pltpu.roll(piece, HEAD_DIM // 2, 1) * sine


def turn_back(piece, cosine, sine):
    return piece * cosine - pltpu.roll(piece, HEAD_DIM // 2, 1) * sine


def stacked(ref, pair):
    low = 2 * pair * HEAD_DIM
    return jnp.concatenate(
        [ref[:, pl.ds(low, HEAD_DIM)], ref[:, pl.ds(low + HEAD_DIM, HEAD_DIM)]], axis=0
    )


def unstack(ref, pair, value):
    low, rows = 2 * pair * HEAD_DIM, value.shape[0] // 2
    ref[:, pl.ds(low, HEAD_DIM)] = value[:rows]
    ref[:, pl.ds(low + HEAD_DIM, HEAD_DIM)] = value[rows:]


def put_gain(out, total):
    groups, _, lanes = out.shape
    size = total.shape[1] // groups
    for f in range(groups):
        row = total[:, f * size : (f + 1) * size]
        out[f, 0:1, :] = row[:, :lanes]
        out[f, 1:2, pl.ds(0, size - lanes)] = row[:, lanes:]


def key_kernel(place, src, gain, raw_own, raw_other, cos, sin, normed_o, scale_o, send_o, weight_o):
    core = place[0]
    groups, kv_rows, width = raw_own.shape
    kv_width = weight_o.shape[1] // 2
    parts = width // kv_width
    source = src[...].astype(F32)
    scale = lax.rsqrt(jnp.mean(source * source, axis=-1, keepdims=True) + EPSILON)
    scale_o[...] = jnp.broadcast_to(scale, scale_o.shape)
    normed = (source * scale * gain[...]).astype(BF)
    normed_o[...] = normed
    send(scale_o, normed_o)
    for raw, which in ((raw_own, core), (raw_other, 1 - core)):
        at = pl.ds(pl.multiple_of(which * kv_width, kv_width), kv_width)
        for f in range(groups):
            for j in range(parts):
                weight_o[pl.ds((f * parts + j) * kv_rows, kv_rows), at] = raw[
                    f, :, pl.ds(j * kv_width, kv_width)
                ]
    send(weight_o)
    pre = dot(normed, weight_o[...])
    for head in range(2 * KV_HEADS):
        low, high = head * HEAD_DIM, (head + 1) * HEAD_DIM
        piece = pre[:, low:high]
        if head < KV_HEADS:
            piece = turn(piece, cos[...], sin[...])
        for f in range(groups):
            send_o[f, :, low:high] = piece.astype(BF)


def front_kernel(place, normed, kv, bias, src, gain, hot_t, cos, sin, *refs):
    pieces = refs[:8]
    query_w, output_w, query_o, mixed_o, probs_o, resid_o, scale_o, send_o, sems = refs[8:]
    core, s, t = place[0], place[2], place[3]
    _, rows, half = pieces[0].shape
    copies = []
    for n, block in enumerate(pieces):
        weight, bit = ((query_w, s), (output_w, t))[n // 4]
        which = core if n % 4 < 2 else 1 - core
        part = bit if n % 2 == 0 else 1 - bit
        at = pl.ds(pl.multiple_of(part * rows, rows), rows)
        cols = pl.ds(pl.multiple_of(which * half, half), half)
        copy = pltpu.make_async_copy(block, weight.ref.at[:, at, cols], sems.at[n])
        copy.start()
        copies.append(copy)
    width = 2 * half
    for copy in copies[:4]:
        copy.wait()
    query_w.send()
    pre = dot(normed[...], query_w[...].reshape(width, width))
    for head in range(HEADS):
        low, high = head * HEAD_DIM, (head + 1) * HEAD_DIM
        query_o[:, low:high] = turn(pre[:, low:high], cos[...], sin[...]).astype(BF)
    query_o.send()
    kv_width = kv.shape[1] // 2
    for pair in range(HEADS // 2):
        group = 2 * pair // (HEADS // KV_HEADS)
        keys = kv[:, pl.ds(group * HEAD_DIM, HEAD_DIM)]
        values = kv[:, pl.ds(kv_width + group * HEAD_DIM, HEAD_DIM)]
        scores = dot_t(keys, stacked(query_o, pair)) * HEAD_DIM ** (-0.5) + bias[...]
        weights = jnp.exp(scores - jnp.max(scores, axis=0, keepdims=True))
        probs = (weights * (1.0 / jnp.sum(weights, axis=0, keepdims=True))).astype(BF)
        probs_o[pair] = probs
        unstack(mixed_o, pair, t_dot(probs, values).astype(BF))
    send(probs_o, mixed_o)
    for copy in copies[4:]:
        copy.wait()
    output_w.send()
    resid = src[...].astype(F32) + dot(mixed_o[...], output_w[...].reshape(width, width))
    resid_o[...] = resid
    resid_o.send()
    scale = lax.rsqrt(jnp.mean(resid * resid, axis=-1, keepdims=True) + EPSILON)
    scale_o[...] = jnp.broadcast_to(scale, scale_o.shape)
    second = (resid * scale * gain[...]).astype(BF)
    send_o[...] = t_dot(hot_t[...], second).astype(BF)


def expert_kernel(place, rows, grad_hidden, gate_w, up_w, hidden_o, own_o, sent_o, back_o):
    core = place[0]
    count = rows.shape[0]
    step = count // 2
    for n, low in enumerate(range(0, count, step)):
        at = pl.ds(low, step)
        block = rows.part(n)[at, :]
        gate = dot(block, gate_w[...])
        up = dot(block, up_w[...])
        sigmoid = 1.0 / (1.0 + jnp.exp(-gate))
        silu = gate * sigmoid
        hidden_o[at, :] = (silu * up).astype(BF)
        grad = grad_hidden.part(n)[at, :]
        grad_gate = (grad * up * (sigmoid * (1.0 + gate * (1.0 - sigmoid)))).astype(BF)
        grad_up = (grad * silu).astype(BF)
        own_o[at, :] = jnp.where(core == 0, grad_gate, grad_up)
        sent_o[at, :] = jnp.where(core == 0, grad_up, grad_gate)
        for result in (sent_o, hidden_o, own_o):
            result.send(n + 1)
        back_o[at, :] = (dot_t(grad_gate, gate_w[...]) + dot_t(grad_up, up_w[...])).astype(BF)
        back_o.send(n + 1)


def expert_weight_kernel(
    place, rows, rows_got, pre, pre_got, hidden, hidden_got, arrived, upper_got,
    keep_a, send_a, keep_b, send_b, total,
):
    s, t = place[2], place[3]
    width, half = rows.shape[1], hidden.shape[1]
    upper = arrived[:, pl.ds(pl.multiple_of(place[0] * half, half), half)]
    step = 256
    for low in range(0, width, step):
        at = pl.ds(low, step)
        total[at, :] = (t_dot(rows[:, at], pre[...]) + t_dot(rows_got[:, at], pre_got[...])).astype(
            BF
        )
    for low in range(0, half, step):
        at = pl.ds(low, step)
        total[pl.ds(width + low, step), :] = (
            t_dot(hidden[:, at], upper) + t_dot(hidden_got[:, at], upper_got[...])
        ).astype(BF)
    big, small = width // 8, half // 8
    for out, side, spots in (
        (send_a, 0, ((1 - s, 0), (1 - s, 1))),
        (send_b, 1, ((0, 1 - t), (1, 1 - t))),
        (keep_a, 0, ((s, 0), (s, 1))),
        (keep_b, 1, ((0, t), (1, t))),
    ):
        for j, (row_s, row_t) in enumerate(spots):
            piece = side * 4 + 2 * row_s + row_t
            out[j, pl.ds(0, big), :] = total[pl.ds(pl.multiple_of(piece * big, big), big), :]
            start = pl.multiple_of(width + piece * small, small)
            out[j, pl.ds(big, small), :] = total[pl.ds(start, small), :]
        out.send()


def expert_step_kernel(place, keep_a, got_a, keep_b, got_b, keep_ao, send_ao, keep_bo, send_bo):
    s, t = place[2], place[3]
    send_ao[...] = add(keep_a[1 - t], got_a[1 - t])
    send_ao.send()
    send_bo[...] = add(keep_b[1 - s], got_b[1 - s])
    send_bo.send()
    keep_ao[...] = add(keep_a[t], got_a[t])
    keep_ao.send()
    keep_bo[...] = add(keep_b[s], got_b[s])


def expert_end_kernel(place, keep_a, got_a, keep_b, got_b, mark, out):
    out[0] = add(keep_a[...], got_a[...])
    out[1] = add(keep_b[...], got_b[...])


def pair_kernel(place, a, b, one, two):
    one[...] = add(a[0], b[0])
    one.send()
    two[...] = add(a[1], b[1])


def place_experts(place, blocks, outs, stage, sems):
    core = place[0]
    gate_o, up_o, down_o = outs
    half = stage.shape[2]
    big = gate_o.shape[0] // 8
    small = stage.shape[1] - big
    moves = []
    for n, (side, row_s, row_t, which, block) in enumerate(blocks):
        stage[n] = block[...].astype(F32)
        piece = side * 4 + 2 * row_s + row_t
        at = pl.ds(pl.multiple_of(piece * big, big), big)
        cols = pl.ds(pl.multiple_of(which * half, half), half)
        to_gate = pltpu.make_async_copy(stage.at[n, pl.ds(0, big)], gate_o.at[at], sems.at[2 * n])
        to_up = pltpu.make_async_copy(stage.at[n, pl.ds(0, big)], up_o.at[at], sems.at[2 * n])
        to_down = pltpu.make_async_copy(
            stage.at[n, pl.ds(big, small)],
            down_o.at[pl.ds(pl.multiple_of(piece * small, small), small), cols],
            sems.at[2 * n + 1],
        )

        @pl.when(which == 0)
        def _():
            to_gate.start()

        @pl.when(which == 1)
        def _():
            to_up.start()

        to_down.start()
        moves.append((which, to_gate, to_up, to_down))
    for which, to_gate, to_up, to_down in moves:

        @pl.when(which == 0)
        def _():
            to_gate.wait()

        @pl.when(which == 1)
        def _():
            to_up.wait()

        to_down.wait()


def expert_most_kernel(place, *refs):
    core, s, t = place[0], place[2], place[3]
    gate_o, up_o, down_o, mark_o, stage, sems = refs[12:]
    mark_o[...] = jnp.zeros(mark_o.shape, F32)
    blocks = []
    for first, which in ((0, core), (6, 1 - core)):
        zero_a, zero_b, one_a, one_b, two_a, two_b = refs[first : first + 6]
        blocks += [
            (0, s, t, which, zero_a),
            (1, s, t, which, zero_b),
            (0, s, 1 - t, which, one_a),
            (1, 1 - s, t, which, one_b),
            (0, 1 - s, t, which, two_a),
            (1, s, 1 - t, which, two_b),
        ]
    place_experts(place, blocks, (gate_o, up_o, down_o), stage, sems)


def expert_rest_kernel(place, *refs):
    core, s, t = place[0], place[2], place[3]
    gate_o, up_o, down_o, mark_o, stage, sems = refs[9:]
    mark_o[...] = jnp.zeros(mark_o.shape, F32)
    blocks = []
    for first, which in ((0, core), (2, 1 - core)):
        for side in range(2):
            blocks.append((side, 1 - s, 1 - t, which, refs[first + side]))
    place_experts(place, blocks, (gate_o, up_o, down_o), stage, sems)


def expert_outputs(kernel, args, before, part, width, half):
    near = pl.BlockSpec(memory_space=pltpu.VMEM)
    away = pl.BlockSpec(memory_space=pl.ANY)
    shapes = [
        jax.ShapeDtypeStruct(shape, F32)
        for shape in ((width, half), (width, half), (half, width), (8, HEAD_DIM))
    ]
    blocks = 12 if not before else 4
    return pl.pallas_call(
        kernel,
        out_shape=shapes,
        in_specs=[pl.BlockSpec(memory_space=pltpu.SMEM)]
        + [near] * (len(args) - 1)
        + [away] * len(before),
        out_specs=[away] * 3 + [near],
        scratch_shapes=[
            pltpu.VMEM((blocks,) + part, F32),
            pltpu.SemaphoreType.DMA((2 * blocks,)),
        ],
        input_output_aliases={len(args) + n: n for n in range(len(before))},
        compiler_params=pltpu.CompilerParams(vmem_limit_bytes=56 * 1024 * 1024),
        cost_estimate=pl.CostEstimate(flops=0, bytes_accessed=0, transcendentals=0),
    )(*args, *before)


def back_kernel(
    place, back, hot_t, resid_i, scale_i, gain, cot, weight, probs_i, kv, q, cos, sin,
    grad_resid_o, attended_o, gain_o, query_o, kv_o, *sent_o,
):
    kv_width = kv.shape[1] // 2
    resid = resid_i[...]
    scale = scale_i[:, :1]
    grad_second = dot(hot_t[...], back[...])
    weighted = grad_second * gain[...]
    inner = jnp.sum(weighted * resid, axis=-1, keepdims=True)
    grad_resid = (
        cot[...].astype(F32)
        + scale * weighted
        - resid * (scale * scale * scale * inner * (1.0 / resid.shape[-1]))
    )
    put_gain(gain_o, jnp.sum(grad_second * resid * scale, axis=0, keepdims=True))
    grad_resid_o[...] = grad_resid
    grad_resid_o.send()
    attended = grad_resid.astype(BF)
    attended_o[...] = attended
    grad_mixed = dot_t(attended, weight[...]).astype(BF)
    pairs = HEADS // KV_HEADS // 2
    rows = resid.shape[0]
    for group in range(KV_HEADS):
        keys = kv[:, pl.ds(group * HEAD_DIM, HEAD_DIM)]
        values = kv[:, pl.ds(kv_width + group * HEAD_DIM, HEAD_DIM)]
        grad_keys = jnp.zeros(keys.shape, F32)
        grad_values = jnp.zeros(keys.shape, F32)
        for pair in range(group * pairs, (group + 1) * pairs):
            low, high = 2 * pair * HEAD_DIM, (2 * pair + 1) * HEAD_DIM
            upper = jnp.concatenate(
                [grad_mixed[:, low:high], grad_mixed[:, high : high + HEAD_DIM]], axis=0
            )
            probs = probs_i[pair]
            wide = probs.astype(F32)
            grad_probs = dot_t(values, upper)
            total = jnp.sum(wide * grad_probs, axis=0, keepdims=True)
            grad_scores = (wide * (grad_probs - total)).astype(BF)
            grad_values = grad_values + dot(probs, upper)
            grad_keys = grad_keys + dot(grad_scores, stacked(q, pair))
            grad_query = t_dot(grad_scores, keys) * HEAD_DIM ** (-0.5)
            for at, part in ((low, grad_query[:rows]), (high, grad_query[rows:])):
                turned = turn_back(part, cos[...], sin[...])
                query_o[:, pl.ds(at, HEAD_DIM)] = turned.astype(BF)
        at = pl.ds(group * HEAD_DIM, HEAD_DIM)
        kv_o[:, at] = (grad_keys * HEAD_DIM ** (-0.5)).astype(BF)
        kv_o[:, pl.ds(kv_width + group * HEAD_DIM, HEAD_DIM)] = grad_values.astype(BF)
    kv_o.send()
    size = resid.shape[1] // XS
    for out, part in zip(sent_o, x_parts(place)):
        at = pl.ds(pl.multiple_of(part * size, size), size)
        one, two = attended_o[:, at], query_o[:, at]
        out[:, pl.ds(0, size)] = jnp.where(place[0] == 0, one, two)
        out[:, pl.ds(size, size)] = jnp.where(place[0] == 0, two, one)


def x_parts(place):
    s, t = place[2], place[3]
    return [
        a + 3 * b - 2 * a * b for a, b in ((s, t), (1 - s, t), (s, 1 - t), (1 - s, 1 - t))
    ]


def collect(pieces, whole, sems, first):
    rows = pieces[0].shape[0]
    copies = []
    for n, piece in enumerate(pieces):
        copy = pltpu.make_async_copy(
            piece, whole.at[pl.ds(n * rows, rows)], sems.at[first + n]
        )
        copy.start()
        copies.append(copy)
    return copies


def interleave(own, other):
    return [piece for pair in zip(own, other) for piece in pair]


def square_weight_kernel(place, *refs):
    own, other, left = refs[:4], refs[4:8], refs[8:16]
    out, all_grads, all_left, sems = refs[16:]
    size = out.shape[1]
    copies = collect(
        interleave(
            [ref.at[:, pl.ds(0, size)] for ref in own],
            [ref.at[:, pl.ds(size, size)] for ref in other],
        ),
        all_grads, sems, 0,
    )
    copies += collect(left, all_left, sems, 8)
    for copy in copies:
        copy.wait()
    step = 256
    for low in range(0, all_left.shape[1], step):
        at = pl.ds(low, step)
        out[at, :] = t_dot(all_left[:, at], all_grads[...]).astype(BF)


def pack_kernel(place, square, one_own, one_got, two_own, two_got, *refs):
    grads, left = refs[:8], refs[8:16]
    out, all_grads, all_left, total, sems = refs[16:]
    copies = collect(interleave(grads[:4], grads[4:]), all_grads, sems, 0)
    copies += collect(left, all_left, sems, 8)
    size, small = square.shape[1], total.shape[1]
    count, groups, part, _ = out.shape
    row = lax.broadcasted_iota(jnp.int32, (part, small), 0)
    lane = lax.broadcasted_iota(jnp.int32, (part, small), 1)
    short = lane < square.shape[0] // groups - small
    gains = []
    for f in range(groups):
        one, two = one_own[f] + one_got[f], two_own[f] + two_got[f]
        block = jnp.where(row == 0, one[0:1], 0.0)
        block = jnp.where((row == 1) & short, one[1:2], block)
        block = jnp.where(row == 2, two[0:1], block)
        gains.append(jnp.where((row == 3) & short, two[1:2], block).astype(BF))
        for y in range(count):
            out[y, f, :, pl.ds(0, size)] = square[pl.ds((f * count + y) * part, part), :]
    for copy in copies:
        copy.wait()
    total[...] = t_dot(all_grads[...], all_left[...]).T.astype(BF)
    even = place[0] == 0
    for y in range(count):
        for f in range(groups):
            at = pl.ds((f * count + y) * part, part)
            out[y, f, :, pl.ds(size, small)] = jnp.where(even, gains[f], total[at, :])
        out.send(y + 1)


def sum_parts(parts):
    half = parts.shape[0] // 2
    total = parts.part(0)[0].astype(F32)
    for k in range(1, 2 * half):
        total = total + parts.part(k // half)[k].astype(F32)
    return total


def sum_kernel(place, parts, out):
    total = sum_parts(parts)
    total = total.astype(BF)
    for k in range(out.shape[0]):
        out[k] = total


def final_kernel(
    place, own, other, mark, output_o, query_o, key_o, value_o, gain_one_o, gain_two_o
):
    even = place[0] == 0
    part = own.shape[1]
    size = output_o.shape[1] // XS
    small = key_o.shape[1] * 2 // XS
    total = jnp.zeros((8, small), F32)
    for y in range(YLO):
        rows = pl.ds(y * part, part)
        for x in range(XS):
            mine, theirs = own[y * XS + x], other[y * XS + x]
            first = jnp.where(even, mine, theirs).astype(F32)
            second = jnp.where(even, theirs, mine).astype(F32)
            at = pl.ds(x * size, size)
            output_o[rows, at] = first[:, :size]
            query_o[rows, at] = second[:, :size]
            into = key_o if x < XS // 2 else value_o
            into[rows, pl.ds(x % (XS // 2) * small, small)] = second[:, size:]
            if y == 0:
                total = total + first[:8, size:]
    for ref, row in ((gain_one_o, 0), (gain_two_o, 2)):
        ref[:, pl.ds(0, small)] = total[row : row + 1]
        ref[:, pl.ds(small, ref.shape[1] - small)] = total[
            row + 1 : row + 2, : ref.shape[1] - small
        ]


def key_back_kernel(place, parts, cos, sin, pre_o, *sent_o):
    kv_width = parts.shape[-1] // 2
    total = sum_parts(parts)
    for head in range(2 * KV_HEADS):
        low, high = head * HEAD_DIM, (head + 1) * HEAD_DIM
        piece = total[:, low:high]
        if head < KV_HEADS:
            piece = turn_back(piece, cos[...], sin[...])
        pre_o[:, low:high] = piece.astype(BF)
    size = 2 * kv_width // XS
    for out, part in zip(sent_o, x_parts(place)):
        out[...] = pre_o[:, pl.ds(pl.multiple_of(part * size, size), size)]


def query_back_kernel(place, query, query_w, out):
    out[...] = dot_t(query[...], query_w[...])


def input_kernel(
    place, partial, pre, src, scale_i, gain, kv_w, grad_resid, input_o, gain_o, mark_o
):
    mark_o[...] = jnp.zeros(mark_o.shape, F32)
    grad_normed = partial[...] + dot_t(pre[...], kv_w[...])
    source = src[...].astype(F32)
    scale = scale_i[:, :1]
    put_gain(gain_o, jnp.sum(grad_normed * source * scale, axis=0, keepdims=True))
    send(gain_o)
    weighted = grad_normed * gain[...]
    inner = jnp.sum(weighted * source, axis=-1, keepdims=True)
    input_o[...] = (
        grad_resid[...]
        + scale * weighted
        - source * (scale * scale * scale * inner * (1.0 / source.shape[-1]))
    ).astype(BF)


class Far:
    def __init__(self, value, kind=None, parts=1):
        self.value, self.kind, self.parts = value, kind, parts


class Coming:
    def __init__(self, source, ref, sems):
        self.ref, self.shape, self.left = ref, ref.shape, 0
        rows = ref.shape[0] // len(sems)
        self.copies = [
            pltpu.make_async_copy(
                source.at[pl.ds(n * rows, rows)], ref.at[pl.ds(n * rows, rows)], sem
            )
            for n, sem in enumerate(sems)
        ]
        for copy in self.copies:
            copy.start()

    def part(self, n):
        for copy in self.copies[self.left : n + 1]:
            copy.wait()
        self.left = max(self.left, n + 1)
        return self.ref

    def now(self):
        return self.part(len(self.copies) - 1)

    def __getitem__(self, index):
        return self.now()[index]

    @property
    def at(self):
        return self.now().at


class Going:
    def __init__(self, ref, target, sems, parts):
        self.ref, self.target, self.shape, self.sent = ref, target, ref.shape, 0
        rows = ref.shape[0] // parts
        self.copies = [
            pltpu.make_async_copy(
                ref.at[pl.ds(n * rows, rows)], target.at[pl.ds(n * rows, rows)], sem
            )
            for n, sem in enumerate(sems)
        ]

    def __getitem__(self, index):
        return self.ref[index]

    def __setitem__(self, index, value):
        self.ref[index] = value

    def send(self, upto=None):
        upto = len(self.copies) if upto is None else upto
        for copy in self.copies[self.sent : upto]:
            copy.start()
        self.sent = max(self.sent, upto)


def send(self):
        if not self.sent:
            self.copy.start()
            self.sent = True


def send(*results):
    for result in results:
        result.send()


def call(kernel, args, outs, scratch=(), micros=0, raw=()):
    outs = [out if isinstance(out, Far) else Far(*out) for out in outs]
    values = [a.value if isinstance(a, Far) else a for a in args]
    far = [i for i, a in enumerate(args) if isinstance(a, Far) and i not in raw]
    count, made = len(args), len(outs)

    def whole(*refs):
        ins, results = list(refs[:count]), refs[count : count + made]
        own = refs[count + made : count + made + len(scratch)]
        rest = refs[count + made + len(scratch) :]
        landing, leaving, sems = rest[: len(far)], rest[len(far) : len(far) + made], rest[-1]
        used = 0
        for n, i in enumerate(far):
            parts = args[i].parts
            ins[i] = Coming(ins[i], landing[n], [sems.at[used + k] for k in range(parts)])
            used += parts
        going = []
        for out, ref, target in zip(outs, leaving, results):
            going.append(
                Going(ref, target, [sems.at[used + n] for n in range(out.parts)], out.parts)
            )
            used += out.parts
        kernel(*ins, *going, *own)
        for i in far:
            ins[i].now()
        send(*going)
        for result in going:
            for copy in result.copies:
                copy.wait()

    near = pl.BlockSpec(memory_space=pltpu.VMEM)
    away = pl.BlockSpec(memory_space=pl.ANY)
    specs = [away if isinstance(a, Far) else near for a in args]
    specs[0] = pl.BlockSpec(memory_space=pltpu.SMEM)
    return pl.pallas_call(
        whole,
        out_shape=[jax.ShapeDtypeStruct(out.value, out.kind) for out in outs],
        in_specs=specs,
        out_specs=[away] * made,
        scratch_shapes=[
            *scratch,
            *[pltpu.VMEM(values[i].shape, values[i].dtype) for i in far],
            *[pltpu.VMEM(out.value, out.kind) for out in outs],
            pltpu.SemaphoreType.DMA((sum(args[i].parts for i in far) + sum(out.parts for out in outs),)),
        ],
        compiler_params=pltpu.CompilerParams(vmem_limit_bytes=56 * 1024 * 1024),
        cost_estimate=pl.CostEstimate(
            flops=int(micros * 1e9), bytes_accessed=0, transcendentals=0
        ),
    )(*values)


def swap(v):
    return lax.ppermute(v, "core", [(0, 1), (1, 0)])


def swap_y(v):
    return lax.ppermute(v, "ylo", [(0, 1), (1, 0)])


def exchange(v, axis):
    return lax.all_to_all(v, axis, 0, 0, tiled=True)


def copies(v, n):
    return lax.optimization_barrier(jnp.broadcast_to(v[None], (n,) + v.shape))


def tie(*values):
    return lax.optimization_barrier(values)


PAIRS_S = [(0, 1), (1, 0), (2, 3), (3, 2)]
PAIRS_T = [(0, 3), (3, 0), (1, 2), (2, 1)]
PAIRS_ST = [(0, 2), (2, 0), (1, 3), (3, 1)]


def x_bits():
    x = lax.axis_index("x")
    return ((x + 1) // 2) % 2, x // 2


def flip(v, pairs):
    return lax.ppermute(v, "x", pairs)


def body(
    inputs,
    segments,
    first_gain,
    query_matrix,
    key_matrix,
    value_matrix,
    output_matrix,
    second_gain,
    expert_ids,
    gate_values,
    priority,
    gate_weight,
    up_weight,
    down_weight,
    cotangent,
):
    tok = inputs.shape[1]
    width = inputs.shape[2]
    rows = query_matrix.shape[0]
    groups = lax.axis_size("fsdp")
    member = lax.axis_index("fsdp")
    core = lax.axis_index("core")
    even = core == 0
    experts = groups
    capacity = 5 * tok * TOP // (4 * experts)
    slots_all = experts * capacity
    half = width // 2
    kv_width = key_matrix.shape[1]
    length = groups * tok
    quarter = rows // XS
    bit_s, bit_t = x_bits()
    place_at = jnp.stack([core, member * tok, bit_s, bit_t]).astype(jnp.int32)

    def pick(a, b):
        return jnp.where(even, a, b)

    parts = width // kv_width
    kv_rows = rows // parts
    kv_half = pick(key_matrix, value_matrix).reshape(parts, kv_rows, kv_width)
    kv_piece = jnp.concatenate([kv_half[j] for j in range(parts)], axis=1)
    gains = jnp.pad(jnp.stack([first_gain, second_gain]), ((0, 6), (0, width - rows)))
    square_piece = jnp.concatenate(
        [
            lax.dynamic_slice(matrix, (bit * (rows // 2), core * half), (rows // 2, half))
            for matrix, bit in ((query_matrix, bit_s), (output_matrix, bit_t))
        ],
        axis=1,
    )
    kv_piece = jnp.concatenate([kv_piece, gains], axis=0)
    gathered = exchange(copies(kv_piece, groups), "fsdp")
    square_piece = copies(square_piece, groups)
    gathered, square_piece, place_at = tie(gathered, square_piece, place_at)
    squares = exchange(square_piece, "fsdp")

    ids = expert_ids[0].reshape(-1)
    order = priority[0, 0]
    earlier = (order[None, :] < order[:, None]) & (ids[None, :] == ids[:, None])
    slots = jnp.sum(earlier.astype(jnp.int32), axis=1)
    kept = slots < capacity
    expert_list = jnp.arange(experts, dtype=jnp.int32)
    chosen = (ids[:, None] == expert_list[None, :]) & kept[:, None]
    slot_of = jnp.sum(
        jnp.where(chosen, slots[:, None] + 1, 0).reshape(tok, TOP, experts), axis=1
    )
    slot_of = slot_of - 1
    gate_table = jnp.sum(
        jnp.where(chosen, gate_values[0].reshape(-1)[:, None], 0.0).reshape(tok, TOP, experts),
        axis=1,
    )
    slot_list = jnp.arange(capacity, dtype=jnp.int32)
    hits = slot_of.T[:, None, :] == slot_list[None, :, None]
    one_hot = hits.astype(BF).reshape(slots_all, tok)
    one_hot_t = (slot_of[:, :, None] == slot_list[None, None, :]).astype(BF)
    one_hot_t = one_hot_t.reshape(tok, slots_all)
    gate_hot = jnp.where(hits, gate_table.T[:, None, :], 0.0).reshape(slots_all, tok)
    slot_gate = jnp.sum(gate_hot, axis=1, keepdims=True)
    gate_high = gate_hot.astype(BF)
    gate_low = (gate_hot - gate_high.astype(F32)).astype(BF)
    send_grad = (dot(one_hot, cotangent[0]) * slot_gate).astype(BF)

    cosine, sine = angles(member * tok + jnp.arange(tok, dtype=jnp.int32))
    segment_row = segments[0]
    query_segments = lax.dynamic_slice_in_dim(segment_row, member * tok, tok)
    key_place = jnp.arange(length, dtype=jnp.int32)[:, None]
    query_place = (member * tok + jnp.arange(tok, dtype=jnp.int32))[None, :]
    allowed = (
        (key_place <= query_place)
        & (query_place - key_place < WINDOW)
        & (segment_row[:, None] == query_segments[None, :])
    )
    bias = jnp.where(allowed, 0.0, NEGATIVE).astype(F32)
    bias = jnp.concatenate([bias, bias], axis=1)
    gathered, cosine, sine = tie(gathered, cosine, sine)
    kv_raw = gathered[:, :kv_rows]
    gain_one = gathered[:, kv_rows, :rows].reshape(1, width).astype(F32)
    gain_two = gathered[:, kv_rows + 1, :rows].reshape(1, width).astype(F32)
    kv_raw_other = swap(kv_raw)

    square = (width, width)
    normed, scale_one, kv_send, kv_weight = call(
        key_kernel,
        [place_at, Far(inputs[0]), gain_one, Far(kv_raw), Far(kv_raw_other), cosine, sine],
        [((tok, width), BF), ((tok, HEAD_DIM), F32), ((groups, tok, 2 * kv_width), BF),
         ((width, 2 * kv_width), BF)],
    )
    kv_send, squares, one_hot_t, gate_high, gate_low, send_grad, bias = tie(
        kv_send, squares, one_hot_t, gate_high, gate_low, send_grad, bias
    )
    q_own, o_own = squares[..., :half], squares[..., half:]
    kv_all = exchange(kv_send, "fsdp").reshape(length, 2 * kv_width)
    q_got, o_got = flip(q_own, PAIRS_S), flip(o_own, PAIRS_T)
    send_grad, kv_all = tie(send_grad, kv_all)
    arrived_grad = exchange(send_grad, "fsdp")
    far_pieces = [
        Far(v)
        for v in (q_own, q_got, swap(q_own), swap(q_got), o_own, o_got, swap(o_own), swap(o_got))
    ]
    weight_parts = (groups, rows, width)
    (query_weight, output_weight, query_rot, mixed, probs, residual, scale_two,
     send_rows) = call(
        front_kernel,
        [place_at, Far(normed), Far(kv_all), Far(bias), Far(inputs[0]), gain_two, Far(one_hot_t),
         cosine, sine, *far_pieces],
        [(weight_parts, BF), (weight_parts, BF), ((tok, width), BF), ((tok, width), BF),
         ((HEADS // 2, length, 2 * tok), BF), ((tok, width), F32), ((tok, HEAD_DIM), F32),
         ((slots_all, width), BF)],
        [pltpu.SemaphoreType.DMA((8,))],
        raw=range(9, 17),
    )
    query_weight = query_weight.reshape(square)
    output_weight = output_weight.reshape(square)

    send_rows, arrived_grad = tie(send_rows, arrived_grad)
    arrived = exchange(send_rows, "fsdp")

    left_a = pick(mixed, normed)
    left_b = swap(pick(normed, mixed))
    left_one_a, left_two_a = flip(left_a, PAIRS_S), flip(left_a, PAIRS_T)
    left_one_b, left_two_b = flip(left_b, PAIRS_T), flip(left_b, PAIRS_S)
    upper_other = swap(lax.dynamic_slice_in_dim(arrived_grad, (1 - core) * half, half, 1))
    grad_hidden = dot_t(arrived_grad, down_weight[0])
    arrived, grad_hidden, upper_other, left_one_a, left_two_a, left_one_b, left_two_b = tie(
        arrived, grad_hidden, upper_other, left_one_a, left_two_a, left_one_b, left_two_b
    )
    left_three_a, left_three_b = flip(left_one_a, PAIRS_T), flip(left_one_b, PAIRS_S)
    arrived_other = swap(arrived)
    hidden, own_pre, sent_pre, grad_rows = call(
        expert_kernel,
        [place_at, Far(arrived, parts=2), Far(grad_hidden, parts=2), gate_weight[0], up_weight[0]],
        [Far((slots_all, half), BF, 2)] * 3 + [Far((slots_all, width), BF, 2)],
    )
    back_rows = exchange(grad_rows, "fsdp")
    expert_rows = width + half

    e_part = (2, expert_rows // 8, half)
    e_keep_a, e_send_a, e_keep_b, e_send_b = call(
        expert_weight_kernel,
        [place_at] + [Far(v) for v in (arrived, arrived_other, own_pre, swap(sent_pre), hidden,
                                       swap(hidden), arrived_grad, upper_other)],
        [(e_part, BF)] * 4,
        [pltpu.VMEM((expert_rows, half), BF)],
    )
    expert_out = dot(hidden, down_weight[0]).astype(BF)
    e_got_a, e_got_b = flip(e_send_a, PAIRS_S), flip(e_send_b, PAIRS_T)
    back_rows, expert_out, e_keep_a, e_keep_b, left_three_a, left_three_b = tie(
        back_rows, expert_out, e_keep_a, e_keep_b, left_three_a, left_three_b
    )
    left = [left_a, left_b, left_one_a, left_two_b, left_two_a, left_one_b, left_three_a,
            left_three_b]

    grad_residual, grad_attended, gain_two_part, grad_query_pre, kv_back, *qo_sent = call(
        back_kernel,
        [place_at, Far(back_rows), Far(one_hot_t), Far(residual), Far(scale_two), gain_two,
         Far(cotangent[0]), Far(output_weight), Far(probs), Far(kv_all), Far(query_rot), cosine,
         sine],
        [((tok, width), F32), ((tok, width), BF), ((groups, 2, HEAD_DIM), F32), ((tok, width), BF),
         ((length, 2 * kv_width), BF)] + [((tok, half), BF)] * XS,
    )
    kv_got = exchange(kv_back, "fsdp")
    e_keep_a, e_send_a, e_keep_b, e_send_b = call(
        expert_step_kernel,
        [place_at, Far(e_keep_a), Far(e_got_a), Far(e_keep_b), Far(e_got_b)],
        [(e_part[1:], BF)] * 4,
    )
    e_got_a, e_got_b = flip(e_send_a, PAIRS_T), flip(e_send_b, PAIRS_S)
    qo_set = fan(qo_sent)
    partial = call(
        query_back_kernel,
        [place_at, Far(grad_query_pre), Far(query_weight)],
        [((tok, width), F32)],
    )[0]
    qo_set[1], qo_set[2], qo_set[3], partial = tie(qo_set[1], qo_set[2], qo_set[3], partial)
    whole = 2 * XS * tok
    square_grad = call(
        square_weight_kernel,
        [place_at] + [Far(v) for v in (*qo_set, *[swap(v) for v in qo_set], *left)],
        [((width, width // XS), BF)],
        [pltpu.VMEM((whole, width // XS), BF), pltpu.VMEM((whole, width), BF),
         pltpu.SemaphoreType.DMA((16,))],
        raw=range(1, 17),
    )[0]
    kv_got, expert_out, square_grad = tie(kv_got, expert_out, square_grad)
    returned = exchange(expert_out, "fsdp")
    grad_kv_pre, *kv_sent = call(
        key_back_kernel,
        [place_at, Far(kv_got.reshape(groups, tok, 2 * kv_width), parts=2), cosine, sine],
        [((tok, 2 * kv_width), BF)] + [((tok, 2 * kv_width // XS), BF)] * XS,
    )
    kv_set = fan(kv_sent)
    input_grad, gain_one_part, mark = call(
        input_kernel,
        [place_at, Far(partial), Far(grad_kv_pre), Far(inputs[0]), Far(scale_one), gain_one,
         Far(kv_weight), Far(grad_residual)],
        [((tok, width), BF), ((groups, 2, HEAD_DIM), F32), ((8, HEAD_DIM), F32)],
        micros=6,
    )

    kv_set[1], kv_set[2], kv_set[3], mark = tie(kv_set[1], kv_set[2], kv_set[3], mark)
    e_got_a, e_got_b, mark = tie(e_got_a, e_got_b, mark)
    e_sum = call(
        expert_end_kernel,
        [place_at, Far(e_keep_a), Far(e_got_a), Far(e_keep_b), Far(e_got_b), mark],
        [(e_part, BF)],
    )[0]
    e_other_y = swap_y(e_sum)
    e_zero_a, e_zero_b = call(pair_kernel, [place_at, Far(e_sum), Far(e_other_y)], [(e_part[1:], BF)] * 2)
    e_one_a, e_one_b = flip(e_zero_a, PAIRS_T), flip(e_zero_b, PAIRS_S)
    e_two_a, e_two_b = flip(e_zero_a, PAIRS_S), flip(e_zero_b, PAIRS_T)

    spare = 2 * kv_width // XS
    part = rows // YLO
    packed_width = width // XS + spare
    packed = call(
        pack_kernel,
        [place_at]
        + [Far(v) for v in (square_grad, gain_one_part, swap(gain_one_part), gain_two_part,
                            swap(gain_two_part))]
        + [Far(v) for v in (*kv_set, *[swap(v) for v in kv_set], *left)],
        [Far((YLO, groups, part, packed_width), BF, 2)],
        [pltpu.VMEM((whole, spare), BF), pltpu.VMEM((whole, width), BF),
         pltpu.VMEM((width, spare), BF), pltpu.SemaphoreType.DMA((16,))],
        raw=range(6, 22),
    )[0]
    packed, returned = tie(packed, returned)
    packed = exchange(packed.reshape(YLO * groups, part, packed_width), ("ylo", "fsdp"))
    mixture = t_dot(gate_high, returned) + t_dot(gate_low, returned)
    outputs = (residual + mixture).astype(BF)
    packed, outputs = tie(packed, outputs)
    packed = call(sum_kernel, [place_at, Far(packed, parts=2)], [((YLO * XS, part, packed_width), BF)])[0]
    spreaded = exchange(packed, ("ylo", "x"))
    most = [e_zero_a, e_zero_b, e_one_a, e_one_b, e_two_a, e_two_b]
    *e_grads, most_mark = expert_outputs(
        expert_most_kernel, [place_at, *most, *[swap(v) for v in most]], [], e_part[1:], width, half
    )
    e_one_a, e_one_b, packed = tie(e_one_a, e_one_b, packed)
    e_three_a, e_three_b = flip(e_one_a, PAIRS_S), flip(e_one_b, PAIRS_T)
    e_three_a, e_three_b, most_mark = tie(e_three_a, e_three_b, most_mark)
    grad_gate, grad_up, grad_down, e_mark = expert_outputs(
        expert_rest_kernel,
        [place_at, e_three_a, e_three_b, swap(e_three_a), swap(e_three_b), most_mark,
         packed[0, :16, :HEAD_DIM]],
        e_grads,
        e_part[1:],
        width,
        half,
    )
    spreaded, e_mark = tie(spreaded, e_mark)
    grad_output_w, grad_query_w, grad_key_w, grad_value_w, grad_one, grad_two = call(
        final_kernel,
        [place_at, Far(spreaded), Far(swap(spreaded)), e_mark],
        [((rows, width), F32), ((rows, width), F32), ((rows, kv_width), F32),
         ((rows, kv_width), F32), ((1, rows), F32), ((1, rows), F32)],
    )
    return (
        outputs[None],
        input_grad[None],
        grad_one[0],
        grad_query_w,
        grad_key_w,
        grad_value_w,
        grad_output_w,
        grad_two[0],
        grad_gate[None],
        grad_up[None],
        grad_down[None],
    )


def solution(mesh):
    shape = mesh.devices.shape
    fine = Mesh(
        mesh.devices.reshape(YLO, XS, CORES, shape[1]), ("ylo", "x", "core", "fsdp")
    )
    return jax.shard_map(
        body,
        mesh=fine,
        in_specs=(
            P(REP, "fsdp", None),
            P(REP, None),
            P("fsdp"),
            P("fsdp", None),
            P("fsdp", None),
            P("fsdp", None),
            P("fsdp", None),
            P("fsdp"),
            P(REP, "fsdp", None),
            P(REP, "fsdp", None),
            P(REP, "fsdp", None),
            P("fsdp", None, None),
            P("fsdp", None, None),
            P("fsdp", None, None),
            P(REP, "fsdp", None),
        ),
        out_specs=(
            P(REP, "fsdp", None),
            P(REP, "fsdp", None),
            P("fsdp"),
            P("fsdp", None),
            P("fsdp", None),
            P("fsdp", None),
            P("fsdp", None),
            P("fsdp"),
            P("fsdp", None, None),
            P("fsdp", None, None),
            P("fsdp", None, None),
        ),
        check_vma=False,
    )
```

```python
import jax
import jax.numpy as jnp
from jax import lax
from jax.experimental import pallas as pl
from jax.experimental.pallas import tpu as pltpu
from jax.sharding import Mesh
from jax.sharding import PartitionSpec as P

HEADS = 12
KV_HEADS = 2
HEAD_DIM = 128
TOP = 4
WINDOW = 1024

EPSILON = 1e-06
THETA = 10000.0
NEGATIVE = -1e30

YLO, XS, CORES = 2, 4, 2
REP = ("ylo", "x", "core")
BF = jnp.bfloat16
F32 = jnp.float32


def angles(positions):
    half_width = HEAD_DIM // 2
    frequency = THETA ** (-(jnp.arange(half_width, dtype=F32) * 2.0) / HEAD_DIM)
    phase = positions.astype(F32)[:, None] * frequency[None, :]
    cosine, sine = jnp.cos(phase), jnp.sin(phase)
    return (
        jnp.concatenate([cosine, cosine], axis=1),
        jnp.concatenate([-sine, sine], axis=1),
    )


def dot(a, b):
    return jnp.dot(a, b, preferred_element_type=F32)


def dot_t(a, b):
    return lax.dot_general(a, b, (((1,), (1,)), ((), ())), preferred_element_type=F32)


def t_dot(a, b):
    return lax.dot_general(a, b, (((0,), (0,)), ((), ())), preferred_element_type=F32)


def fan(pieces):
    return [
        pieces[0],
        flip(pieces[1], PAIRS_S),
        flip(pieces[2], PAIRS_T),
        flip(pieces[3], PAIRS_ST),
    ]


def add(a, b):
    return (a.astype(F32) + b.astype(F32)).astype(BF)


def turn(piece, cosine, sine):
    return piece * cosine + pltpu.roll(piece, HEAD_DIM // 2, 1) * sine


def turn_back(piece, cosine, sine):
    return piece * cosine - pltpu.roll(piece, HEAD_DIM // 2, 1) * sine


def stacked(ref, pair):
    low = 2 * pair * HEAD_DIM
    return jnp.concatenate(
        [ref[:, pl.ds(low, HEAD_DIM)], ref[:, pl.ds(low + HEAD_DIM, HEAD_DIM)]], axis=0
    )


def unstack(ref, pair, value):
    low, rows = 2 * pair * HEAD_DIM, value.shape[0] // 2
    ref[:, pl.ds(low, HEAD_DIM)] = value[:rows]
    ref[:, pl.ds(low + HEAD_DIM, HEAD_DIM)] = value[rows:]


def put_gain(out, total):
    groups, _, lanes = out.shape
    size = total.shape[1] // groups
    for f in range(groups):
        row = total[:, f * size : (f + 1) * size]
        out[f, 0:1, :] = row[:, :lanes]
        out[f, 1:2, pl.ds(0, size - lanes)] = row[:, lanes:]


def key_kernel(place, src, gain, raw_own, raw_other, cos, sin, normed_o, scale_o, send_o, weight_o):
    core = place[0]
    groups, kv_rows, width = raw_own.shape
    kv_width = weight_o.shape[1] // 2
    parts = width // kv_width
    source = src[...].astype(F32)
    scale = lax.rsqrt(jnp.mean(source * source, axis=-1, keepdims=True) + EPSILON)
    scale_o[...] = jnp.broadcast_to(scale, scale_o.shape)
    normed = (source * scale * gain[...]).astype(BF)
    normed_o[...] = normed
    send(scale_o, normed_o)
    for raw, which in ((raw_own, core), (raw_other, 1 - core)):
        at = pl.ds(pl.multiple_of(which * kv_width, kv_width), kv_width)
        for f in range(groups):
            for j in range(parts):
                weight_o[pl.ds((f * parts + j) * kv_rows, kv_rows), at] = raw[
                    f, :, pl.ds(j * kv_width, kv_width)
                ]
    send(weight_o)
    pre = dot(normed, weight_o[...])
    for head in range(2 * KV_HEADS):
        low, high = head * HEAD_DIM, (head + 1) * HEAD_DIM
        piece = pre[:, low:high]
        if head < KV_HEADS:
            piece = turn(piece, cos[...], sin[...])
        for f in range(groups):
            send_o[f, :, low:high] = piece.astype(BF)


def front_kernel(place, normed, kv, bias, src, gain, hot_t, cos, sin, *refs):
    pieces = refs[:8]
    query_w, output_w, query_o, mixed_o, probs_o, resid_o, scale_o, send_o, sems = refs[8:]
    core, s, t = place[0], place[2], place[3]
    _, rows, half = pieces[0].shape
    copies = []
    for n, block in enumerate(pieces):
        weight, bit = ((query_w, s), (output_w, t))[n // 4]
        which = core if n % 4 < 2 else 1 - core
        part = bit if n % 2 == 0 else 1 - bit
        at = pl.ds(pl.multiple_of(part * rows, rows), rows)
        cols = pl.ds(pl.multiple_of(which * half, half), half)
        copy = pltpu.make_async_copy(block, weight.ref.at[:, at, cols], sems.at[n])
        copy.start()
        copies.append(copy)
    width = 2 * half
    for copy in copies[:4]:
        copy.wait()
    query_w.send()
    pre = dot(normed[...], query_w[...].reshape(width, width))
    for head in range(HEADS):
        low, high = head * HEAD_DIM, (head + 1) * HEAD_DIM
        query_o[:, low:high] = turn(pre[:, low:high], cos[...], sin[...]).astype(BF)
    query_o.send()
    kv_width = kv.shape[1] // 2
    for pair in range(HEADS // 2):
        group = 2 * pair // (HEADS // KV_HEADS)
        keys = kv[:, pl.ds(group * HEAD_DIM, HEAD_DIM)]
        values = kv[:, pl.ds(kv_width + group * HEAD_DIM, HEAD_DIM)]
        scores = dot_t(keys, stacked(query_o, pair)) * HEAD_DIM ** (-0.5) + bias[...]
        weights = jnp.exp(scores - jnp.max(scores, axis=0, keepdims=True))
        probs = (weights * (1.0 / jnp.sum(weights, axis=0, keepdims=True))).astype(BF)
        probs_o[pair] = probs
        unstack(mixed_o, pair, t_dot(probs, values).astype(BF))
    send(probs_o, mixed_o)
    for copy in copies[4:]:
        copy.wait()
    output_w.send()
    resid = src[...].astype(F32) + dot(mixed_o[...], output_w[...].reshape(width, width))
    resid_o[...] = resid
    resid_o.send()
    scale = lax.rsqrt(jnp.mean(resid * resid, axis=-1, keepdims=True) + EPSILON)
    scale_o[...] = jnp.broadcast_to(scale, scale_o.shape)
    second = (resid * scale * gain[...]).astype(BF)
    send_o[...] = t_dot(hot_t[...], second).astype(BF)


def expert_kernel(place, rows, grad_hidden, gate_w, up_w, hidden_o, own_o, sent_o, back_o):
    core = place[0]
    count = rows.shape[0]
    step = count // 2
    for n, low in enumerate(range(0, count, step)):
        at = pl.ds(low, step)
        block = rows.part(n)[at, :]
        gate = dot(block, gate_w[...])
        up = dot(block, up_w[...])
        sigmoid = 1.0 / (1.0 + jnp.exp(-gate))
        silu = gate * sigmoid
        hidden_o[at, :] = (silu * up).astype(BF)
        grad = grad_hidden.part(n)[at, :]
        grad_gate = (grad * up * (sigmoid * (1.0 + gate * (1.0 - sigmoid)))).astype(BF)
        grad_up = (grad * silu).astype(BF)
        own_o[at, :] = jnp.where(core == 0, grad_gate, grad_up)
        sent_o[at, :] = jnp.where(core == 0, grad_up, grad_gate)
        for result in (sent_o, hidden_o, own_o):
            result.send(n + 1)
        back_o[at, :] = (dot_t(grad_gate, gate_w[...]) + dot_t(grad_up, up_w[...])).astype(BF)
        back_o.send(n + 1)


def expert_weight_kernel(
    place, rows, rows_got, pre, pre_got, hidden, hidden_got, arrived, upper_got,
    keep_a, send_a, keep_b, send_b, total,
):
    s, t = place[2], place[3]
    width, half = rows.shape[1], hidden.shape[1]
    upper = arrived[:, pl.ds(pl.multiple_of(place[0] * half, half), half)]
    step = 256
    for low in range(0, width, step):
        at = pl.ds(low, step)
        total[at, :] = (t_dot(rows[:, at], pre[...]) + t_dot(rows_got[:, at], pre_got[...])).astype(
            BF
        )
    for low in range(0, half, step):
        at = pl.ds(low, step)
        total[pl.ds(width + low, step), :] = (
            t_dot(hidden[:, at], upper) + t_dot(hidden_got[:, at], upper_got[...])
        ).astype(BF)
    big, small = width // 8, half // 8
    for out, side, spots in (
        (send_a, 0, ((1 - s, 0), (1 - s, 1))),
        (send_b, 1, ((0, 1 - t), (1, 1 - t))),
        (keep_a, 0, ((s, 0), (s, 1))),
        (keep_b, 1, ((0, t), (1, t))),
    ):
        for j, (row_s, row_t) in enumerate(spots):
            piece = side * 4 + 2 * row_s + row_t
            out[j, pl.ds(0, big), :] = total[pl.ds(pl.multiple_of(piece * big, big), big), :]
            start = pl.multiple_of(width + piece * small, small)
            out[j, pl.ds(big, small), :] = total[pl.ds(start, small), :]
        out.send()


def expert_step_kernel(place, keep_a, got_a, keep_b, got_b, keep_ao, send_ao, keep_bo, send_bo):
    s, t = place[2], place[3]
    send_ao[...] = add(keep_a[1 - t], got_a[1 - t])
    send_ao.send()
    send_bo[...] = add(keep_b[1 - s], got_b[1 - s])
    send_bo.send()
    keep_ao[...] = add(keep_a[t], got_a[t])
    keep_ao.send()
    keep_bo[...] = add(keep_b[s], got_b[s])


def expert_end_kernel(place, keep_a, got_a, keep_b, got_b, mark, out):
    out[0] = add(keep_a[...], got_a[...])
    out[1] = add(keep_b[...], got_b[...])


def pair_kernel(place, a, b, one, two):
    one[...] = add(a[0], b[0])
    one.send()
    two[...] = add(a[1], b[1])


def place_experts(place, blocks, outs, stage, sems):
    core = place[0]
    gate_o, up_o, down_o = outs
    half = stage.shape[2]
    big = gate_o.shape[0] // 8
    small = stage.shape[1] - big
    moves = []
    for n, (side, row_s, row_t, which, block) in enumerate(blocks):
        stage[n] = block[...].astype(F32)
        piece = side * 4 + 2 * row_s + row_t
        at = pl.ds(pl.multiple_of(piece * big, big), big)
        cols = pl.ds(pl.multiple_of(which * half, half), half)
        to_gate = pltpu.make_async_copy(stage.at[n, pl.ds(0, big)], gate_o.at[at], sems.at[2 * n])
        to_up = pltpu.make_async_copy(stage.at[n, pl.ds(0, big)], up_o.at[at], sems.at[2 * n])
        to_down = pltpu.make_async_copy(
            stage.at[n, pl.ds(big, small)],
            down_o.at[pl.ds(pl.multiple_of(piece * small, small), small), cols],
            sems.at[2 * n + 1],
        )

        @pl.when(which == 0)
        def _():
            to_gate.start()

        @pl.when(which == 1)
        def _():
            to_up.start()

        to_down.start()
        moves.append((which, to_gate, to_up, to_down))
    for which, to_gate, to_up, to_down in moves:

        @pl.when(which == 0)
        def _():
            to_gate.wait()

        @pl.when(which == 1)
        def _():
            to_up.wait()

        to_down.wait()


def expert_most_kernel(place, *refs):
    core, s, t = place[0], place[2], place[3]
    gate_o, up_o, down_o, mark_o, stage, sems = refs[12:]
    mark_o[...] = jnp.zeros(mark_o.shape, F32)
    blocks = []
    for first, which in ((0, core), (6, 1 - core)):
        zero_a, zero_b, one_a, one_b, two_a, two_b = refs[first : first + 6]
        blocks += [
            (0, s, t, which, zero_a),
            (1, s, t, which, zero_b),
            (0, s, 1 - t, which, one_a),
            (1, 1 - s, t, which, one_b),
            (0, 1 - s, t, which, two_a),
            (1, s, 1 - t, which, two_b),
        ]
    place_experts(place, blocks, (gate_o, up_o, down_o), stage, sems)


def expert_rest_kernel(place, *refs):
    core, s, t = place[0], place[2], place[3]
    gate_o, up_o, down_o, mark_o, stage, sems = refs[9:]
    mark_o[...] = jnp.zeros(mark_o.shape, F32)
    blocks = []
    for first, which in ((0, core), (2, 1 - core)):
        for side in range(2):
            blocks.append((side, 1 - s, 1 - t, which, refs[first + side]))
    place_experts(place, blocks, (gate_o, up_o, down_o), stage, sems)


def expert_outputs(kernel, args, before, part, width, half):
    near = pl.BlockSpec(memory_space=pltpu.VMEM)
    away = pl.BlockSpec(memory_space=pl.ANY)
    shapes = [
        jax.ShapeDtypeStruct(shape, F32)
        for shape in ((width, half), (width, half), (half, width), (8, HEAD_DIM))
    ]
    blocks = 12 if not before else 4
    return pl.pallas_call(
        kernel,
        out_shape=shapes,
        in_specs=[pl.BlockSpec(memory_space=pltpu.SMEM)]
        + [near] * (len(args) - 1)
        + [away] * len(before),
        out_specs=[away] * 3 + [near],
        scratch_shapes=[
            pltpu.VMEM((blocks,) + part, F32),
            pltpu.SemaphoreType.DMA((2 * blocks,)),
        ],
        input_output_aliases={len(args) + n: n for n in range(len(before))},
        compiler_params=pltpu.CompilerParams(vmem_limit_bytes=56 * 1024 * 1024),
        cost_estimate=pl.CostEstimate(flops=0, bytes_accessed=0, transcendentals=0),
    )(*args, *before)


def back_kernel(
    place, back, hot_t, resid_i, scale_i, gain, cot, weight, probs_i, kv, q, cos, sin,
    grad_resid_o, attended_o, gain_o, query_o, kv_o, *sent_o,
):
    kv_width = kv.shape[1] // 2
    resid = resid_i[...]
    scale = scale_i[:, :1]
    grad_second = dot(hot_t[...], back[...])
    weighted = grad_second * gain[...]
    inner = jnp.sum(weighted * resid, axis=-1, keepdims=True)
    grad_resid = (
        cot[...].astype(F32)
        + scale * weighted
        - resid * (scale * scale * scale * inner * (1.0 / resid.shape[-1]))
    )
    put_gain(gain_o, jnp.sum(grad_second * resid * scale, axis=0, keepdims=True))
    grad_resid_o[...] = grad_resid
    grad_resid_o.send()
    attended = grad_resid.astype(BF)
    attended_o[...] = attended
    grad_mixed = dot_t(attended, weight[...]).astype(BF)
    pairs = HEADS // KV_HEADS // 2
    rows = resid.shape[0]
    for group in range(KV_HEADS):
        keys = kv[:, pl.ds(group * HEAD_DIM, HEAD_DIM)]
        values = kv[:, pl.ds(kv_width + group * HEAD_DIM, HEAD_DIM)]
        grad_keys = jnp.zeros(keys.shape, F32)
        grad_values = jnp.zeros(keys.shape, F32)
        for pair in range(group * pairs, (group + 1) * pairs):
            low, high = 2 * pair * HEAD_DIM, (2 * pair + 1) * HEAD_DIM
            upper = jnp.concatenate(
                [grad_mixed[:, low:high], grad_mixed[:, high : high + HEAD_DIM]], axis=0
            )
            probs = probs_i[pair]
            wide = probs.astype(F32)
            grad_probs = dot_t(values, upper)
            total = jnp.sum(wide * grad_probs, axis=0, keepdims=True)
            grad_scores = (wide * (grad_probs - total)).astype(BF)
            grad_values = grad_values + dot(probs, upper)
            grad_keys = grad_keys + dot(grad_scores, stacked(q, pair))
            grad_query = t_dot(grad_scores, keys) * HEAD_DIM ** (-0.5)
            for at, part in ((low, grad_query[:rows]), (high, grad_query[rows:])):
                turned = turn_back(part, cos[...], sin[...])
                query_o[:, pl.ds(at, HEAD_DIM)] = turned.astype(BF)
        at = pl.ds(group * HEAD_DIM, HEAD_DIM)
        kv_o[:, at] = (grad_keys * HEAD_DIM ** (-0.5)).astype(BF)
        kv_o[:, pl.ds(kv_width + group * HEAD_DIM, HEAD_DIM)] = grad_values.astype(BF)
    kv_o.send()
    size = resid.shape[1] // XS
    for out, part in zip(sent_o, x_parts(place)):
        at = pl.ds(pl.multiple_of(part * size, size), size)
        one, two = attended_o[:, at], query_o[:, at]
        out[:, pl.ds(0, size)] = jnp.where(place[0] == 0, one, two)
        out[:, pl.ds(size, size)] = jnp.where(place[0] == 0, two, one)


def x_parts(place):
    s, t = place[2], place[3]
    return [
        a + 3 * b - 2 * a * b for a, b in ((s, t), (1 - s, t), (s, 1 - t), (1 - s, 1 - t))
    ]


def collect(pieces, whole, sems, first):
    rows = pieces[0].shape[0]
    copies = []
    for n, piece in enumerate(pieces):
        copy = pltpu.make_async_copy(
            piece, whole.at[pl.ds(n * rows, rows)], sems.at[first + n]
        )
        copy.start()
        copies.append(copy)
    return copies


def interleave(own, other):
    return [piece for pair in zip(own, other) for piece in pair]


def square_weight_kernel(place, *refs):
    own, other, left = refs[:4], refs[4:8], refs[8:16]
    out, all_grads, all_left, sems = refs[16:]
    size = out.shape[1]
    copies = collect(
        interleave(
            [ref.at[:, pl.ds(0, size)] for ref in own],
            [ref.at[:, pl.ds(size, size)] for ref in other],
        ),
        all_grads, sems, 0,
    )
    copies += collect(left, all_left, sems, 8)
    for copy in copies:
        copy.wait()
    step = 256
    for low in range(0, all_left.shape[1], step):
        at = pl.ds(low, step)
        out[at, :] = t_dot(all_left[:, at], all_grads[...]).astype(BF)


def pack_kernel(place, square, one_own, one_got, two_own, two_got, *refs):
    grads, left = refs[:8], refs[8:16]
    out, all_grads, all_left, total, sems = refs[16:]
    copies = collect(interleave(grads[:4], grads[4:]), all_grads, sems, 0)
    copies += collect(left, all_left, sems, 8)
    size, small = square.shape[1], total.shape[1]
    count, groups, part, _ = out.shape
    row = lax.broadcasted_iota(jnp.int32, (part, small), 0)
    lane = lax.broadcasted_iota(jnp.int32, (part, small), 1)
    short = lane < square.shape[0] // groups - small
    gains = []
    for f in range(groups):
        one, two = one_own[f] + one_got[f], two_own[f] + two_got[f]
        block = jnp.where(row == 0, one[0:1], 0.0)
        block = jnp.where((row == 1) & short, one[1:2], block)
        block = jnp.where(row == 2, two[0:1], block)
        gains.append(jnp.where((row == 3) & short, two[1:2], block).astype(BF))
        for y in range(count):
            out[y, f, :, pl.ds(0, size)] = square[pl.ds((f * count + y) * part, part), :]
    for copy in copies:
        copy.wait()
    total[...] = t_dot(all_grads[...], all_left[...]).T.astype(BF)
    even = place[0] == 0
    for y in range(count):
        for f in range(groups):
            at = pl.ds((f * count + y) * part, part)
            out[y, f, :, pl.ds(size, small)] = jnp.where(even, gains[f], total[at, :])
        out.send(y + 1)


def sum_parts(parts):
    half = parts.shape[0] // 2
    total = parts.part(0)[0].astype(F32)
    for k in range(1, 2 * half):
        total = total + parts.part(k // half)[k].astype(F32)
    return total


def sum_kernel(place, parts, out):
    total = sum_parts(parts)
    total = total.astype(BF)
    for k in range(out.shape[0]):
        out[k] = total


def final_kernel(
    place, own, other, mark, output_o, query_o, key_o, value_o, gain_one_o, gain_two_o
):
    even = place[0] == 0
    part = own.shape[1]
    size = output_o.shape[1] // XS
    small = key_o.shape[1] * 2 // XS
    total = jnp.zeros((8, small), F32)
    for y in range(YLO):
        rows = pl.ds(y * part, part)
        for x in range(XS):
            mine, theirs = own.part(y)[y * XS + x], other.part(y)[y * XS + x]
            first = jnp.where(even, mine, theirs).astype(F32)
            second = jnp.where(even, theirs, mine).astype(F32)
            at = pl.ds(x * size, size)
            output_o[rows, at] = first[:, :size]
            query_o[rows, at] = second[:, :size]
            into = key_o if x < XS // 2 else value_o
            into[rows, pl.ds(x % (XS // 2) * small, small)] = second[:, size:]
            if y == 0:
                total = total + first[:8, size:]
        for out in (output_o, query_o, key_o, value_o):
            out.send(y + 1)
    for ref, row in ((gain_one_o, 0), (gain_two_o, 2)):
        ref[:, pl.ds(0, small)] = total[row : row + 1]
        ref[:, pl.ds(small, ref.shape[1] - small)] = total[
            row + 1 : row + 2, : ref.shape[1] - small
        ]


def key_back_kernel(place, parts, cos, sin, pre_o, *sent_o):
    kv_width = parts.shape[-1] // 2
    total = sum_parts(parts)
    for head in range(2 * KV_HEADS):
        low, high = head * HEAD_DIM, (head + 1) * HEAD_DIM
        piece = total[:, low:high]
        if head < KV_HEADS:
            piece = turn_back(piece, cos[...], sin[...])
        pre_o[:, low:high] = piece.astype(BF)
    size = 2 * kv_width // XS
    for out, part in zip(sent_o, x_parts(place)):
        out[...] = pre_o[:, pl.ds(pl.multiple_of(part * size, size), size)]


def query_back_kernel(place, query, query_w, out):
    out[...] = dot_t(query[...], query_w[...])


def input_kernel(
    place, partial, pre, src, scale_i, gain, kv_w, grad_resid, input_o, gain_o, mark_o
):
    mark_o[...] = jnp.zeros(mark_o.shape, F32)
    grad_normed = partial[...] + dot_t(pre[...], kv_w[...])
    source = src[...].astype(F32)
    scale = scale_i[:, :1]
    put_gain(gain_o, jnp.sum(grad_normed * source * scale, axis=0, keepdims=True))
    send(gain_o)
    weighted = grad_normed * gain[...]
    inner = jnp.sum(weighted * source, axis=-1, keepdims=True)
    input_o[...] = (
        grad_resid[...]
        + scale * weighted
        - source * (scale * scale * scale * inner * (1.0 / source.shape[-1]))
    ).astype(BF)


class Far:
    def __init__(self, value, kind=None, parts=1):
        self.value, self.kind, self.parts = value, kind, parts


class Coming:
    def __init__(self, source, ref, sems):
        self.ref, self.shape, self.left = ref, ref.shape, 0
        rows = ref.shape[0] // len(sems)
        self.copies = [
            pltpu.make_async_copy(
                source.at[pl.ds(n * rows, rows)], ref.at[pl.ds(n * rows, rows)], sem
            )
            for n, sem in enumerate(sems)
        ]
        for copy in self.copies:
            copy.start()

    def part(self, n):
        for copy in self.copies[self.left : n + 1]:
            copy.wait()
        self.left = max(self.left, n + 1)
        return self.ref

    def now(self):
        return self.part(len(self.copies) - 1)

    def __getitem__(self, index):
        return self.now()[index]

    @property
    def at(self):
        return self.now().at


class Going:
    def __init__(self, ref, target, sems, parts):
        self.ref, self.target, self.shape, self.sent = ref, target, ref.shape, 0
        rows = ref.shape[0] // parts
        self.copies = [
            pltpu.make_async_copy(
                ref.at[pl.ds(n * rows, rows)], target.at[pl.ds(n * rows, rows)], sem
            )
            for n, sem in enumerate(sems)
        ]

    def __getitem__(self, index):
        return self.ref[index]

    def __setitem__(self, index, value):
        self.ref[index] = value

    def send(self, upto=None):
        upto = len(self.copies) if upto is None else upto
        for copy in self.copies[self.sent : upto]:
            copy.start()
        self.sent = max(self.sent, upto)


def send(self):
        if not self.sent:
            self.copy.start()
            self.sent = True


def send(*results):
    for result in results:
        result.send()


def call(kernel, args, outs, scratch=(), micros=0, raw=()):
    outs = [out if isinstance(out, Far) else Far(*out) for out in outs]
    values = [a.value if isinstance(a, Far) else a for a in args]
    far = [i for i, a in enumerate(args) if isinstance(a, Far) and i not in raw]
    count, made = len(args), len(outs)

    def whole(*refs):
        ins, results = list(refs[:count]), refs[count : count + made]
        own = refs[count + made : count + made + len(scratch)]
        rest = refs[count + made + len(scratch) :]
        landing, leaving, sems = rest[: len(far)], rest[len(far) : len(far) + made], rest[-1]
        used = 0
        for n, i in enumerate(far):
            parts = args[i].parts
            ins[i] = Coming(ins[i], landing[n], [sems.at[used + k] for k in range(parts)])
            used += parts
        going = []
        for out, ref, target in zip(outs, leaving, results):
            going.append(
                Going(ref, target, [sems.at[used + n] for n in range(out.parts)], out.parts)
            )
            used += out.parts
        kernel(*ins, *going, *own)
        for i in far:
            ins[i].now()
        send(*going)
        for result in going:
            for copy in result.copies:
                copy.wait()

    near = pl.BlockSpec(memory_space=pltpu.VMEM)
    away = pl.BlockSpec(memory_space=pl.ANY)
    specs = [away if isinstance(a, Far) else near for a in args]
    specs[0] = pl.BlockSpec(memory_space=pltpu.SMEM)
    return pl.pallas_call(
        whole,
        out_shape=[jax.ShapeDtypeStruct(out.value, out.kind) for out in outs],
        in_specs=specs,
        out_specs=[away] * made,
        scratch_shapes=[
            *scratch,
            *[pltpu.VMEM(values[i].shape, values[i].dtype) for i in far],
            *[pltpu.VMEM(out.value, out.kind) for out in outs],
            pltpu.SemaphoreType.DMA((sum(args[i].parts for i in far) + sum(out.parts for out in outs),)),
        ],
        compiler_params=pltpu.CompilerParams(vmem_limit_bytes=56 * 1024 * 1024),
        cost_estimate=pl.CostEstimate(
            flops=int(micros * 1e9), bytes_accessed=0, transcendentals=0
        ),
    )(*values)


def swap(v):
    return lax.ppermute(v, "core", [(0, 1), (1, 0)])


def swap_y(v):
    return lax.ppermute(v, "ylo", [(0, 1), (1, 0)])


def exchange(v, axis):
    return lax.all_to_all(v, axis, 0, 0, tiled=True)


def copies(v, n):
    return lax.optimization_barrier(jnp.broadcast_to(v[None], (n,) + v.shape))


def tie(*values):
    return lax.optimization_barrier(values)


PAIRS_S = [(0, 1), (1, 0), (2, 3), (3, 2)]
PAIRS_T = [(0, 3), (3, 0), (1, 2), (2, 1)]
PAIRS_ST = [(0, 2), (2, 0), (1, 3), (3, 1)]


def x_bits():
    x = lax.axis_index("x")
    return ((x + 1) // 2) % 2, x // 2


def flip(v, pairs):
    return lax.ppermute(v, "x", pairs)


def body(
    inputs,
    segments,
    first_gain,
    query_matrix,
    key_matrix,
    value_matrix,
    output_matrix,
    second_gain,
    expert_ids,
    gate_values,
    priority,
    gate_weight,
    up_weight,
    down_weight,
    cotangent,
):
    tok = inputs.shape[1]
    width = inputs.shape[2]
    rows = query_matrix.shape[0]
    groups = lax.axis_size("fsdp")
    member = lax.axis_index("fsdp")
    core = lax.axis_index("core")
    even = core == 0
    experts = groups
    capacity = 5 * tok * TOP // (4 * experts)
    slots_all = experts * capacity
    half = width // 2
    kv_width = key_matrix.shape[1]
    length = groups * tok
    quarter = rows // XS
    bit_s, bit_t = x_bits()
    place_at = jnp.stack([core, member * tok, bit_s, bit_t]).astype(jnp.int32)

    def pick(a, b):
        return jnp.where(even, a, b)

    parts = width // kv_width
    kv_rows = rows // parts
    kv_half = pick(key_matrix, value_matrix).reshape(parts, kv_rows, kv_width)
    kv_piece = jnp.concatenate([kv_half[j] for j in range(parts)], axis=1)
    gains = jnp.pad(jnp.stack([first_gain, second_gain]), ((0, 6), (0, width - rows)))
    square_piece = jnp.concatenate(
        [
            lax.dynamic_slice(matrix, (bit * (rows // 2), core * half), (rows // 2, half))
            for matrix, bit in ((query_matrix, bit_s), (output_matrix, bit_t))
        ],
        axis=1,
    )
    kv_piece = jnp.concatenate([kv_piece, gains], axis=0)
    gathered = exchange(copies(kv_piece, groups), "fsdp")
    square_piece = copies(square_piece, groups)
    gathered, square_piece, place_at = tie(gathered, square_piece, place_at)
    squares = exchange(square_piece, "fsdp")

    ids = expert_ids[0].reshape(-1)
    order = priority[0, 0]
    earlier = (order[None, :] < order[:, None]) & (ids[None, :] == ids[:, None])
    slots = jnp.sum(earlier.astype(jnp.int32), axis=1)
    kept = slots < capacity
    expert_list = jnp.arange(experts, dtype=jnp.int32)
    chosen = (ids[:, None] == expert_list[None, :]) & kept[:, None]
    slot_of = jnp.sum(
        jnp.where(chosen, slots[:, None] + 1, 0).reshape(tok, TOP, experts), axis=1
    )
    slot_of = slot_of - 1
    gate_table = jnp.sum(
        jnp.where(chosen, gate_values[0].reshape(-1)[:, None], 0.0).reshape(tok, TOP, experts),
        axis=1,
    )
    slot_list = jnp.arange(capacity, dtype=jnp.int32)
    hits = slot_of.T[:, None, :] == slot_list[None, :, None]
    one_hot = hits.astype(BF).reshape(slots_all, tok)
    one_hot_t = (slot_of[:, :, None] == slot_list[None, None, :]).astype(BF)
    one_hot_t = one_hot_t.reshape(tok, slots_all)
    gate_hot = jnp.where(hits, gate_table.T[:, None, :], 0.0).reshape(slots_all, tok)
    slot_gate = jnp.sum(gate_hot, axis=1, keepdims=True)
    gate_high = gate_hot.astype(BF)
    gate_low = (gate_hot - gate_high.astype(F32)).astype(BF)
    send_grad = (dot(one_hot, cotangent[0]) * slot_gate).astype(BF)

    cosine, sine = angles(member * tok + jnp.arange(tok, dtype=jnp.int32))
    segment_row = segments[0]
    query_segments = lax.dynamic_slice_in_dim(segment_row, member * tok, tok)
    key_place = jnp.arange(length, dtype=jnp.int32)[:, None]
    query_place = (member * tok + jnp.arange(tok, dtype=jnp.int32))[None, :]
    allowed = (
        (key_place <= query_place)
        & (query_place - key_place < WINDOW)
        & (segment_row[:, None] == query_segments[None, :])
    )
    bias = jnp.where(allowed, 0.0, NEGATIVE).astype(F32)
    bias = jnp.concatenate([bias, bias], axis=1)
    gathered, cosine, sine = tie(gathered, cosine, sine)
    kv_raw = gathered[:, :kv_rows]
    gain_one = gathered[:, kv_rows, :rows].reshape(1, width).astype(F32)
    gain_two = gathered[:, kv_rows + 1, :rows].reshape(1, width).astype(F32)
    kv_raw_other = swap(kv_raw)

    square = (width, width)
    normed, scale_one, kv_send, kv_weight = call(
        key_kernel,
        [place_at, Far(inputs[0]), gain_one, Far(kv_raw), Far(kv_raw_other), cosine, sine],
        [((tok, width), BF), ((tok, HEAD_DIM), F32), ((groups, tok, 2 * kv_width), BF),
         ((width, 2 * kv_width), BF)],
    )
    kv_send, squares, one_hot_t, gate_high, gate_low, send_grad, bias = tie(
        kv_send, squares, one_hot_t, gate_high, gate_low, send_grad, bias
    )
    q_own, o_own = squares[..., :half], squares[..., half:]
    kv_all = exchange(kv_send, "fsdp").reshape(length, 2 * kv_width)
    q_got, o_got = flip(q_own, PAIRS_S), flip(o_own, PAIRS_T)
    send_grad, kv_all = tie(send_grad, kv_all)
    arrived_grad = exchange(send_grad, "fsdp")
    far_pieces = [
        Far(v)
        for v in (q_own, q_got, swap(q_own), swap(q_got), o_own, o_got, swap(o_own), swap(o_got))
    ]
    weight_parts = (groups, rows, width)
    (query_weight, output_weight, query_rot, mixed, probs, residual, scale_two,
     send_rows) = call(
        front_kernel,
        [place_at, Far(normed), Far(kv_all), Far(bias), Far(inputs[0]), gain_two, Far(one_hot_t),
         cosine, sine, *far_pieces],
        [(weight_parts, BF), (weight_parts, BF), ((tok, width), BF), ((tok, width), BF),
         ((HEADS // 2, length, 2 * tok), BF), ((tok, width), F32), ((tok, HEAD_DIM), F32),
         ((slots_all, width), BF)],
        [pltpu.SemaphoreType.DMA((8,))],
        raw=range(9, 17),
    )
    query_weight = query_weight.reshape(square)
    output_weight = output_weight.reshape(square)

    send_rows, arrived_grad = tie(send_rows, arrived_grad)
    arrived = exchange(send_rows, "fsdp")

    left_a = pick(mixed, normed)
    left_b = swap(pick(normed, mixed))
    left_one_a, left_two_a = flip(left_a, PAIRS_S), flip(left_a, PAIRS_T)
    left_one_b, left_two_b = flip(left_b, PAIRS_T), flip(left_b, PAIRS_S)
    upper_other = swap(lax.dynamic_slice_in_dim(arrived_grad, (1 - core) * half, half, 1))
    grad_hidden = dot_t(arrived_grad, down_weight[0])
    arrived, grad_hidden, upper_other, left_one_a, left_two_a, left_one_b, left_two_b = tie(
        arrived, grad_hidden, upper_other, left_one_a, left_two_a, left_one_b, left_two_b
    )
    left_three_a, left_three_b = flip(left_one_a, PAIRS_T), flip(left_one_b, PAIRS_S)
    arrived_other = swap(arrived)
    hidden, own_pre, sent_pre, grad_rows = call(
        expert_kernel,
        [place_at, Far(arrived, parts=2), Far(grad_hidden, parts=2), gate_weight[0], up_weight[0]],
        [Far((slots_all, half), BF, 2)] * 3 + [Far((slots_all, width), BF, 2)],
    )
    back_rows = exchange(grad_rows, "fsdp")
    expert_rows = width + half

    e_part = (2, expert_rows // 8, half)
    e_keep_a, e_send_a, e_keep_b, e_send_b = call(
        expert_weight_kernel,
        [place_at] + [Far(v) for v in (arrived, arrived_other, own_pre, swap(sent_pre), hidden,
                                       swap(hidden), arrived_grad, upper_other)],
        [(e_part, BF)] * 4,
        [pltpu.VMEM((expert_rows, half), BF)],
    )
    expert_out = dot(hidden, down_weight[0]).astype(BF)
    e_got_a, e_got_b = flip(e_send_a, PAIRS_S), flip(e_send_b, PAIRS_T)
    back_rows, expert_out, e_keep_a, e_keep_b, left_three_a, left_three_b = tie(
        back_rows, expert_out, e_keep_a, e_keep_b, left_three_a, left_three_b
    )
    left = [left_a, left_b, left_one_a, left_two_b, left_two_a, left_one_b, left_three_a,
            left_three_b]

    grad_residual, grad_attended, gain_two_part, grad_query_pre, kv_back, *qo_sent = call(
        back_kernel,
        [place_at, Far(back_rows), Far(one_hot_t), Far(residual), Far(scale_two), gain_two,
         Far(cotangent[0]), Far(output_weight), Far(probs), Far(kv_all), Far(query_rot), cosine,
         sine],
        [((tok, width), F32), ((tok, width), BF), ((groups, 2, HEAD_DIM), F32), ((tok, width), BF),
         ((length, 2 * kv_width), BF)] + [((tok, half), BF)] * XS,
    )
    kv_got = exchange(kv_back, "fsdp")
    e_keep_a, e_send_a, e_keep_b, e_send_b = call(
        expert_step_kernel,
        [place_at, Far(e_keep_a), Far(e_got_a), Far(e_keep_b), Far(e_got_b)],
        [(e_part[1:], BF)] * 4,
    )
    e_got_a, e_got_b = flip(e_send_a, PAIRS_T), flip(e_send_b, PAIRS_S)
    qo_set = fan(qo_sent)
    partial = call(
        query_back_kernel,
        [place_at, Far(grad_query_pre), Far(query_weight)],
        [((tok, width), F32)],
    )[0]
    qo_set[1], qo_set[2], qo_set[3], partial = tie(qo_set[1], qo_set[2], qo_set[3], partial)
    whole = 2 * XS * tok
    square_grad = call(
        square_weight_kernel,
        [place_at] + [Far(v) for v in (*qo_set, *[swap(v) for v in qo_set], *left)],
        [((width, width // XS), BF)],
        [pltpu.VMEM((whole, width // XS), BF), pltpu.VMEM((whole, width), BF),
         pltpu.SemaphoreType.DMA((16,))],
        raw=range(1, 17),
    )[0]
    kv_got, expert_out, square_grad = tie(kv_got, expert_out, square_grad)
    returned = exchange(expert_out, "fsdp")
    grad_kv_pre, *kv_sent = call(
        key_back_kernel,
        [place_at, Far(kv_got.reshape(groups, tok, 2 * kv_width), parts=2), cosine, sine],
        [((tok, 2 * kv_width), BF)] + [((tok, 2 * kv_width // XS), BF)] * XS,
    )
    kv_set = fan(kv_sent)
    input_grad, gain_one_part, mark = call(
        input_kernel,
        [place_at, Far(partial), Far(grad_kv_pre), Far(inputs[0]), Far(scale_one), gain_one,
         Far(kv_weight), Far(grad_residual)],
        [((tok, width), BF), ((groups, 2, HEAD_DIM), F32), ((8, HEAD_DIM), F32)],
        micros=6,
    )

    kv_set[1], kv_set[2], kv_set[3], mark = tie(kv_set[1], kv_set[2], kv_set[3], mark)
    e_got_a, e_got_b, mark = tie(e_got_a, e_got_b, mark)
    e_sum = call(
        expert_end_kernel,
        [place_at, Far(e_keep_a), Far(e_got_a), Far(e_keep_b), Far(e_got_b), mark],
        [(e_part, BF)],
    )[0]
    e_other_y = swap_y(e_sum)
    e_zero_a, e_zero_b = call(pair_kernel, [place_at, Far(e_sum), Far(e_other_y)], [(e_part[1:], BF)] * 2)
    e_one_a, e_one_b = flip(e_zero_a, PAIRS_T), flip(e_zero_b, PAIRS_S)
    e_two_a, e_two_b = flip(e_zero_a, PAIRS_S), flip(e_zero_b, PAIRS_T)

    spare = 2 * kv_width // XS
    part = rows // YLO
    packed_width = width // XS + spare
    packed = call(
        pack_kernel,
        [place_at]
        + [Far(v) for v in (square_grad, gain_one_part, swap(gain_one_part), gain_two_part,
                            swap(gain_two_part))]
        + [Far(v) for v in (*kv_set, *[swap(v) for v in kv_set], *left)],
        [Far((YLO, groups, part, packed_width), BF, 2)],
        [pltpu.VMEM((whole, spare), BF), pltpu.VMEM((whole, width), BF),
         pltpu.VMEM((width, spare), BF), pltpu.SemaphoreType.DMA((16,))],
        raw=range(6, 22),
    )[0]
    packed, returned = tie(packed, returned)
    packed = exchange(packed.reshape(YLO * groups, part, packed_width), ("ylo", "fsdp"))
    mixture = t_dot(gate_high, returned) + t_dot(gate_low, returned)
    outputs = (residual + mixture).astype(BF)
    packed, outputs = tie(packed, outputs)
    packed = call(sum_kernel, [place_at, Far(packed, parts=2)], [((YLO * XS, part, packed_width), BF)])[0]
    spreaded = exchange(packed, ("ylo", "x"))
    most = [e_zero_a, e_zero_b, e_one_a, e_one_b, e_two_a, e_two_b]
    *e_grads, most_mark = expert_outputs(
        expert_most_kernel, [place_at, *most, *[swap(v) for v in most]], [], e_part[1:], width, half
    )
    e_one_a, e_one_b, packed = tie(e_one_a, e_one_b, packed)
    e_three_a, e_three_b = flip(e_one_a, PAIRS_S), flip(e_one_b, PAIRS_T)
    e_three_a, e_three_b, most_mark = tie(e_three_a, e_three_b, most_mark)
    grad_gate, grad_up, grad_down, e_mark = expert_outputs(
        expert_rest_kernel,
        [place_at, e_three_a, e_three_b, swap(e_three_a), swap(e_three_b), most_mark,
         packed[0, :16, :HEAD_DIM]],
        e_grads,
        e_part[1:],
        width,
        half,
    )
    spreaded, e_mark = tie(spreaded, e_mark)
    grad_output_w, grad_query_w, grad_key_w, grad_value_w, grad_one, grad_two = call(
        final_kernel,
        [place_at, Far(spreaded, parts=2), Far(swap(spreaded), parts=2), e_mark],
        [Far((rows, width), F32, 2), Far((rows, width), F32, 2), Far((rows, kv_width), F32, 2),
         Far((rows, kv_width), F32, 2), ((1, rows), F32), ((1, rows), F32)],
    )
    return (
        outputs[None],
        input_grad[None],
        grad_one[0],
        grad_query_w,
        grad_key_w,
        grad_value_w,
        grad_output_w,
        grad_two[0],
        grad_gate[None],
        grad_up[None],
        grad_down[None],
    )


def solution(mesh):
    shape = mesh.devices.shape
    fine = Mesh(
        mesh.devices.reshape(YLO, XS, CORES, shape[1]), ("ylo", "x", "core", "fsdp")
    )
    return jax.shard_map(
        body,
        mesh=fine,
        in_specs=(
            P(REP, "fsdp", None),
            P(REP, None),
            P("fsdp"),
            P("fsdp", None),
            P("fsdp", None),
            P("fsdp", None),
            P("fsdp", None),
            P("fsdp"),
            P(REP, "fsdp", None),
            P(REP, "fsdp", None),
            P(REP, "fsdp", None),
            P("fsdp", None, None),
            P("fsdp", None, None),
            P("fsdp", None, None),
            P(REP, "fsdp", None),
        ),
        out_specs=(
            P(REP, "fsdp", None),
            P(REP, "fsdp", None),
            P("fsdp"),
            P("fsdp", None),
            P("fsdp", None),
            P("fsdp", None),
            P("fsdp", None),
            P("fsdp"),
            P("fsdp", None, None),
            P("fsdp", None, None),
            P("fsdp", None, None),
        ),
        check_vma=False,
    )
```
